512 devices in a mesh: ctx: 64 (over x_lo, z, core), dp: 8 (over y, x_hi).
Axes of the slice: x: 4 (x_hi: 2, x_lo: 2; x = x_hi * 2 + x_lo), y: 4, z: 16, core: 2. Of those that a mesh axis runs over, the one named last changes fastest.
Arguments:
- query_states: bfloat16 [8, 8192, 2048], P('dp', 'ctx'), may hold values from -6 to 6
- key_activations: bfloat16 [8, 8192, 512], P('dp', 'ctx'), may hold values from -6 to 6
- value_activations: bfloat16 [8, 8192, 512], P('dp', 'ctx'), may hold values from -6 to 6
- out_grad: bfloat16 [8, 8192, 2048], P('dp', 'ctx'), may hold values from -6 to 6
- logsumexp: bfloat16 [8, 16, 8192], P('dp', None, 'ctx'), may hold values from 4 to 5
- row_delta: bfloat16 [8, 16, 8192], P('dp', None, 'ctx'), may hold values from -1 to 1
- layer_input: bfloat16 [8, 8192, 2048], P('dp', 'ctx'), may hold values from -16 to 16
- chosen: int32 [8, 128, 4, 3], P('dp', 'ctx'), may hold values from -1 to 125, as said below
Outputs:
- query_grad: bfloat16 [8, 8192, 2048], P('dp', 'ctx')
- key_gradient: bfloat16 [8, 8192, 512], P('dp', 'ctx')
- value_gradient: bfloat16 [8, 8192, 512], P('dp', 'ctx')
- key_weight_grad: float32 [2048, 512], P(('ctx', 'dp'))
The draws below stay inside these ranges and needn't reach their ends.
Inputs may be any that keep to these rules, and one draw needn't show every extreme that they name: `chosen`: -1 marks an unused choice. Every other entry names a block of an earlier shard of 128 positions of the same sequence; the 3 used entries of one query block and key-value head differ. The used entries of the query blocks of one shard name blocks of one other shard at most 2 times, and exactly 2 times for some pair of shards.
All inputs are finite; a program needn't handle non-finite values.
Results may differ from the reference program's by a relative error of at most 0.0052.
Values may be sent and summed in bfloat16 or wider, within the bound.
A program may use at most 192 MiB of HBM per device.

```python
import jax
import jax.numpy as jnp
from jax import lax

QUERY_HEADS = 16
KEY_VALUE_HEADS = 4
HEAD_WIDTH = 128
DW = 2048
BLOCK_LENGTH = 64
CHOSEN_BLOCKS = 3
CAP = 2
SHARD_TOKENS = 128
SHARD_BLOCKS = 2
SEQUENCE_LENGTH = 8192
SEQUENCE_BLOCKS = 128
BATCH_COUNT = 8


def draw_chosen(key, part):
    key = jax.random.fold_in(key, 7)
    shards = SEQUENCE_BLOCKS // SHARD_BLOCKS
    request_number = SHARD_BLOCKS * KEY_VALUE_HEADS * CHOSEN_BLOCKS
    pair_count = CAP * shards
    pair_ids = jnp.arange(pair_count, dtype=jnp.int32)
    owners = pair_ids // CAP
    lane_index = pair_ids % CAP

    def one_shard(shard_key, device):
        first_key, second_key, third_key = jax.random.split(shard_key, 3)
        raw_draw = jax.random.randint(first_key, (pair_count,), 0, 16384, dtype=jnp.int32)
        bonuses = jnp.where(owners == device - 1, 1 << 26, 0) + jnp.where(owners == 0, 1 << 25, 0)
        scores = jnp.where(owners < device, raw_draw * 1024 + pair_ids + bonuses, -1 - pair_ids)
        ordering = jnp.argsort(-scores)
        shuffled = jax.random.permutation(second_key, request_number)
        placing = jnp.argsort(shuffled)
        picked = ordering[jnp.minimum(placing, pair_count - 1)]
        valid_mask = (placing < pair_count) & (scores[picked] >= 0)
        base_block = jax.random.randint(third_key, (shards,), 0, SHARD_BLOCKS, dtype=jnp.int32)
        shard_ids = jnp.arange(shards, dtype=jnp.int32)
        base_block = jnp.where(shard_ids == device - 1, SHARD_BLOCKS - 1, base_block)
        owner_of = owners[picked]
        block_numbers = owner_of * SHARD_BLOCKS + (base_block[owner_of] + lane_index[picked]) % SHARD_BLOCKS
        return jnp.where(valid_mask, block_numbers, -1).astype(jnp.int32).reshape(SHARD_BLOCKS, KEY_VALUE_HEADS, CHOSEN_BLOCKS)

    def one_sequence(seq_key):
        shard_keys = jax.random.split(seq_key, shards)
        sampled_picks = jax.vmap(one_shard)(shard_keys, jnp.arange(shards, dtype=jnp.int32))
        return sampled_picks.reshape(SEQUENCE_BLOCKS, KEY_VALUE_HEADS, CHOSEN_BLOCKS)
    return jax.vmap(one_sequence)(jax.random.split(key, BATCH_COUNT))


def spiked(array, own_key, source, target, shards_of, factor):
    def block_of(position):
        return (jnp.arange(array.shape[position]) // (array.shape[position] // shards_of)).reshape((-1,) + (1,) * (array.ndim - 1 - position))

    first = jax.random.permutation(own_key, shards_of)[block_of(target)]
    second = (block_of(target) + shards_of // 2) % shards_of
    return jnp.where((block_of(source) == first) | (block_of(source) == second), factor * array, array)


def steps_of(own_key, extent, cuts, smallest, top_value):
    level, own = 1.0, jax.random.fold_in(own_key, 6)
    for dim, shards_of in cuts:
        draws = jnp.exp(jax.random.uniform(jax.random.fold_in(own, dim), (shards_of,), jnp.float32, smallest / len(cuts), top_value / len(cuts)))
        level = level * jnp.repeat(draws, extent[dim] // shards_of).reshape([-1 if axis == dim else 1 for axis in range(len(extent))])
    return level


def normal_values(key, shape, width, bound, cuts=(), held_as=jnp.bfloat16):
    level = steps_of(key, shape, cuts, -0.22, 0.18) if cuts else 1.0
    result = jax.random.normal(key, shape, jnp.float32) * width * level
    return jnp.minimum(jnp.maximum(result, -bound), bound).astype(held_as)


def noise_with(key, extent, width, reach, cuts, heavy, held_as=jnp.bfloat16):
    drawn = width * jax.random.normal(key, extent, jnp.float32)
    if cuts:
        drawn = drawn * steps_of(key, extent, cuts, -0.22, 0.18)
    return jnp.clip(spiked(drawn, jax.random.fold_in(key, 3), *heavy), -reach, reach).astype(held_as)


def setup_inputs(seed: int = 0) -> dict:
    arg_keys = jax.random.split(jax.random.key(seed), 9)
    query_states = normal_values(arg_keys[0], (BATCH_COUNT, SEQUENCE_LENGTH, QUERY_HEADS * HEAD_WIDTH), 1.0, 6.0, ((0, 8), (1, 64)))
    key_activations = normal_values(arg_keys[1], (BATCH_COUNT, SEQUENCE_LENGTH, KEY_VALUE_HEADS * HEAD_WIDTH), 1.0, 6.0, ((0, 8), (1, 64)))
    value_activations = normal_values(arg_keys[2], (BATCH_COUNT, SEQUENCE_LENGTH, KEY_VALUE_HEADS * HEAD_WIDTH), 1.0, 6.0, ((0, 8), (1, 64)))
    out_grad = normal_values(arg_keys[3], (BATCH_COUNT, SEQUENCE_LENGTH, QUERY_HEADS * HEAD_WIDTH), 0.5, 6.0, ((0, 8), (1, 64)))
    logsumexp = jnp.clip(4.0 + 1.0 * jax.random.uniform(arg_keys[4], (BATCH_COUNT, QUERY_HEADS, SEQUENCE_LENGTH), jnp.float32) ** steps_of(arg_keys[4], (BATCH_COUNT, QUERY_HEADS, SEQUENCE_LENGTH), ((0, 8), (2, 64)), -0.2, 0.2), 4.0, 5.0).astype(jnp.bfloat16)
    row_delta = jnp.clip(jax.random.uniform(arg_keys[5], (BATCH_COUNT, QUERY_HEADS, SEQUENCE_LENGTH), jnp.float32, -1.0, 1.0) * steps_of(arg_keys[5], (BATCH_COUNT, QUERY_HEADS, SEQUENCE_LENGTH), ((0, 8), (2, 64)), -0.4, 0.0), -1.0, 1.0).astype(jnp.bfloat16)
    layer_input = noise_with(arg_keys[6], (BATCH_COUNT, SEQUENCE_LENGTH, DW), 1.0, 16.0, ((0, 8), (1, 64)), (1, 2, 64, 4.0))
    chosen = draw_chosen(jax.random.fold_in(arg_keys[8], 71), 0)
    return {"query_states": query_states, "key_activations": key_activations, "value_activations": value_activations, "out_grad": out_grad, "logsumexp": logsumexp, "row_delta": row_delta, "layer_input": layer_input, "chosen": chosen}


def round_low(values_in):
    return lax.optimization_barrier(values_in.astype(jnp.bfloat16)).astype(jnp.float32)


def pair_grads(keys_blk, values_blk, rows_blk, grads_blk, lse_blk, delta_blk, valid_mask, score_scale):
    highest = lax.Precision.HIGHEST
    scores = jnp.einsum("...kd,...rd->...kr", keys_blk, rows_blk, precision=highest) * score_scale
    prob_vals = jnp.where(valid_mask, jnp.exp(scores - lse_blk[..., None, :]), 0.0)
    dprob_vals = jnp.einsum("...kd,...rd->...kr", values_blk, grads_blk, precision=highest)
    dscore_low = round_low(prob_vals * (dprob_vals - delta_blk[..., None, :]))
    prob_low = round_low(prob_vals)
    row_grad = jnp.einsum("...kr,...kd->...rd", dscore_low, keys_blk, precision=highest) * score_scale
    key_part = jnp.einsum("...kr,...rd->...kd", dscore_low, rows_blk, precision=highest) * score_scale
    value_part = jnp.einsum("...kr,...rd->...kd", prob_low, grads_blk, precision=highest)
    return row_grad, key_part, value_part


def reference(query_states, key_activations, value_activations, out_grad, logsumexp, row_delta, layer_input, chosen):
    score_scale = HEAD_WIDTH ** -0.5
    head_group_width = QUERY_HEADS // KEY_VALUE_HEADS
    row_number = head_group_width * BLOCK_LENGTH
    weight_scale = 1.0 / (SEQUENCE_LENGTH * BATCH_COUNT) ** 0.5
    token_pos = jnp.arange(SHARD_TOKENS, dtype=jnp.int32)
    causal = token_pos[:, None] <= jnp.tile(token_pos, head_group_width)[None, :]
    head_numbers = jnp.arange(KEY_VALUE_HEADS, dtype=jnp.int32)[None, :, None]

    def one_sequence(pieces):
        queries_all, gathered_keys, gathered_values, grads_all, lse_all, delta_all, picks_all, inputs_all = pieces
        key_lookup = gathered_keys.astype(jnp.float32).reshape(SEQUENCE_BLOCKS, BLOCK_LENGTH, KEY_VALUE_HEADS, HEAD_WIDTH)
        value_lookup = gathered_values.astype(jnp.float32).reshape(SEQUENCE_BLOCKS, BLOCK_LENGTH, KEY_VALUE_HEADS, HEAD_WIDTH)

        def shard_step(carry, shard):
            remote_key_accumulator, remote_value_accumulator = carry
            first_row = shard * SHARD_TOKENS
            query_rows = lax.dynamic_slice_in_dim(queries_all, first_row, SHARD_TOKENS, 0).astype(jnp.float32)
            query_rows = query_rows.reshape(SHARD_TOKENS, KEY_VALUE_HEADS, head_group_width, HEAD_WIDTH).transpose(1, 2, 0, 3)
            rowwise_gradient = lax.dynamic_slice_in_dim(grads_all, first_row, SHARD_TOKENS, 0).astype(jnp.float32)
            rowwise_gradient = rowwise_gradient.reshape(SHARD_TOKENS, KEY_VALUE_HEADS, head_group_width, HEAD_WIDTH).transpose(1, 2, 0, 3)
            shard_key_rows = lax.dynamic_slice_in_dim(gathered_keys, first_row, SHARD_TOKENS, 0).astype(jnp.float32)
            shard_key_rows = shard_key_rows.reshape(SHARD_TOKENS, KEY_VALUE_HEADS, HEAD_WIDTH).transpose(1, 0, 2)
            shard_value_rows = lax.dynamic_slice_in_dim(gathered_values, first_row, SHARD_TOKENS, 0).astype(jnp.float32)
            shard_value_rows = shard_value_rows.reshape(SHARD_TOKENS, KEY_VALUE_HEADS, HEAD_WIDTH).transpose(1, 0, 2)
            rowwise_logsum = lax.dynamic_slice_in_dim(lse_all, first_row, SHARD_TOKENS, 1).astype(jnp.float32)
            rowwise_logsum = rowwise_logsum.reshape(KEY_VALUE_HEADS, head_group_width, SHARD_TOKENS)
            rowwise_delta = lax.dynamic_slice_in_dim(delta_all, first_row, SHARD_TOKENS, 1).astype(jnp.float32)
            rowwise_delta = rowwise_delta.reshape(KEY_VALUE_HEADS, head_group_width, SHARD_TOKENS)
            nearby_rows, nearby_keys, nearby_values = pair_grads(
                shard_key_rows, shard_value_rows,
                query_rows.reshape(KEY_VALUE_HEADS, head_group_width * SHARD_TOKENS, HEAD_WIDTH), rowwise_gradient.reshape(KEY_VALUE_HEADS, head_group_width * SHARD_TOKENS, HEAD_WIDTH),
                rowwise_logsum.reshape(KEY_VALUE_HEADS, head_group_width * SHARD_TOKENS), rowwise_delta.reshape(KEY_VALUE_HEADS, head_group_width * SHARD_TOKENS),
                causal[None], score_scale)
            picked = lax.dynamic_slice_in_dim(picks_all, shard * SHARD_BLOCKS, SHARD_BLOCKS, 0)
            active_mask = picked >= 0
            block_numbers = jnp.maximum(picked, 0).astype(jnp.int32)
            remote_key_incoming = key_lookup[block_numbers, :, head_numbers].reshape(SHARD_BLOCKS, KEY_VALUE_HEADS, CHOSEN_BLOCKS * BLOCK_LENGTH, HEAD_WIDTH)
            remote_value_incoming = value_lookup[block_numbers, :, head_numbers].reshape(SHARD_BLOCKS, KEY_VALUE_HEADS, CHOSEN_BLOCKS * BLOCK_LENGTH, HEAD_WIDTH)
            blockwise_queries = query_rows.reshape(KEY_VALUE_HEADS, head_group_width, SHARD_BLOCKS, BLOCK_LENGTH, HEAD_WIDTH).transpose(2, 0, 1, 3, 4).reshape(SHARD_BLOCKS, KEY_VALUE_HEADS, row_number, HEAD_WIDTH)
            blockwise_gradient = rowwise_gradient.reshape(KEY_VALUE_HEADS, head_group_width, SHARD_BLOCKS, BLOCK_LENGTH, HEAD_WIDTH).transpose(2, 0, 1, 3, 4).reshape(SHARD_BLOCKS, KEY_VALUE_HEADS, row_number, HEAD_WIDTH)
            blockwise_logsum = rowwise_logsum.reshape(KEY_VALUE_HEADS, head_group_width, SHARD_BLOCKS, BLOCK_LENGTH).transpose(2, 0, 1, 3).reshape(SHARD_BLOCKS, KEY_VALUE_HEADS, row_number)
            blockwise_delta = rowwise_delta.reshape(KEY_VALUE_HEADS, head_group_width, SHARD_BLOCKS, BLOCK_LENGTH).transpose(2, 0, 1, 3).reshape(SHARD_BLOCKS, KEY_VALUE_HEADS, row_number)
            valid_mask = jnp.repeat(active_mask, BLOCK_LENGTH, axis=2)[..., None]
            remote_row_list, remote_key_rows, remote_value_rows = pair_grads(
                remote_key_incoming, remote_value_incoming, blockwise_queries, blockwise_gradient, blockwise_logsum, blockwise_delta, valid_mask, score_scale)
            remote_key_accumulator = remote_key_accumulator.at[block_numbers, :, head_numbers].add(remote_key_rows.reshape(SHARD_BLOCKS, KEY_VALUE_HEADS, CHOSEN_BLOCKS, BLOCK_LENGTH, HEAD_WIDTH))
            remote_value_accumulator = remote_value_accumulator.at[block_numbers, :, head_numbers].add(remote_value_rows.reshape(SHARD_BLOCKS, KEY_VALUE_HEADS, CHOSEN_BLOCKS, BLOCK_LENGTH, HEAD_WIDTH))
            remote_row_list = remote_row_list.reshape(SHARD_BLOCKS, KEY_VALUE_HEADS, head_group_width, BLOCK_LENGTH, HEAD_WIDTH).transpose(1, 2, 0, 3, 4)
            overall_rows = nearby_rows + remote_row_list.reshape(KEY_VALUE_HEADS, head_group_width * SHARD_TOKENS, HEAD_WIDTH)
            overall_rows = overall_rows.reshape(KEY_VALUE_HEADS, head_group_width, SHARD_TOKENS, HEAD_WIDTH).transpose(2, 0, 1, 3).reshape(SHARD_TOKENS, QUERY_HEADS * HEAD_WIDTH)
            return (remote_key_accumulator, remote_value_accumulator), (overall_rows.astype(jnp.bfloat16), nearby_keys, nearby_values)

        blank_lookup = jnp.zeros((SEQUENCE_BLOCKS, BLOCK_LENGTH, KEY_VALUE_HEADS, HEAD_WIDTH), jnp.float32)
        shard_ids = jnp.arange(SEQUENCE_LENGTH // SHARD_TOKENS, dtype=jnp.int32)
        (remote_key_accumulator, remote_value_accumulator), (query_grad, nearby_keys, nearby_values) = lax.scan(
            shard_step, (blank_lookup, blank_lookup), shard_ids)
        nearby_keys = nearby_keys.transpose(0, 2, 1, 3).reshape(SEQUENCE_LENGTH, KEY_VALUE_HEADS, HEAD_WIDTH)
        nearby_values = nearby_values.transpose(0, 2, 1, 3).reshape(SEQUENCE_LENGTH, KEY_VALUE_HEADS, HEAD_WIDTH)
        key_gradient = (nearby_keys + remote_key_accumulator.reshape(SEQUENCE_LENGTH, KEY_VALUE_HEADS, HEAD_WIDTH)).astype(jnp.bfloat16).reshape(SEQUENCE_LENGTH, KEY_VALUE_HEADS * HEAD_WIDTH)
        value_gradient = (nearby_values + remote_value_accumulator.reshape(SEQUENCE_LENGTH, KEY_VALUE_HEADS, HEAD_WIDTH)).astype(jnp.bfloat16).reshape(SEQUENCE_LENGTH, KEY_VALUE_HEADS * HEAD_WIDTH)
        weight_part = jnp.dot(inputs_all.T, key_gradient, preferred_element_type=jnp.float32)
        return query_grad.reshape(SEQUENCE_LENGTH, QUERY_HEADS * HEAD_WIDTH), key_gradient, value_gradient, weight_part

    query_grad, key_gradient, value_gradient, weight_parts = lax.map(
        one_sequence, (query_states, key_activations, value_activations, out_grad, logsumexp, row_delta, chosen, layer_input))
    key_weight_grad = jnp.sum(weight_parts, axis=0) * weight_scale
    return query_grad, key_gradient, value_gradient, key_weight_grad
```

```python
import functools
import math

import jax
import jax.numpy as jnp
from jax import lax
from jax.experimental import pallas as pl
from jax.experimental.pallas import tpu as pltpu
from jax.sharding import PartitionSpec as P

HEAD_WIDTH = 128
BLOCK_LENGTH = 64
CHOSEN_BLOCKS = 3
CAP = 2
KV_HEADS = 4
GROUP = 4
TOKENS = 128
UNITS = TOKENS // BLOCK_LENGTH * KV_HEADS
PAIR = 2 * HEAD_WIDTH
MESH = pl.DeviceIdType.MESH


def place(ring):
    i = lax.axis_index("ctx")
    return i // (2 * ring), lax.rem(i // 2, ring), lax.rem(i, 2)


def member(ring, j):
    x, z, c = place(ring)
    mx = lax.rem(x + j // 2, 2)
    mc = lax.rem(c + j % 2, 2)
    return mx * (2 * ring) + z * 2 + mc, mx * 2 + mc


def along(ring, step):
    x, z, c = place(ring)
    return x * (2 * ring) + lax.rem(z + step + ring, ring) * 2 + c


def greet(ring):
    barrier = pltpu.get_barrier_semaphore()
    for other in (along(ring, 1), along(ring, -1)) + tuple(member(ring, j)[0] for j in (1, 2, 3)):
        pl.semaphore_signal(barrier, inc=1, device_id={"ctx": other}, device_id_type=MESH)
    pl.semaphore_wait(barrier, 5)


def push(src, dst, send, recv, other):
    return pltpu.make_async_remote_copy(
        src_ref=src, dst_ref=dst, send_sem=send, recv_sem=recv,
        device_id={"ctx": other}, device_id_type=MESH,
    )


def gather_kernel(
    ring, k_ref, v_ref, want_ref, slots_ref, wants_ref,
    up, down, stage, work, want_smem,
    up_send, up_recv, down_send, down_recv, w_send, w_recv, s_send, s_recv, local_sem, smem_sem,
):
    half = ring // 2
    x, z, c = place(ring)
    cls = x * 2 + c
    above, below = along(ring, 1), along(ring, -1)
    greet(ring)

    def up_copy(s, part, src=None):
        src = up.at[s - 1, part] if src is None else src
        return push(src, up.at[s, part], up_send.at[s, part], up_recv.at[s, part], above)

    def down_copy(s, part, src=None):
        src = down.at[s - 1, part] if src is None else src
        return push(src, down.at[s, part], down_send.at[s, part], down_recv.at[s, part], below)

    def want_copy(j):
        other, other_cls = member(ring, j)
        return push(want_ref.at[other_cls], wants_ref.at[j], w_send.at[j - 1], w_recv.at[j - 1], other)

    for j in (1, 2, 3):
        want_copy(j).start()
    for part, ref in ((0, k_ref), (1, v_ref)):
        up_copy(0, part, ref).start()
        down_copy(0, part, ref).start()

    own = pltpu.make_async_copy(want_ref.at[cls], wants_ref.at[0], smem_sem)
    own.start()
    own.wait()
    for j in (1, 2, 3):
        want_copy(j).wait()
    table = pltpu.make_async_copy(wants_ref, want_smem, smem_sem)
    table.start()
    table.wait()

    def slot_copy(j, r):
        owner = lax.rem(z + r, ring)
        return push(
            stage.at[r, j], slots_ref.at[cls, owner], s_send.at[j - 1, r], s_recv.at[j - 1, r],
            member(ring, j)[0],
        )

    def own_copy(r):
        return pltpu.make_async_copy(
            stage.at[r, 0], slots_ref.at[cls, lax.rem(z + r, ring)], local_sem.at[r]
        )

    def extract(r, keys, values):
        owner = lax.rem(z + r, ring)
        for b in range(2):
            for h in range(KV_HEADS):
                rows, lanes = pl.ds(b * BLOCK_LENGTH, BLOCK_LENGTH), pl.ds(h * HEAD_WIDTH, HEAD_WIDTH)
                work[b * KV_HEADS + h, :, :HEAD_WIDTH] = keys[rows, lanes]
                work[b * KV_HEADS + h, :, HEAD_WIDTH:] = values[rows, lanes]
        for j in range(4):
            for rank in range(CAP):
                unit = jnp.maximum(want_smem[j, 0, owner * CAP + rank], 0)
                stage[r, j, rank] = work[unit]
        for j in (1, 2, 3):
            slot_copy(j, r).start()
        own_copy(r).start()

    extract(0, k_ref, v_ref)

    def step(s, _):
        for part in range(2):
            up_copy(s, part, k_ref).wait_recv()
            up_copy(s + 1, part).start()
            down_copy(s, part, k_ref).wait_recv()
            down_copy(s + 1, part).start()
        extract(ring - 1 - s, up.at[s, 0], up.at[s, 1])
        extract(1 + s, down.at[s, 0], down.at[s, 1])
        return 0

    lax.fori_loop(0, half - 2, step, 0)
    s = half - 2
    for part in range(2):
        up_copy(s, part, k_ref).wait_recv()
        if part == 0:
            up_copy(s + 1, part).start()
        down_copy(s, part, k_ref).wait_recv()
        if part == 1:
            down_copy(s + 1, part).start()
    extract(ring - 1 - s, up.at[s, 0], up.at[s, 1])
    extract(1 + s, down.at[s, 0], down.at[s, 1])
    up_copy(half - 1, 0, k_ref).wait_recv()
    down_copy(half - 1, 1, k_ref).wait_recv()
    extract(half, up.at[half - 1, 0], down.at[half - 1, 1])

    def drain(s, _):
        for part in range(2):
            up_copy(s, part, k_ref).wait_send()
            down_copy(s, part, k_ref).wait_send()
        return 0

    lax.fori_loop(0, half - 1, drain, 0)
    up_copy(half - 1, 0, k_ref).wait_send()
    down_copy(half - 1, 1, k_ref).wait_send()

    def drain_slots(r, _):
        for j in (1, 2, 3):
            slot_copy(j, r).wait()
        own_copy(r).wait()
        return 0

    lax.fori_loop(0, ring, drain_slots, 0)


def gather_call(ring, keys, values, want):
    half = ring // 2
    ring_buffer = pltpu.VMEM((half, 2, TOKENS, KV_HEADS * HEAD_WIDTH), jnp.bfloat16)
    ring_sem = pltpu.SemaphoreType.DMA((half, 2))
    return pl.pallas_call(
        functools.partial(gather_kernel, ring),
        out_shape=(
            jax.ShapeDtypeStruct((4, ring, CAP, BLOCK_LENGTH, PAIR), jnp.bfloat16),
            jax.ShapeDtypeStruct((4, 8, 128), jnp.int32),
        ),
        in_specs=[pl.BlockSpec(memory_space=pltpu.VMEM)] * 3,
        out_specs=(pl.BlockSpec(memory_space=pl.ANY), pl.BlockSpec(memory_space=pltpu.VMEM)),
        scratch_shapes=[
            ring_buffer,
            ring_buffer,
            pltpu.VMEM((ring, 4, CAP, BLOCK_LENGTH, PAIR), jnp.bfloat16),
            pltpu.VMEM((UNITS, BLOCK_LENGTH, PAIR), jnp.bfloat16),
            pltpu.SMEM((4, 8, 128), jnp.int32),
            ring_sem, ring_sem, ring_sem, ring_sem,
            pltpu.SemaphoreType.DMA((3,)),
            pltpu.SemaphoreType.DMA((3,)),
            pltpu.SemaphoreType.DMA((3, ring)),
            pltpu.SemaphoreType.DMA((3, ring)),
            pltpu.SemaphoreType.DMA((ring,)),
            pltpu.SemaphoreType.DMA,
        ],
        compiler_params=pltpu.CompilerParams(
            collective_id=0, has_side_effects=True, vmem_limit_bytes=40 * 1024 * 1024
        ),
        name="gather_blocks",
    )(keys, values, want)


def reduce_kernel(
    ring, part_ref, wants_ref, dk_ref, dv_ref, kg_ref, vg_ref,
    up, down, ups, downs, arrived, want_smem,
    up_send, up_recv, down_send, down_recv, s_send, s_recv, smem_sem,
):
    half = ring // 2
    x, z, c = place(ring)
    cls = x * 2 + c
    above, below = along(ring, 1), along(ring, -1)
    greet(ring)

    def slot_copy(j, r):
        other, other_cls = member(ring, j)
        owner = lax.rem(z + r, ring)
        return push(
            part_ref.at[other_cls, owner], arrived.at[j - 1, r],
            s_send.at[j - 1, r], s_recv.at[j - 1, r], other,
        )

    for j in (1, 2, 3):
        slot_copy(j, half).start()

    def send_slots(s, _):
        for j in (1, 2, 3):
            slot_copy(j, half - s).start()
            slot_copy(j, half + s).start()
        return 0

    lax.fori_loop(1, half, send_slots, 0)
    for j in (1, 2, 3):
        slot_copy(j, 0).start()
    table = pltpu.make_async_copy(wants_ref, want_smem, smem_sem)
    table.start()
    blank = jnp.zeros((TOKENS, KV_HEADS * HEAD_WIDTH), jnp.bfloat16)
    up[0, 1] = blank
    down[0, 0] = blank
    table.wait()

    def up_copy(s, part):
        return push(ups.at[s, part], up.at[s, part], up_send.at[s, part], up_recv.at[s, part], above)

    def down_copy(s, part):
        return push(
            downs.at[s, part], down.at[s, part], down_send.at[s, part], down_recv.at[s, part], below
        )

    def total(r, part, incoming, target):
        owner = lax.rem(z + r, ring)
        lanes = pl.ds(part * HEAD_WIDTH, HEAD_WIDTH)
        units = [[want_smem[j, 0, owner * CAP + rank] for rank in range(CAP)] for j in range(4)]
        for b in range(2):
            for h in range(KV_HEADS):
                at = (pl.ds(b * BLOCK_LENGTH, BLOCK_LENGTH), pl.ds(h * HEAD_WIDTH, HEAD_WIDTH))
                acc = jnp.zeros((BLOCK_LENGTH, HEAD_WIDTH), jnp.float32)
                for ref in incoming:
                    acc = acc + ref[at].astype(jnp.float32)
                for j in range(4):
                    for rank in range(CAP):
                        if j == 0:
                            term = part_ref[cls, owner, rank, :, lanes]
                        else:
                            term = arrived[j - 1, r, rank, :, lanes]
                        hit = units[j][rank] == b * KV_HEADS + h
                        acc = acc + jnp.where(hit, term.astype(jnp.float32), 0.0)
                target[at] = acc.astype(jnp.bfloat16)

    for j in (1, 2, 3):
        slot_copy(j, half).wait_recv()
    total(half, 0, [], ups.at[0, 0])
    up_copy(0, 0).start()
    total(half, 1, [], downs.at[0, 1])
    down_copy(0, 1).start()

    def step(s, _):
        for j in (1, 2, 3):
            slot_copy(j, half - s).wait_recv()
            slot_copy(j, half + s).wait_recv()

        up_copy(s - 1, 0).wait_recv()
        total(half - s, 0, [up.at[s - 1, 0]], ups.at[s, 0])
        up_copy(s, 0).start()
        down_copy(s - 1, 1).wait_recv()
        total(half + s, 1, [down.at[s - 1, 1]], downs.at[s, 1])
        down_copy(s, 1).start()

        @pl.when(s > 1)
        def _():
            up_copy(s - 1, 1).wait_recv()
            down_copy(s - 1, 0).wait_recv()

        total(half - s, 1, [up.at[s - 1, 1]], ups.at[s, 1])
        up_copy(s, 1).start()
        total(half + s, 0, [down.at[s - 1, 0]], downs.at[s, 0])
        down_copy(s, 0).start()
        return 0

    lax.fori_loop(1, half, step, 0)
    for j in (1, 2, 3):
        slot_copy(j, 0).wait_recv()
    for part, near, out in ((0, dk_ref, kg_ref), (1, dv_ref, vg_ref)):
        up_copy(half - 1, part).wait_recv()
        down_copy(half - 1, part).wait_recv()
        total(0, part, [near, up.at[half - 1, part], down.at[half - 1, part]], out)

    up_copy(0, 0).wait_send()
    down_copy(0, 1).wait_send()

    def drain(s, _):
        for part in range(2):
            up_copy(s, part).wait_send()
            down_copy(s, part).wait_send()
        return 0

    lax.fori_loop(1, half, drain, 0)

    def drain_slots(r, _):
        for j in (1, 2, 3):
            slot_copy(j, r).wait_send()
        return 0

    lax.fori_loop(0, ring, drain_slots, 0)


def reduce_call(ring, parts, wants, dk, dv):
    half = ring // 2
    width = KV_HEADS * HEAD_WIDTH
    ring_buffer = pltpu.VMEM((half, 2, TOKENS, width), jnp.bfloat16)
    ring_sem = pltpu.SemaphoreType.DMA((half, 2))
    return pl.pallas_call(
        functools.partial(reduce_kernel, ring),
        out_shape=(jax.ShapeDtypeStruct((TOKENS, width), jnp.bfloat16),) * 2,
        in_specs=[pl.BlockSpec(memory_space=pltpu.VMEM)] * 4,
        out_specs=(pl.BlockSpec(memory_space=pltpu.VMEM),) * 2,
        scratch_shapes=[
            ring_buffer, ring_buffer, ring_buffer, ring_buffer,
            pltpu.VMEM((3, ring, CAP, BLOCK_LENGTH, PAIR), jnp.bfloat16),
            pltpu.SMEM((4, 8, 128), jnp.int32),
            ring_sem, ring_sem, ring_sem, ring_sem,
            pltpu.SemaphoreType.DMA((3, ring)),
            pltpu.SemaphoreType.DMA((3, ring)),
            pltpu.SemaphoreType.DMA,
        ],
        compiler_params=pltpu.CompilerParams(
            collective_id=1, has_side_effects=True, vmem_limit_bytes=40 * 1024 * 1024
        ),
        name="reduce_blocks",
    )(parts, wants, dk, dv)


def attend_kernel(
    place_ref, valid_ref, q_ref, g_ref, k_ref, v_ref, lse_ref, delta_ref, f0, f1, f2,
    dq_ref, dk_ref, dv_ref, part_ref,
):
    h, b = pl.program_id(0), pl.program_id(1)
    scale = HEAD_WIDTH ** (-0.5)
    first = (b * KV_HEADS + h) * CHOSEN_BLOCKS
    fetched = (f0, f1, f2)
    local = TOKENS
    keys_n = local + CHOSEN_BLOCKS * BLOCK_LENGTH
    rows_n = GROUP * BLOCK_LENGTH

    @pl.when((h == 0) & (b == 0))
    def _():
        part_ref[...] = jnp.zeros_like(part_ref)

    def stack(ref):
        return jnp.concatenate(
            [ref[:, i * HEAD_WIDTH : (i + 1) * HEAD_WIDTH] for i in range(GROUP)], axis=0
        )

    queries, grads = stack(q_ref), stack(g_ref)
    zero = jnp.zeros((BLOCK_LENGTH, PAIR), jnp.bfloat16)
    far = [jnp.where(valid_ref[first + i] > 0, ref[0], zero) for i, ref in enumerate(fetched)]
    keys = jnp.concatenate([k_ref[...]] + [f[:, :HEAD_WIDTH] for f in far], axis=0)
    values = jnp.concatenate([v_ref[...]] + [f[:, HEAD_WIDTH:] for f in far], axis=0)
    row = lax.broadcasted_iota(jnp.int32, (keys_n, rows_n), 1) % BLOCK_LENGTH + b * BLOCK_LENGTH
    key = lax.broadcasted_iota(jnp.int32, (keys_n, rows_n), 0)
    mask = (key < local) & (key <= row)
    for i in range(CHOSEN_BLOCKS):
        begin = local + i * BLOCK_LENGTH
        limit = jnp.where(valid_ref[first + i] > 0, begin + BLOCK_LENGTH, begin)
        mask = mask | ((key >= begin) & (key < limit))
    nt = (((1,), (1,)), ((), ()))
    tn = (((0,), (0,)), ((), ()))
    scores = lax.dot_general(keys, queries, nt, preferred_element_type=jnp.float32) * scale
    prob = jnp.where(mask, jnp.exp(scores - lse_ref[0, 0]), 0.0)
    dprob = lax.dot_general(values, grads, nt, preferred_element_type=jnp.float32)
    dscore = (prob * (dprob - delta_ref[0, 0])).astype(jnp.bfloat16)
    prob_low = prob.astype(jnp.bfloat16)
    dq = (lax.dot_general(dscore, keys, tn, preferred_element_type=jnp.float32) * scale).astype(
        jnp.bfloat16
    )
    for i in range(GROUP):
        dq_ref[:, i * HEAD_WIDTH : (i + 1) * HEAD_WIDTH] = dq[
            i * BLOCK_LENGTH : (i + 1) * BLOCK_LENGTH
        ]
    dk = jnp.dot(dscore, queries, preferred_element_type=jnp.float32) * scale
    dv = jnp.dot(prob_low, grads, preferred_element_type=jnp.float32)

    @pl.when(b == 0)
    def _():
        dk_ref[...] = dk[:local]
        dv_ref[...] = dv[:local]

    @pl.when(b > 0)
    def _():
        dk_ref[...] += dk[:local]
        dv_ref[...] += dv[:local]

    for i in range(CHOSEN_BLOCKS):
        at = pl.ds(local + i * BLOCK_LENGTH, BLOCK_LENGTH)
        lo = local + i * BLOCK_LENGTH

        @pl.when(valid_ref[first + i] > 0)
        def _():
            slot = place_ref[first + i]
            part_ref[slot, :, :HEAD_WIDTH] = dk[lo : lo + BLOCK_LENGTH].astype(jnp.bfloat16)
            part_ref[slot, :, HEAD_WIDTH:] = dv[lo : lo + BLOCK_LENGTH].astype(jnp.bfloat16)


def attend_call(slot_place, valid, queries, grads, keys, values, lse, delta, slots):
    slot_total = slots.shape[0]
    group_width = GROUP * HEAD_WIDTH

    def far_spec(i):
        return pl.BlockSpec(
            (1, BLOCK_LENGTH, PAIR),
            lambda h, b, sp, va: (sp[(b * KV_HEADS + h) * CHOSEN_BLOCKS + i], 0, 0),
        )

    rows = pl.BlockSpec((BLOCK_LENGTH, group_width), lambda h, b, sp, va: (b, h))
    shard = pl.BlockSpec((TOKENS, HEAD_WIDTH), lambda h, b, sp, va: (0, h))
    stat = pl.BlockSpec((1, 1, 1, GROUP * BLOCK_LENGTH), lambda h, b, sp, va: (b, h, 0, 0))
    return pl.pallas_call(
        attend_kernel,
        grid_spec=pltpu.PrefetchScalarGridSpec(
            num_scalar_prefetch=2,
            grid=(KV_HEADS, TOKENS // BLOCK_LENGTH),
            in_specs=[rows, rows, shard, shard, stat, stat, far_spec(0), far_spec(1), far_spec(2)],
            out_specs=[
                rows,
                shard,
                shard,
                pl.BlockSpec((slot_total, BLOCK_LENGTH, PAIR), lambda h, b, sp, va: (0, 0, 0)),
            ],
        ),
        out_shape=(
            jax.ShapeDtypeStruct(queries.shape, jnp.bfloat16),
            jax.ShapeDtypeStruct(keys.shape, jnp.float32),
            jax.ShapeDtypeStruct(keys.shape, jnp.float32),
            jax.ShapeDtypeStruct(slots.shape, jnp.bfloat16),
        ),
        compiler_params=pltpu.CompilerParams(vmem_limit_bytes=40 * 1024 * 1024),
        name="attend_blocks",
    )(slot_place, valid, queries, grads, keys, values, lse, delta, slots, slots, slots)


def request_table(choices, ring):
    number = choices.shape[0]
    active = choices >= 0
    owner = jnp.where(active, choices // 2, -1)
    position = jnp.arange(number, dtype=jnp.int32)
    same = (owner[:, None] == owner[None, :]) & active[None, :]
    same = same & (position[None, :] < position[:, None])
    rank = jnp.sum(same.astype(jnp.int32), axis=1)
    cls = owner // (2 * ring) * 2 + owner % 2
    slot = (cls * ring + owner // 2 % ring) * CAP + rank
    slot = jnp.where(active, slot, -1)
    unit = choices % 2 * KV_HEADS + position // CHOSEN_BLOCKS % KV_HEADS
    spot = jnp.arange(4 * ring * CAP, dtype=jnp.int32)
    match = slot[:, None] == spot[None, :]
    want = jnp.max(jnp.where(match, unit[:, None], -1), axis=0)
    want = want.reshape(4, 1, ring * CAP)
    want = jnp.pad(want, ((0, 0), (0, 7), (0, 128 - ring * CAP)), constant_values=-1)
    return jnp.maximum(slot, 0), active.astype(jnp.int32), want


def body(
    query_states,
    key_activations,
    value_activations,
    out_grad,
    logsumexp,
    row_delta,
    layer_input,
    chosen,
):
    shards = lax.axis_size("ctx")
    replicas = lax.axis_size("dp")
    ring = shards // 4
    slot_place, valid, want = request_table(chosen[0].reshape(-1), ring)
    keys, values = key_activations[0], value_activations[0]
    slots, wants = gather_call(ring, keys, values, want)

    def blockwise(stat):
        return (
            stat[0]
            .reshape(KV_HEADS, GROUP, 2, BLOCK_LENGTH)
            .transpose(2, 0, 1, 3)
            .reshape(2, KV_HEADS, 1, GROUP * BLOCK_LENGTH)
            .astype(jnp.float32)
        )

    query_grad, dk, dv, parts = attend_call(
        slot_place, valid, query_states[0], out_grad[0], keys, values,
        blockwise(logsumexp), blockwise(row_delta),
        slots.reshape(4 * ring * CAP, BLOCK_LENGTH, PAIR),
    )
    key_gradient, value_gradient = reduce_call(
        ring, parts.reshape(4, ring, CAP, BLOCK_LENGTH, PAIR), wants, dk, dv
    )
    weight_scale = 1.0 / math.sqrt(TOKENS * shards * replicas)
    key_weight_grad = lax.psum_scatter(
        jnp.einsum("td,tk->dk", layer_input[0], key_gradient, preferred_element_type=jnp.float32)
        * weight_scale,
        ("ctx", "dp"),
        scatter_dimension=0,
        tiled=True,
    )
    return (query_grad[None], key_gradient[None], value_gradient[None], key_weight_grad)


def solution(mesh):
    seq = P("dp", "ctx", None)
    stat = P("dp", None, "ctx")
    return jax.shard_map(
        body,
        mesh=mesh,
        in_specs=(seq, seq, seq, seq, stat, stat, seq, P("dp", "ctx", None, None)),
        out_specs=(seq, seq, seq, P(("ctx", "dp"), None)),
        check_vma=False,
    )
```

```python
import functools
import math

import jax
import jax.numpy as jnp
from jax import lax
from jax.experimental import pallas as pl
from jax.experimental.pallas import tpu as pltpu
from jax.sharding import PartitionSpec as P

HEAD_WIDTH = 128
BLOCK_LENGTH = 64
CHOSEN_BLOCKS = 3
CAP = 2
KV_HEADS = 4
GROUP = 4
TOKENS = 128
UNITS = TOKENS // BLOCK_LENGTH * KV_HEADS
PAIR = 2 * HEAD_WIDTH
MESH = pl.DeviceIdType.MESH


def place(ring):
    i = lax.axis_index("ctx")
    return i // (2 * ring), lax.rem(i // 2, ring), lax.rem(i, 2)


def member(ring, j):
    x, z, c = place(ring)
    mx = lax.rem(x + j // 2, 2)
    mc = lax.rem(c + j % 2, 2)
    return mx * (2 * ring) + z * 2 + mc, mx * 2 + mc


def along(ring, step):
    x, z, c = place(ring)
    return x * (2 * ring) + lax.rem(z + step + ring, ring) * 2 + c


def column_mate(step):
    i, d = lax.axis_index("ctx"), lax.axis_index("dp")
    rows = lax.axis_size("dp") // 2
    return {"ctx": i, "dp": lax.rem(d // 2 + step, rows) * 2 + lax.rem(d, 2)}


def row_mate(ring, j):
    x, z, c = place(ring)
    d = lax.axis_index("dp")
    lo, hi = lax.rem(x + j // 2, 2), lax.rem(lax.rem(d, 2) + j % 2, 2)
    return {"ctx": lo * (2 * ring) + z * 2 + c, "dp": d // 2 * 2 + hi}, lo, hi


def greet(others):
    barrier = pltpu.get_barrier_semaphore()
    for other in others:
        pl.semaphore_signal(barrier, inc=1, device_id=other, device_id_type=MESH)
    pl.semaphore_wait(barrier, len(others))


def neighbours(ring):
    places = [along(ring, 1), along(ring, -1)] + [member(ring, j)[0] for j in (1, 2, 3)]
    return [{"ctx": other} for other in places]


def push(src, dst, send, recv, other):
    other = other if isinstance(other, dict) else {"ctx": other}
    return pltpu.make_async_remote_copy(
        src_ref=src, dst_ref=dst, send_sem=send, recv_sem=recv,
        device_id=other, device_id_type=MESH,
    )


def gather_kernel(
    ring, rows_y, k_ref, v_ref, want_ref, x_ref, slots_ref, wants_ref, xg_ref,
    up, down, stage, work, want_smem, xt,
    up_send, up_recv, down_send, down_recv, w_send, w_recv, s_send, s_recv, local_sem, smem_sem,
    x_send, x_recv,
):
    half = ring // 2
    x, z, c = place(ring)
    cls = x * 2 + c
    above, below = along(ring, 1), along(ring, -1)
    greet(neighbours(ring) + [column_mate(t) for t in range(1, rows_y)])

    def up_copy(s, part, src=None):
        src = up.at[s - 1, part] if src is None else src
        return push(src, up.at[s, part], up_send.at[s, part], up_recv.at[s, part], above)

    def down_copy(s, part, src=None):
        src = down.at[s - 1, part] if src is None else src
        return push(src, down.at[s, part], down_send.at[s, part], down_recv.at[s, part], below)

    def want_copy(j):
        other, other_cls = member(ring, j)
        return push(want_ref.at[other_cls], wants_ref.at[j], w_send.at[j - 1], w_recv.at[j - 1], other)

    for j in (1, 2, 3):
        want_copy(j).start()
    for part, ref in ((0, k_ref), (1, v_ref)):
        up_copy(0, part, ref).start()
        down_copy(0, part, ref).start()

    own = pltpu.make_async_copy(want_ref.at[cls], wants_ref.at[0], smem_sem)
    own.start()
    own.wait()
    for j in (1, 2, 3):
        want_copy(j).wait()
    table = pltpu.make_async_copy(wants_ref, want_smem, smem_sem)
    table.start()
    table.wait()

    def slot_copy(j, r):
        owner = lax.rem(z + r, ring)
        return push(
            stage.at[r, j], slots_ref.at[cls, owner], s_send.at[j - 1, r], s_recv.at[j - 1, r],
            member(ring, j)[0],
        )

    def own_copy(r):
        return pltpu.make_async_copy(
            stage.at[r, 0], slots_ref.at[cls, lax.rem(z + r, ring)], local_sem.at[r]
        )

    def extract(r, keys, values):
        owner = lax.rem(z + r, ring)
        for b in range(2):
            for h in range(KV_HEADS):
                rows, lanes = pl.ds(b * BLOCK_LENGTH, BLOCK_LENGTH), pl.ds(h * HEAD_WIDTH, HEAD_WIDTH)
                work[b * KV_HEADS + h, :, :HEAD_WIDTH] = keys[rows, lanes]
                work[b * KV_HEADS + h, :, HEAD_WIDTH:] = values[rows, lanes]
        for j in range(4):
            for rank in range(CAP):
                unit = jnp.maximum(want_smem[j, 0, owner * CAP + rank], 0)
                stage[r, j, rank] = work[unit]
        for j in (1, 2, 3):
            slot_copy(j, r).start()
        own_copy(r).start()

    extract(0, k_ref, v_ref)

    y = lax.axis_index("dp") // 2
    lines = 16 * ring
    half_width = lines * rows_y

    def x_copy(t):
        return push(
            xt.at[t], xg_ref.at[:, :, pl.ds(pl.multiple_of(y * TOKENS, TOKENS), TOKENS)],
            x_send.at[t], x_recv.at[t], column_mate(t),
        )

    def keep_copy():
        return pltpu.make_async_copy(
            xt.at[0], xg_ref.at[:, :, pl.ds(pl.multiple_of(y * TOKENS, TOKENS), TOKENS)], x_send.at[0]
        )

    def deal(t):
        to = lax.rem(y + t, rows_y)
        line = lax.broadcasted_iota(jnp.int32, (lines, half_width), 0)
        column = lax.broadcasted_iota(jnp.int32, (lines, half_width), 1)
        core, high, spot = line // (8 * ring), line // (4 * ring) % 2, line % (4 * ring)
        source = spot // 4 * (16 * rows_y) + core * (8 * rows_y) + to * 8 + high * 4 + spot % 4
        pick = jnp.where(column == source, 1.0, 0.0).astype(jnp.bfloat16)
        for lo in range(2):
            part = x_ref[:, lo * half_width : (lo + 1) * half_width]
            xt[t, lo] = lax.dot_general(
                pick, part, (((1,), (1,)), ((), ())), preferred_element_type=jnp.float32
            ).astype(jnp.bfloat16)

    for t in range(rows_y):
        deal(t)
        if t == 0:
            keep_copy().start()
        else:
            x_copy(t).start()

    def step(s, _):
        for part in range(2):
            up_copy(s, part, k_ref).wait_recv()
            up_copy(s + 1, part).start()
            down_copy(s, part, k_ref).wait_recv()
            down_copy(s + 1, part).start()
        extract(ring - 1 - s, up.at[s, 0], up.at[s, 1])
        extract(1 + s, down.at[s, 0], down.at[s, 1])
        return 0

    lax.fori_loop(0, half - 2, step, 0)
    s = half - 2
    for part in range(2):
        up_copy(s, part, k_ref).wait_recv()
        if part == 0:
            up_copy(s + 1, part).start()
        down_copy(s, part, k_ref).wait_recv()
        if part == 1:
            down_copy(s + 1, part).start()
    extract(ring - 1 - s, up.at[s, 0], up.at[s, 1])
    extract(1 + s, down.at[s, 0], down.at[s, 1])
    up_copy(half - 1, 0, k_ref).wait_recv()
    down_copy(half - 1, 1, k_ref).wait_recv()
    extract(half, up.at[half - 1, 0], down.at[half - 1, 1])

    def drain(s, _):
        for part in range(2):
            up_copy(s, part, k_ref).wait_send()
            down_copy(s, part, k_ref).wait_send()
        return 0

    lax.fori_loop(0, half - 1, drain, 0)
    up_copy(half - 1, 0, k_ref).wait_send()
    down_copy(half - 1, 1, k_ref).wait_send()

    def drain_slots(r, _):
        for j in (1, 2, 3):
            slot_copy(j, r).wait()
        own_copy(r).wait()
        return 0

    lax.fori_loop(0, ring, drain_slots, 0)
    keep_copy().wait()
    for t in range(1, rows_y):
        x_copy(t).wait()


def gather_call(ring, rows_y, keys, values, want, inputs):
    half = ring // 2
    lines = 16 * ring
    ring_buffer = pltpu.VMEM((half, 2, TOKENS, KV_HEADS * HEAD_WIDTH), jnp.bfloat16)
    ring_sem = pltpu.SemaphoreType.DMA((half, 2))
    return pl.pallas_call(
        functools.partial(gather_kernel, ring, rows_y),
        out_shape=(
            jax.ShapeDtypeStruct((4, ring, CAP, BLOCK_LENGTH, PAIR), jnp.bfloat16),
            jax.ShapeDtypeStruct((4, 8, 128), jnp.int32),
            jax.ShapeDtypeStruct((2, lines, rows_y * TOKENS), jnp.bfloat16),
        ),
        in_specs=[pl.BlockSpec(memory_space=pltpu.VMEM)] * 4,
        out_specs=(
            pl.BlockSpec(memory_space=pl.ANY),
            pl.BlockSpec(memory_space=pltpu.VMEM),
            pl.BlockSpec(memory_space=pltpu.VMEM),
        ),
        scratch_shapes=[
            ring_buffer,
            ring_buffer,
            pltpu.VMEM((ring, 4, CAP, BLOCK_LENGTH, PAIR), jnp.bfloat16),
            pltpu.VMEM((UNITS, BLOCK_LENGTH, PAIR), jnp.bfloat16),
            pltpu.SMEM((4, 8, 128), jnp.int32),
            pltpu.VMEM((rows_y, 2, lines, TOKENS), jnp.bfloat16),
            ring_sem, ring_sem, ring_sem, ring_sem,
            pltpu.SemaphoreType.DMA((3,)),
            pltpu.SemaphoreType.DMA((3,)),
            pltpu.SemaphoreType.DMA((3, ring)),
            pltpu.SemaphoreType.DMA((3, ring)),
            pltpu.SemaphoreType.DMA((ring,)),
            pltpu.SemaphoreType.DMA,
            pltpu.SemaphoreType.DMA((rows_y,)),
            pltpu.SemaphoreType.DMA((rows_y,)),
        ],
        compiler_params=pltpu.CompilerParams(
            collective_id=0, has_side_effects=True, vmem_limit_bytes=40 * 1024 * 1024
        ),
        name="gather_blocks",
    )(keys, values, want, inputs)


def reduce_kernel(
    ring, rows_y, weight_scale,
    part_ref, wants_ref, dk_ref, dv_ref, xg_ref, kg_ref, vg_ref, wg_ref,
    up, down, ups, downs, arrived, want_smem, all_k, own, across, shared, from_x, pieces, from_z,
    up_send, up_recv, down_send, down_recv, s_send, s_recv, smem_sem,
    y_send, y_recv, c_send, c_recv, x_send, x_recv, z_send, z_recv,
):
    half = ring // 2
    x, z, c = place(ring)
    high = lax.rem(lax.axis_index("dp"), 2)
    cls = x * 2 + c
    above, below = along(ring, 1), along(ring, -1)
    far_x = [row_mate(ring, j)[0] for j in (1, 3)]
    far_z = [{"ctx": along(ring, d)} for d in range(2, ring - 1)]
    greet(neighbours(ring) + [column_mate(t) for t in range(1, rows_y)] + far_x + far_z)

    def slot_copy(part, j, r):
        other, other_cls = member(ring, j)
        owner = lax.rem(z + r, ring)
        return push(
            part_ref.at[part, other_cls, owner], arrived.at[part, j - 1, r],
            s_send.at[part, j - 1, r], s_recv.at[part, j - 1, r], other,
        )

    def send_slots(part):
        for j in (1, 2, 3):
            slot_copy(part, j, half).start()

        def some(s, _):
            for j in (1, 2, 3):
                slot_copy(part, j, half - s).start()
                slot_copy(part, j, half + s).start()
            return 0

        lax.fori_loop(1, half, some, 0)
        for j in (1, 2, 3):
            slot_copy(part, j, 0).start()

    send_slots(0)
    table = pltpu.make_async_copy(wants_ref, want_smem, smem_sem)
    table.start()
    blank = jnp.zeros((BLOCK_LENGTH, KV_HEADS * HEAD_WIDTH), jnp.bfloat16)
    for part in range(2):
        up[part, 0, 1] = blank
        down[part, 0, 0] = blank
    table.wait()

    def up_copy(part, s, b):
        return push(
            ups.at[part, s, b], up.at[part, s, b], up_send.at[part, s, b], up_recv.at[part, s, b], above
        )

    def down_copy(part, s, b):
        return push(
            downs.at[part, s, b], down.at[part, s, b],
            down_send.at[part, s, b], down_recv.at[part, s, b], below,
        )

    def total(part, r, b, incoming, targets):
        owner = lax.rem(z + r, ring)
        units = [[want_smem[j, 0, owner * CAP + rank] for rank in range(CAP)] for j in range(4)]
        for h in range(KV_HEADS):
            lanes = slice(h * HEAD_WIDTH, (h + 1) * HEAD_WIDTH)
            acc = jnp.zeros((BLOCK_LENGTH, HEAD_WIDTH), jnp.float32)
            for ref in incoming:
                acc = acc + ref[:, lanes].astype(jnp.float32)
            for j in range(4):
                for rank in range(CAP):
                    if j == 0:
                        term = part_ref[part, cls, owner, rank]
                    else:
                        term = arrived[part, j - 1, r, rank]
                    hit = units[j][rank] == b * KV_HEADS + h
                    acc = acc + jnp.where(hit, term.astype(jnp.float32), 0.0)
            for target in targets:
                target[:, lanes] = acc.astype(jnp.bfloat16)

    def phase(part, hooks, after):
        for j in (1, 2, 3):
            slot_copy(part, j, half).wait_recv()
        total(part, half, 0, [], [ups.at[part, 0, 0]])
        up_copy(part, 0, 0).start()
        total(part, half, 1, [], [downs.at[part, 0, 1]])
        down_copy(part, 0, 1).start()

        def step(s, _):
            for j in (1, 2, 3):
                slot_copy(part, j, half - s).wait_recv()
                slot_copy(part, j, half + s).wait_recv()
            up_copy(part, s - 1, 0).wait_recv()
            total(part, half - s, 0, [up.at[part, s - 1, 0]], [ups.at[part, s, 0]])
            up_copy(part, s, 0).start()
            down_copy(part, s - 1, 1).wait_recv()
            total(part, half + s, 1, [down.at[part, s - 1, 1]], [downs.at[part, s, 1]])
            down_copy(part, s, 1).start()

            @pl.when(s > 1)
            def _():
                up_copy(part, s - 1, 1).wait_recv()
                down_copy(part, s - 1, 0).wait_recv()

            total(part, half - s, 1, [up.at[part, s - 1, 1]], [ups.at[part, s, 1]])
            up_copy(part, s, 1).start()
            total(part, half + s, 0, [down.at[part, s - 1, 0]], [downs.at[part, s, 0]])
            down_copy(part, s, 0).start()
            for at, hook in hooks.items():
                pl.when(s == at)(hook)
            return 0

        lax.fori_loop(1, half, step, 0)
        for j in (1, 2, 3):
            slot_copy(part, j, 0).wait_recv()
        near, outs = ((dk_ref, (kg_ref, own)), (dv_ref, (vg_ref,)))[part]
        for b in range(2):
            up_copy(part, half - 1, b).wait_recv()
            down_copy(part, half - 1, b).wait_recv()
            rows = pl.ds(b * BLOCK_LENGTH, BLOCK_LENGTH)
            total(
                part, 0, b,
                [near.at[rows], up.at[part, half - 1, b], down.at[part, half - 1, b]],
                [out.at[rows] for out in outs],
            )
        after()

    y = lax.axis_index("dp") // 2

    def y_copy(t):
        return push(own, all_k.at[y], y_send.at[t - 1], y_recv.at[t - 1], column_mate(t))

    def c_copy():
        return push(across.at[:, 1 - c], shared, c_send, c_recv, member(ring, 1)[0])

    def x_copy(j):
        mate, lo, hi = row_mate(ring, j)
        return push(
            across.at[lo, c, hi], from_x.at[j - 1], x_send.at[j - 1], x_recv.at[j - 1], mate
        )

    def z_copy(d):
        return push(
            pieces.at[lax.rem(z + d, ring)], from_z.at[d - 1],
            z_send.at[d - 1], z_recv.at[d - 1], along(ring, d),
        )

    def start_weights():
        for t in range(1, rows_y):
            y_copy(t).start()
        all_k[y] = own[...]
        send_slots(1)

    def multiply():
        for t in range(1, rows_y):
            y_copy(t).wait_recv()
        gathered = all_k[...].reshape(rows_y * TOKENS, KV_HEADS * HEAD_WIDTH)
        for lo in range(2):
            product = jnp.dot(xg_ref[lo], gathered, preferred_element_type=jnp.float32)
            for core in range(2):
                for hi in range(2):
                    begin = (core * 2 + hi) * 4 * ring
                    across[lo, core, hi] = product[begin : begin + 4 * ring]
        c_copy().start()

    def add_core():
        c_copy().wait()
        for lo in range(2):
            for hi in range(2):
                across[lo, c, hi] += shared[lo, hi]
        for j in (1, 2, 3):
            x_copy(j).start()

    def add_row():
        for j in (1, 2, 3):
            x_copy(j).wait()
        value = across[x, c, high] + from_x[0] + from_x[1] + from_x[2]
        for i in range(ring):
            pieces[i] = value[4 * i : 4 * i + 4]
        for d in range(1, ring):
            z_copy(d).start()

    def nothing():
        pass

    phase(0, {}, start_weights)
    hooks = {2: multiply, 4: add_core, 6: add_row} if half >= 8 else {}
    phase(1, hooks, nothing)
    if not hooks:
        multiply()
        add_core()
        add_row()
    value = pieces[z]
    for d in range(1, ring):
        z_copy(d).wait_recv()
        value = value + from_z[d - 1]
    wg_ref[...] = value * weight_scale

    for t in range(1, rows_y):
        y_copy(t).wait_send()
    for d in range(1, ring):
        z_copy(d).wait_send()
    for part in range(2):
        up_copy(part, 0, 0).wait_send()
        down_copy(part, 0, 1).wait_send()

        def drain(s, _):
            for b in range(2):
                up_copy(part, s, b).wait_send()
                down_copy(part, s, b).wait_send()
            return 0

        lax.fori_loop(1, half, drain, 0)

        def drain_slots(r, _):
            for j in (1, 2, 3):
                slot_copy(part, j, r).wait_send()
            return 0

        lax.fori_loop(0, ring, drain_slots, 0)


def reduce_call(ring, rows_y, weight_scale, parts, wants, dk, dv, xg):
    half = ring // 2
    width = KV_HEADS * HEAD_WIDTH
    ring_buffer = pltpu.VMEM((2, half, 2, BLOCK_LENGTH, width), jnp.bfloat16)
    ring_sem = pltpu.SemaphoreType.DMA((2, half, 2))
    dma = pltpu.SemaphoreType.DMA
    return pl.pallas_call(
        functools.partial(reduce_kernel, ring, rows_y, weight_scale),
        out_shape=(
            jax.ShapeDtypeStruct((TOKENS, width), jnp.bfloat16),
            jax.ShapeDtypeStruct((TOKENS, width), jnp.bfloat16),
            jax.ShapeDtypeStruct((4, width), jnp.float32),
        ),
        in_specs=[pl.BlockSpec(memory_space=pltpu.VMEM)] * 5,
        out_specs=(pl.BlockSpec(memory_space=pltpu.VMEM),) * 3,
        scratch_shapes=[
            ring_buffer, ring_buffer, ring_buffer, ring_buffer,
            pltpu.VMEM((2, 3, ring, CAP, BLOCK_LENGTH, HEAD_WIDTH), jnp.bfloat16),
            pltpu.SMEM((4, 8, 128), jnp.int32),
            pltpu.VMEM((rows_y, TOKENS, width), jnp.bfloat16),
            pltpu.VMEM((TOKENS, width), jnp.bfloat16),
            pltpu.VMEM((2, 2, 2, 4 * ring, width), jnp.float32),
            pltpu.VMEM((2, 2, 4 * ring, width), jnp.float32),
            pltpu.VMEM((3, 4 * ring, width), jnp.float32),
            pltpu.VMEM((ring, 4, width), jnp.float32),
            pltpu.VMEM((ring - 1, 4, width), jnp.float32),
            ring_sem, ring_sem, ring_sem, ring_sem,
            dma((2, 3, ring)), dma((2, 3, ring)), dma,
            dma((rows_y - 1,)), dma((rows_y - 1,)), dma, dma,
            dma((3,)), dma((3,)), dma((ring - 1,)), dma((ring - 1,)),
        ],
        compiler_params=pltpu.CompilerParams(
            collective_id=1, has_side_effects=True, vmem_limit_bytes=48 * 1024 * 1024
        ),
        name="reduce_blocks",
    )(parts, wants, dk, dv, xg)


def attend_kernel(
    place_ref, valid_ref, q_ref, g_ref, k_ref, v_ref, lse_ref, delta_ref, f0, f1, f2,
    dq_ref, dk_ref, dv_ref, part_ref,
):
    h, b = pl.program_id(0), pl.program_id(1)
    scale = HEAD_WIDTH ** (-0.5)
    first = (b * KV_HEADS + h) * CHOSEN_BLOCKS
    fetched = (f0, f1, f2)
    local = TOKENS
    keys_n = local + CHOSEN_BLOCKS * BLOCK_LENGTH
    rows_n = GROUP * BLOCK_LENGTH

    @pl.when((h == 0) & (b == 0))
    def _():
        part_ref[...] = jnp.zeros_like(part_ref)

    def stack(ref):
        return jnp.concatenate(
            [ref[:, i * HEAD_WIDTH : (i + 1) * HEAD_WIDTH] for i in range(GROUP)], axis=0
        )

    queries, grads = stack(q_ref), stack(g_ref)
    zero = jnp.zeros((BLOCK_LENGTH, PAIR), jnp.bfloat16)
    far = [jnp.where(valid_ref[first + i] > 0, ref[0], zero) for i, ref in enumerate(fetched)]
    keys = jnp.concatenate([k_ref[...]] + [f[:, :HEAD_WIDTH] for f in far], axis=0)
    values = jnp.concatenate([v_ref[...]] + [f[:, HEAD_WIDTH:] for f in far], axis=0)
    row = lax.broadcasted_iota(jnp.int32, (keys_n, rows_n), 1) % BLOCK_LENGTH + b * BLOCK_LENGTH
    key = lax.broadcasted_iota(jnp.int32, (keys_n, rows_n), 0)
    mask = (key < local) & (key <= row)
    for i in range(CHOSEN_BLOCKS):
        begin = local + i * BLOCK_LENGTH
        limit = jnp.where(valid_ref[first + i] > 0, begin + BLOCK_LENGTH, begin)
        mask = mask | ((key >= begin) & (key < limit))
    nt = (((1,), (1,)), ((), ()))
    tn = (((0,), (0,)), ((), ()))
    scores = lax.dot_general(keys, queries, nt, preferred_element_type=jnp.float32) * scale
    prob = jnp.where(mask, jnp.exp(scores - lse_ref[0, 0]), 0.0)
    dprob = lax.dot_general(values, grads, nt, preferred_element_type=jnp.float32)
    dscore = (prob * (dprob - delta_ref[0, 0])).astype(jnp.bfloat16)
    prob_low = prob.astype(jnp.bfloat16)
    dq = (lax.dot_general(dscore, keys, tn, preferred_element_type=jnp.float32) * scale).astype(
        jnp.bfloat16
    )
    for i in range(GROUP):
        dq_ref[:, i * HEAD_WIDTH : (i + 1) * HEAD_WIDTH] = dq[
            i * BLOCK_LENGTH : (i + 1) * BLOCK_LENGTH
        ]
    dk = jnp.dot(dscore, queries, preferred_element_type=jnp.float32) * scale
    dv = jnp.dot(prob_low, grads, preferred_element_type=jnp.float32)

    @pl.when(b == 0)
    def _():
        dk_ref[...] = dk[:local]
        dv_ref[...] = dv[:local]

    @pl.when(b > 0)
    def _():
        dk_ref[...] += dk[:local]
        dv_ref[...] += dv[:local]

    for i in range(CHOSEN_BLOCKS):
        lo = local + i * BLOCK_LENGTH

        @pl.when(valid_ref[first + i] > 0)
        def _():
            slot = place_ref[first + i]
            part_ref[0, slot] = dk[lo : lo + BLOCK_LENGTH].astype(jnp.bfloat16)
            part_ref[1, slot] = dv[lo : lo + BLOCK_LENGTH].astype(jnp.bfloat16)


def attend_call(slot_place, valid, queries, grads, keys, values, lse, delta, slots):
    slot_total = slots.shape[0]
    group_width = GROUP * HEAD_WIDTH

    def far_spec(i):
        return pl.BlockSpec(
            (1, BLOCK_LENGTH, PAIR),
            lambda h, b, sp, va: (sp[(b * KV_HEADS + h) * CHOSEN_BLOCKS + i], 0, 0),
        )

    rows = pl.BlockSpec((BLOCK_LENGTH, group_width), lambda h, b, sp, va: (b, h))
    shard = pl.BlockSpec((TOKENS, HEAD_WIDTH), lambda h, b, sp, va: (0, h))
    stat = pl.BlockSpec((1, 1, 1, GROUP * BLOCK_LENGTH), lambda h, b, sp, va: (b, h, 0, 0))
    return pl.pallas_call(
        attend_kernel,
        grid_spec=pltpu.PrefetchScalarGridSpec(
            num_scalar_prefetch=2,
            grid=(KV_HEADS, TOKENS // BLOCK_LENGTH),
            in_specs=[rows, rows, shard, shard, stat, stat, far_spec(0), far_spec(1), far_spec(2)],
            out_specs=[
                rows,
                shard,
                shard,
                pl.BlockSpec(
                    (2, slot_total, BLOCK_LENGTH, HEAD_WIDTH), lambda h, b, sp, va: (0, 0, 0, 0)
                ),
            ],
        ),
        out_shape=(
            jax.ShapeDtypeStruct(queries.shape, jnp.bfloat16),
            jax.ShapeDtypeStruct(keys.shape, jnp.float32),
            jax.ShapeDtypeStruct(keys.shape, jnp.float32),
            jax.ShapeDtypeStruct((2, slot_total, BLOCK_LENGTH, HEAD_WIDTH), jnp.bfloat16),
        ),
        compiler_params=pltpu.CompilerParams(vmem_limit_bytes=40 * 1024 * 1024),
        name="attend_blocks",
    )(slot_place, valid, queries, grads, keys, values, lse, delta, slots, slots, slots)


def request_table(choices, ring):
    number = choices.shape[0]
    active = choices >= 0
    owner = jnp.where(active, choices // 2, -1)
    position = jnp.arange(number, dtype=jnp.int32)
    same = (owner[:, None] == owner[None, :]) & active[None, :]
    same = same & (position[None, :] < position[:, None])
    rank = jnp.sum(same.astype(jnp.int32), axis=1)
    cls = owner // (2 * ring) * 2 + owner % 2
    slot = (cls * ring + owner // 2 % ring) * CAP + rank
    slot = jnp.where(active, slot, -1)
    unit = choices % 2 * KV_HEADS + position // CHOSEN_BLOCKS % KV_HEADS
    spot = jnp.arange(4 * ring * CAP, dtype=jnp.int32)
    match = slot[:, None] == spot[None, :]
    want = jnp.max(jnp.where(match, unit[:, None], -1), axis=0)
    want = want.reshape(4, 1, ring * CAP)
    want = jnp.pad(want, ((0, 0), (0, 7), (0, 128 - ring * CAP)), constant_values=-1)
    return jnp.maximum(slot, 0), active.astype(jnp.int32), want


def body(
    query_states,
    key_activations,
    value_activations,
    out_grad,
    logsumexp,
    row_delta,
    layer_input,
    chosen,
):
    shards = lax.axis_size("ctx")
    replicas = lax.axis_size("dp")
    ring = shards // 4
    slot_place, valid, want = request_table(chosen[0].reshape(-1), ring)
    keys, values = key_activations[0], value_activations[0]
    rows_y = replicas // 2
    slots, wants, xg = gather_call(ring, rows_y, keys, values, want, layer_input[0])

    def blockwise(stat):
        return (
            stat[0]
            .reshape(KV_HEADS, GROUP, 2, BLOCK_LENGTH)
            .transpose(2, 0, 1, 3)
            .reshape(2, KV_HEADS, 1, GROUP * BLOCK_LENGTH)
            .astype(jnp.float32)
        )

    query_grad, dk, dv, parts = attend_call(
        slot_place, valid, query_states[0], out_grad[0], keys, values,
        blockwise(logsumexp), blockwise(row_delta),
        slots.reshape(4 * ring * CAP, BLOCK_LENGTH, PAIR),
    )
    weight_scale = 1.0 / math.sqrt(TOKENS * shards * replicas)
    key_gradient, value_gradient, key_weight_grad = reduce_call(
        ring, rows_y, weight_scale,
        parts.reshape(2, 4, ring, CAP, BLOCK_LENGTH, HEAD_WIDTH), wants, dk, dv, xg,
    )
    return (query_grad[None], key_gradient[None], value_gradient[None], key_weight_grad)


def solution(mesh):
    seq = P("dp", "ctx", None)
    stat = P("dp", None, "ctx")
    return jax.shard_map(
        body,
        mesh=mesh,
        in_specs=(seq, seq, seq, seq, stat, stat, seq, P("dp", "ctx", None, None)),
        out_specs=(seq, seq, seq, P(("ctx", "dp"), None)),
        check_vma=False,
    )
```

```python
import functools
import math

import jax
import jax.numpy as jnp
from jax import lax
from jax.experimental import pallas as pl
from jax.experimental.pallas import tpu as pltpu
from jax.sharding import PartitionSpec as P

HEAD_WIDTH = 128
BLOCK_LENGTH = 64
CHOSEN_BLOCKS = 3
CAP = 2
KV_HEADS = 4
GROUP = 4
TOKENS = 128
UNITS = TOKENS // BLOCK_LENGTH * KV_HEADS
PAIR = 2 * HEAD_WIDTH
LAG = 4
AHEAD = 3
VMEM_BYTES = 58 * 1024 * 1024
MESH = pl.DeviceIdType.MESH


def place(ring):
    i = lax.axis_index("ctx")
    return i // (2 * ring), lax.rem(i // 2, ring), lax.rem(i, 2)


def member(ring, j):
    x, z, c = place(ring)
    mx = lax.rem(x + j // 2, 2)
    mc = lax.rem(c + j % 2, 2)
    return mx * (2 * ring) + z * 2 + mc, mx * 2 + mc


def along(ring, step):
    x, z, c = place(ring)
    return x * (2 * ring) + lax.rem(z + step + ring, ring) * 2 + c


def column_mate(step):
    i, d = lax.axis_index("ctx"), lax.axis_index("dp")
    rows = lax.axis_size("dp") // 2
    return {"ctx": i, "dp": lax.rem(d // 2 + step, rows) * 2 + lax.rem(d, 2)}


def row_mate(ring, j):
    x, z, c = place(ring)
    d = lax.axis_index("dp")
    lo, hi = lax.rem(x + j // 2, 2), lax.rem(lax.rem(d, 2) + j % 2, 2)
    return {"ctx": lo * (2 * ring) + z * 2 + c, "dp": d // 2 * 2 + hi}, lo, hi


def greet(others):
    barrier = pltpu.get_barrier_semaphore()
    for other in others:
        pl.semaphore_signal(barrier, inc=1, device_id=other, device_id_type=MESH)
    pl.semaphore_wait(barrier, len(others))


def neighbours(ring):
    places = [along(ring, 1), along(ring, -1)] + [member(ring, j)[0] for j in (1, 2, 3)]
    return [{"ctx": other} for other in places]


def push(src, dst, send, recv, other):
    other = other if isinstance(other, dict) else {"ctx": other}
    return pltpu.make_async_remote_copy(
        src_ref=src, dst_ref=dst, send_sem=send, recv_sem=recv,
        device_id=other, device_id_type=MESH,
    )


def gather_kernel(
    ring, rows_y, chosen_ref, k_ref, v_ref, x_ref, slots_ref, wants_ref, index_ref, meta_ref, xg_ref,
    up, down, stage, work, want, want_smem, xt, near, xin,
    up_send, up_recv, down_send, down_recv, w_send, w_recv, s_send, s_recv, local_sem, smem_sem,
    x_send, x_recv, in_sem,
):
    half = ring // 2
    x, z, c = place(ring)
    cls = x * 2 + c
    above, below = along(ring, 1), along(ring, -1)
    loads = [
        pltpu.make_async_copy(k_ref, near.at[0], in_sem.at[0]),
        pltpu.make_async_copy(v_ref, near.at[1], in_sem.at[1]),
        pltpu.make_async_copy(x_ref, xin, in_sem.at[2]),
    ]
    for load in loads:
        load.start()
    greet(neighbours(ring) + [column_mate(t) for t in range(1, rows_y)])

    def up_copy(s, part, src=None):
        src = up.at[s - 1, part] if src is None else src
        return push(src, up.at[s, part], up_send.at[s, part], up_recv.at[s, part], above)

    def down_copy(s, part, src=None):
        src = down.at[s - 1, part] if src is None else src
        return push(src, down.at[s, part], down_send.at[s, part], down_recv.at[s, part], below)

    for part, ref in ((0, k_ref), (1, v_ref)):
        up_copy(0, part, ref).start()
        down_copy(0, part, ref).start()

    shape = (4, 8, 128)
    spot = lax.broadcasted_iota(jnp.int32, shape, 0) * 128 + lax.broadcasted_iota(jnp.int32, shape, 2)
    wanted = jnp.full(shape, -1, jnp.int32)
    index = jnp.zeros(shape, jnp.int32)
    owners = []
    for i in range(2 * KV_HEADS * CHOSEN_BLOCKS):
        choice = chosen_ref[i]
        active = choice >= 0
        block = jnp.maximum(choice, 0)
        owner = block // 2
        marked = jnp.where(active, owner, -1)
        rank = jnp.int32(0)
        for other in owners:
            rank = rank + jnp.where(other == marked, 1, 0)
        owners.append(marked)
        line = (owner // (2 * ring)) * 2 + lax.rem(owner, 2)
        entry = lax.rem(owner // 2, ring) * CAP + rank
        hit = spot == jnp.where(active, line * 128 + entry, -1)
        wanted = jnp.where(hit, lax.rem(block, 2) * KV_HEADS + i // CHOSEN_BLOCKS % KV_HEADS, wanted)
        index = jnp.where(hit, i, index)
        meta_ref[i] = jnp.where(active, line * ring * CAP + entry, 0)
        meta_ref[64 + i] = jnp.where(active, 1, 0)
    want[...] = wanted
    index_ref[...] = index

    def want_copy(j):
        other, other_cls = member(ring, j)
        return push(want.at[other_cls], wants_ref.at[j], w_send.at[j - 1], w_recv.at[j - 1], other)

    for j in (1, 2, 3):
        want_copy(j).start()
    wants_ref[0] = want[cls]

    y = lax.axis_index("dp") // 2
    lines = 16 * ring
    half_width = lines * rows_y

    def x_copy(t):
        return push(
            xt.at[t], xg_ref.at[:, :, pl.ds(pl.multiple_of(y * TOKENS, TOKENS), TOKENS)],
            x_send.at[t], x_recv.at[t], column_mate(t),
        )

    def keep_copy():
        return pltpu.make_async_copy(
            xt.at[0], xg_ref.at[:, :, pl.ds(pl.multiple_of(y * TOKENS, TOKENS), TOKENS)], x_send.at[0]
        )

    def deal(t):
        to = lax.rem(y + t, rows_y)
        line = lax.broadcasted_iota(jnp.int32, (lines, half_width), 0)
        column = lax.broadcasted_iota(jnp.int32, (lines, half_width), 1)
        core, high, rest = line // (8 * ring), line // (4 * ring) % 2, line % (4 * ring)
        source = rest // 4 * (16 * rows_y) + core * (8 * rows_y) + to * 8 + high * 4 + rest % 4
        pick = jnp.where(column == source, 1.0, 0.0).astype(jnp.bfloat16)
        for lo in range(2):
            part = xin[:, lo * half_width : (lo + 1) * half_width]
            xt[t, lo] = lax.dot_general(
                pick, part, (((1,), (1,)), ((), ())), preferred_element_type=jnp.float32
            ).astype(jnp.bfloat16)

    for load in loads:
        load.wait()
    for j in (1, 2, 3):
        want_copy(j).wait()
    table = pltpu.make_async_copy(wants_ref, want_smem, smem_sem)
    table.start()
    table.wait()

    def slot_copy(j, r):
        owner = lax.rem(z + r, ring)
        return push(
            stage.at[r, j], slots_ref.at[cls, owner], s_send.at[j - 1, r], s_recv.at[j - 1, r],
            member(ring, j)[0],
        )

    def own_copy(r):
        return pltpu.make_async_copy(
            stage.at[r, 0], slots_ref.at[cls, lax.rem(z + r, ring)], local_sem.at[r]
        )

    def extract(r, keys, values):
        owner = lax.rem(z + r, ring)
        for b in range(2):
            for h in range(KV_HEADS):
                rows, lanes = pl.ds(b * BLOCK_LENGTH, BLOCK_LENGTH), pl.ds(h * HEAD_WIDTH, HEAD_WIDTH)
                work[b * KV_HEADS + h, :, :HEAD_WIDTH] = keys[rows, lanes]
                work[b * KV_HEADS + h, :, HEAD_WIDTH:] = values[rows, lanes]
        for j in (2, 3, 1, 0):
            for rank in range(CAP):
                unit = jnp.maximum(want_smem[j, 0, owner * CAP + rank], 0)
                stage[r, j, rank] = work[unit]
            if j:
                slot_copy(j, r).start()
        own_copy(r).start()

    extract(0, near.at[0], near.at[1])
    for t in range(rows_y):
        deal(t)
        if t == 0:
            keep_copy().start()
        else:
            x_copy(t).start()

    def step(s, _):
        for part in range(2):
            up_copy(s, part, k_ref).wait_recv()
            up_copy(s + 1, part).start()
            down_copy(s, part, k_ref).wait_recv()
            down_copy(s + 1, part).start()
        extract(ring - 1 - s, up.at[s, 0], up.at[s, 1])
        extract(1 + s, down.at[s, 0], down.at[s, 1])
        return 0

    lax.fori_loop(0, half - 2, step, 0)
    s = half - 2
    for part in range(2):
        up_copy(s, part, k_ref).wait_recv()
        if part == 0:
            up_copy(s + 1, part).start()
        down_copy(s, part, k_ref).wait_recv()
        if part == 1:
            down_copy(s + 1, part).start()
    extract(ring - 1 - s, up.at[s, 0], up.at[s, 1])
    extract(1 + s, down.at[s, 0], down.at[s, 1])
    up_copy(half - 1, 0, k_ref).wait_recv()
    down_copy(half - 1, 1, k_ref).wait_recv()
    extract(half, up.at[half - 1, 0], down.at[half - 1, 1])

    def drain(s, _):
        for part in range(2):
            up_copy(s, part, k_ref).wait_send()
            down_copy(s, part, k_ref).wait_send()
        return 0

    lax.fori_loop(0, half - 1, drain, 0)
    up_copy(half - 1, 0, k_ref).wait_send()
    down_copy(half - 1, 1, k_ref).wait_send()

    def drain_slots(r, _):
        for j in (1, 2, 3):
            slot_copy(j, r).wait()
        own_copy(r).wait()
        return 0

    lax.fori_loop(0, ring, drain_slots, 0)
    keep_copy().wait()
    for t in range(1, rows_y):
        x_copy(t).wait()


def gather_call(ring, rows_y, chosen, keys, values, inputs):
    half = ring // 2
    lines = 16 * ring
    ring_buffer = pltpu.VMEM((half, 2, TOKENS, KV_HEADS * HEAD_WIDTH), jnp.bfloat16)
    ring_sem = pltpu.SemaphoreType.DMA((half, 2))
    hbm, vmem = pl.BlockSpec(memory_space=pl.ANY), pl.BlockSpec(memory_space=pltpu.VMEM)
    smem = pl.BlockSpec(memory_space=pltpu.SMEM)
    dma = pltpu.SemaphoreType.DMA
    return pl.pallas_call(
        functools.partial(gather_kernel, ring, rows_y),
        out_shape=(
            jax.ShapeDtypeStruct((4, ring, CAP, BLOCK_LENGTH, PAIR), jnp.bfloat16),
            jax.ShapeDtypeStruct((4, 8, 128), jnp.int32),
            jax.ShapeDtypeStruct((4, 8, 128), jnp.int32),
            jax.ShapeDtypeStruct((128,), jnp.int32),
            jax.ShapeDtypeStruct((2, lines, rows_y * TOKENS), jnp.bfloat16),
        ),
        in_specs=[smem, hbm, hbm, hbm],
        out_specs=(hbm, vmem, vmem, smem, vmem),
        scratch_shapes=[
            ring_buffer,
            ring_buffer,
            pltpu.VMEM((ring, 4, CAP, BLOCK_LENGTH, PAIR), jnp.bfloat16),
            pltpu.VMEM((UNITS, BLOCK_LENGTH, PAIR), jnp.bfloat16),
            pltpu.VMEM((4, 8, 128), jnp.int32),
            pltpu.SMEM((4, 8, 128), jnp.int32),
            pltpu.VMEM((rows_y, 2, lines, TOKENS), jnp.bfloat16),
            pltpu.VMEM((2,) + keys.shape, jnp.bfloat16),
            pltpu.VMEM(inputs.shape, jnp.bfloat16),
            ring_sem, ring_sem, ring_sem, ring_sem,
            dma((3,)), dma((3,)), dma((3, ring)), dma((3, ring)), dma((ring,)), dma,
            dma((rows_y,)), dma((rows_y,)), dma((3,)),
        ],
        compiler_params=pltpu.CompilerParams(
            collective_id=0, has_side_effects=True, vmem_limit_bytes=VMEM_BYTES
        ),
        name="gather_blocks",
    )(chosen, keys, values, inputs)


def attend_kernel(
    meta_ref, q_ref, g_ref, k_ref, v_ref, lse_ref, delta_ref, slots_ref,
    dq_ref, dk_ref, dv_ref, part_ref, q, g, k, v, far, in_sem, far_sem,
):
    scale = HEAD_WIDTH ** (-0.5)
    inputs = [
        pltpu.make_async_copy(src, dst, in_sem.at[i])
        for i, (src, dst) in enumerate(((q_ref, q), (g_ref, g), (k_ref, k), (v_ref, v)))
    ]
    number = 2 * KV_HEADS * CHOSEN_BLOCKS
    fetches = [
        pltpu.make_async_copy(slots_ref.at[meta_ref[i]], far.at[i], far_sem.at[i])
        for i in range(number)
    ]
    for copy in inputs + fetches:
        copy.start()
    lse, delta = lse_ref[...].astype(jnp.float32), delta_ref[...].astype(jnp.float32)
    rows_n = GROUP * BLOCK_LENGTH
    nt = (((1,), (1,)), ((), ()))
    tn = (((0,), (0,)), ((), ()))

    def line(stat, h, b):
        return jnp.concatenate(
            [
                stat[h * GROUP + i : h * GROUP + i + 1, b * BLOCK_LENGTH : (b + 1) * BLOCK_LENGTH]
                for i in range(GROUP)
            ],
            axis=1,
        )

    def stack(ref, h, b):
        rows = slice(b * BLOCK_LENGTH, (b + 1) * BLOCK_LENGTH)
        heads = [h * GROUP + i for i in range(GROUP)]
        return jnp.concatenate(
            [ref[rows, i * HEAD_WIDTH : (i + 1) * HEAD_WIDTH] for i in heads], axis=0
        )

    for copy in inputs + fetches:
        copy.wait()
    for h in range(KV_HEADS):
        lanes = slice(h * HEAD_WIDTH, (h + 1) * HEAD_WIDTH)
        for b in range(2):
            first = (b * KV_HEADS + h) * CHOSEN_BLOCKS
            local = (b + 1) * BLOCK_LENGTH
            keys_n = local + CHOSEN_BLOCKS * BLOCK_LENGTH
            queries, grads = stack(q, h, b), stack(g, h, b)
            chosen = [far[first + i] for i in range(CHOSEN_BLOCKS)]
            keys = jnp.concatenate([k[:local, lanes]] + [f[:, :HEAD_WIDTH] for f in chosen], axis=0)
            values = jnp.concatenate([v[:local, lanes]] + [f[:, HEAD_WIDTH:] for f in chosen], axis=0)
            row = lax.broadcasted_iota(jnp.int32, (keys_n, rows_n), 1) % BLOCK_LENGTH
            key = lax.broadcasted_iota(jnp.int32, (keys_n, rows_n), 0)
            mask = (key < local) & (key <= row + b * BLOCK_LENGTH)
            for i in range(CHOSEN_BLOCKS):
                begin = local + i * BLOCK_LENGTH
                limit = jnp.where(meta_ref[64 + first + i] > 0, begin + BLOCK_LENGTH, begin)
                mask = mask | ((key >= begin) & (key < limit))
            scores = lax.dot_general(keys, queries, nt, preferred_element_type=jnp.float32) * scale
            prob = jnp.where(mask, jnp.exp(scores - line(lse, h, b)), 0.0)
            dprob = lax.dot_general(values, grads, nt, preferred_element_type=jnp.float32)
            dscore = (prob * (dprob - line(delta, h, b))).astype(jnp.bfloat16)
            prob_low = prob.astype(jnp.bfloat16)
            dq = lax.dot_general(dscore, keys, tn, preferred_element_type=jnp.float32) * scale
            dq = dq.astype(jnp.bfloat16)
            for i in range(GROUP):
                head = h * GROUP + i
                dq_ref[
                    b * BLOCK_LENGTH : (b + 1) * BLOCK_LENGTH,
                    head * HEAD_WIDTH : (head + 1) * HEAD_WIDTH,
                ] = dq[i * BLOCK_LENGTH : (i + 1) * BLOCK_LENGTH]
            dk = jnp.dot(dscore, queries, preferred_element_type=jnp.float32) * scale
            dv = jnp.dot(prob_low, grads, preferred_element_type=jnp.float32)
            for out, grad in ((dk_ref, dk), (dv_ref, dv)):
                if b == 0:
                    out[:BLOCK_LENGTH, lanes] = grad[:BLOCK_LENGTH]
                else:
                    out[:BLOCK_LENGTH, lanes] += grad[:BLOCK_LENGTH]
                    out[BLOCK_LENGTH:, lanes] = grad[BLOCK_LENGTH : 2 * BLOCK_LENGTH]
            for i in range(CHOSEN_BLOCKS):
                begin = local + i * BLOCK_LENGTH
                part_ref[0, first + i] = dk[begin : begin + BLOCK_LENGTH].astype(jnp.bfloat16)
                part_ref[1, first + i] = dv[begin : begin + BLOCK_LENGTH].astype(jnp.bfloat16)


def attend_call(meta, queries, grads, keys, values, lse, delta, slots):
    number = 2 * KV_HEADS * CHOSEN_BLOCKS
    hbm, vmem = pl.BlockSpec(memory_space=pl.ANY), pl.BlockSpec(memory_space=pltpu.VMEM)
    smem = pl.BlockSpec(memory_space=pltpu.SMEM)
    return pl.pallas_call(
        attend_kernel,
        in_specs=[smem, hbm, hbm, hbm, hbm, vmem, vmem, hbm],
        out_specs=(vmem,) * 4,
        out_shape=(
            jax.ShapeDtypeStruct(queries.shape, jnp.bfloat16),
            jax.ShapeDtypeStruct(keys.shape, jnp.float32),
            jax.ShapeDtypeStruct(keys.shape, jnp.float32),
            jax.ShapeDtypeStruct((2, number, BLOCK_LENGTH, HEAD_WIDTH), jnp.bfloat16),
        ),
        scratch_shapes=[
            pltpu.VMEM(queries.shape, jnp.bfloat16),
            pltpu.VMEM(queries.shape, jnp.bfloat16),
            pltpu.VMEM(keys.shape, jnp.bfloat16),
            pltpu.VMEM(keys.shape, jnp.bfloat16),
            pltpu.VMEM((number, BLOCK_LENGTH, PAIR), jnp.bfloat16),
            pltpu.SemaphoreType.DMA((4,)),
            pltpu.SemaphoreType.DMA((number,)),
        ],
        compiler_params=pltpu.CompilerParams(vmem_limit_bytes=VMEM_BYTES),
        name="attend_blocks",
    )(meta, queries, grads, keys, values, lse, delta, slots)


def reduce_kernel(
    ring, rows_y, weight_scale,
    part_ref, wants_ref, index_ref, dk_ref, dv_ref, xg_ref, kg_ref, vg_ref, wg_ref,
    up, down, ups, downs, arrived, stage, mine, want_smem, index_smem,
    all_k, own, across, shared, from_x, pieces, from_z,
    up_send, up_recv, down_send, down_recv, s_send, s_recv, smem_sem,
    y_send, y_recv, c_send, c_recv, x_send, x_recv, z_send, z_recv,
):
    half = ring // 2
    x, z, c = place(ring)
    high = lax.rem(lax.axis_index("dp"), 2)
    cls = x * 2 + c
    above, below = along(ring, 1), along(ring, -1)
    far_x = [row_mate(ring, j)[0] for j in (1, 3)]
    far_z = [{"ctx": along(ring, d)} for d in range(2, ring - 1)]
    tables = [
        pltpu.make_async_copy(wants_ref, want_smem, smem_sem.at[0]),
        pltpu.make_async_copy(index_ref, index_smem, smem_sem.at[1]),
    ]
    for table in tables:
        table.start()
    greet(neighbours(ring) + [column_mate(t) for t in range(1, rows_y)] + far_x + far_z)
    for table in tables:
        table.wait()

    def slot_copy(part, j, r):
        return push(
            stage.at[part, j - 1, r], arrived.at[part, j - 1, r],
            s_send.at[part, j - 1, r], s_recv.at[part, j - 1, r], member(ring, j)[0],
        )

    def term_of(part, line, owner, rank):
        return part_ref[part, index_smem[line, 0, owner * CAP + rank]]

    def send_slots(part, r):
        owner = lax.rem(z + r, ring)
        for j in (2, 3, 1):
            line = member(ring, j)[1]
            for rank in range(CAP):
                stage[part, j - 1, r, rank] = term_of(part, line, owner, rank)
            slot_copy(part, j, r).start()

    def both(act, part, s):
        act(part, half - s)
        pl.when((s > 0) & (s < half))(lambda: act(part, half + s))

    def up_copy(part, s, b):
        return push(
            ups.at[part, s, b], up.at[part, s, b], up_send.at[part, s, b], up_recv.at[part, s, b], above
        )

    def down_copy(part, s, b):
        return push(
            downs.at[part, s, b], down.at[part, s, b],
            down_send.at[part, s, b], down_recv.at[part, s, b], below,
        )

    def gather_terms(part, r):
        for j in (1, 2, 3):
            slot_copy(part, j, r).wait_recv()
        owner = lax.rem(z + r, ring)
        units = [[want_smem[j, 0, owner * CAP + rank] for rank in range(CAP)] for j in range(4)]
        for b in range(2):
            for h in range(KV_HEADS):
                acc = jnp.zeros((BLOCK_LENGTH, HEAD_WIDTH), jnp.float32)
                for j in range(4):
                    for rank in range(CAP):
                        if j == 0:
                            term = term_of(part, cls, owner, rank)
                        else:
                            term = arrived[part, j - 1, r, rank]
                        hit = units[j][rank] == b * KV_HEADS + h
                        acc = acc + jnp.where(hit, term.astype(jnp.float32), 0.0)
                mine[part, r, b, :, h * HEAD_WIDTH : (h + 1) * HEAD_WIDTH] = acc

    def first(part):
        ups[part, 0, 0] = mine[part, half, 0].astype(jnp.bfloat16)
        up_copy(part, 0, 0).start()
        downs[part, 0, 1] = mine[part, half, 1].astype(jnp.bfloat16)
        down_copy(part, 0, 1).start()

    def hop(part, s):
        up_copy(part, s - 1, 0).wait_recv()
        ups[part, s, 0] = (up[part, s - 1, 0].astype(jnp.float32) + mine[part, half - s, 0]).astype(
            jnp.bfloat16
        )
        up_copy(part, s, 0).start()
        down_copy(part, s - 1, 1).wait_recv()
        downs[part, s, 1] = (
            down[part, s - 1, 1].astype(jnp.float32) + mine[part, half + s, 1]
        ).astype(jnp.bfloat16)
        down_copy(part, s, 1).start()

        @pl.when(s > 1)
        def _():
            up_copy(part, s - 1, 1).wait_recv()

        ups[part, s, 1] = (up[part, s - 1, 1].astype(jnp.float32) + mine[part, half - s, 1]).astype(
            jnp.bfloat16
        )
        up_copy(part, s, 1).start()

        @pl.when(s > 1)
        def _():
            down_copy(part, s - 1, 0).wait_recv()

        downs[part, s, 0] = (
            down[part, s - 1, 0].astype(jnp.float32) + mine[part, half + s, 0]
        ).astype(jnp.bfloat16)
        down_copy(part, s, 0).start()

    def last(part):
        near, outs = ((dk_ref, (kg_ref, own)), (dv_ref, (vg_ref,)))[part]
        for b in range(2):
            up_copy(part, half - 1, b).wait_recv()
            down_copy(part, half - 1, b).wait_recv()
            rows = slice(b * BLOCK_LENGTH, (b + 1) * BLOCK_LENGTH)
            value = near[rows] + mine[part, 0, b]
            value = value + up[part, half - 1, b].astype(jnp.float32)
            value = value + down[part, half - 1, b].astype(jnp.float32)
            for out in outs:
                out[rows] = value.astype(jnp.bfloat16)

    for s in range(AHEAD + 1):
        both(send_slots, 0, s)
        if s >= LAG:
            both(send_slots, 1, s - LAG)
    blank = jnp.zeros((BLOCK_LENGTH, KV_HEADS * HEAD_WIDTH), jnp.bfloat16)
    for part in range(2):
        up[part, 0, 1] = blank
        down[part, 0, 0] = blank

    y = lax.axis_index("dp") // 2

    def y_copy(t):
        return push(own, all_k.at[y], y_send.at[t - 1], y_recv.at[t - 1], column_mate(t))

    def c_copy():
        return push(across.at[:, 1 - c], shared, c_send, c_recv, member(ring, 1)[0])

    def x_copy(j):
        mate, lo, hi = row_mate(ring, j)
        return push(
            across.at[lo, c, hi], from_x.at[j - 1], x_send.at[j - 1], x_recv.at[j - 1], mate
        )

    def z_copy(d):
        return push(
            pieces.at[lax.rem(z + d, ring)], from_z.at[d - 1],
            z_send.at[d - 1], z_recv.at[d - 1], along(ring, d),
        )

    def start_weights():
        for t in range(1, rows_y):
            y_copy(t).start()
        all_k[y] = own[...]

    def multiply():
        for t in range(1, rows_y):
            y_copy(t).wait_recv()
        gathered = all_k[...].reshape(rows_y * TOKENS, KV_HEADS * HEAD_WIDTH)
        for lo in range(2):
            product = jnp.dot(xg_ref[lo], gathered, preferred_element_type=jnp.float32)
            for core in range(2):
                for hi in range(2):
                    begin = (core * 2 + hi) * 4 * ring
                    across[lo, core, hi] = product[begin : begin + 4 * ring]
        c_copy().start()

    def add_core():
        c_copy().wait()
        for lo in range(2):
            for hi in range(2):
                across[lo, c, hi] += shared[lo, hi]
        for j in (1, 2, 3):
            x_copy(j).start()

    def add_row():
        for j in (1, 2, 3):
            x_copy(j).wait()
        value = across[x, c, high] + from_x[0] + from_x[1] + from_x[2]
        for i in range(ring):
            pieces[i] = value[4 * i : 4 * i + 4]
        for d in range(1, ring):
            z_copy(d).start()

    gather_terms(0, half)
    first(0)
    both(gather_terms, 0, 1)
    after = {half: start_weights, half + 2: multiply, half + 3: add_core}
    end = half + LAG
    after = {t: act for t, act in after.items() if t < end}

    def step(t, _):
        pl.when(t < half)(lambda: hop(0, t))
        pl.when(t == LAG)(lambda: first(1))
        pl.when(t > LAG)(lambda: hop(1, t - LAG))
        pl.when(t == half)(lambda: last(0))
        for at, act in after.items():
            pl.when(t == at)(act)
        pl.when(t + AHEAD <= half)(lambda: both(send_slots, 0, t + AHEAD))
        pl.when((t + AHEAD >= LAG) & (t + AHEAD <= end))(lambda: both(send_slots, 1, t + AHEAD - LAG))
        pl.when(t + 1 <= half)(lambda: both(gather_terms, 0, t + 1))
        pl.when((t + 1 >= LAG) & (t + 1 <= end))(lambda: both(gather_terms, 1, t + 1 - LAG))
        return 0

    lax.fori_loop(1, end, step, 0)
    for at, act in ((half, start_weights), (half + 2, multiply), (half + 3, add_core)):
        if at not in after:
            act()
    last(1)
    add_row()
    value = pieces[z]
    for d in range(1, ring):
        z_copy(d).wait_recv()
        value = value + from_z[d - 1]
    wg_ref[...] = value * weight_scale

    for t in range(1, rows_y):
        y_copy(t).wait_send()
    for d in range(1, ring):
        z_copy(d).wait_send()
    for part in range(2):
        up_copy(part, 0, 0).wait_send()
        down_copy(part, 0, 1).wait_send()

        def drain(s, _):
            for b in range(2):
                up_copy(part, s, b).wait_send()
                down_copy(part, s, b).wait_send()
            return 0

        lax.fori_loop(1, half, drain, 0)

        def drain_slots(r, _):
            for j in (1, 2, 3):
                slot_copy(part, j, r).wait_send()
            return 0

        lax.fori_loop(0, ring, drain_slots, 0)


def reduce_call(ring, rows_y, weight_scale, parts, wants, index, dk, dv, xg):
    half = ring // 2
    width = KV_HEADS * HEAD_WIDTH
    ring_buffer = pltpu.VMEM((2, half, 2, BLOCK_LENGTH, width), jnp.bfloat16)
    ring_sem = pltpu.SemaphoreType.DMA((2, half, 2))
    dma = pltpu.SemaphoreType.DMA
    return pl.pallas_call(
        functools.partial(reduce_kernel, ring, rows_y, weight_scale),
        out_shape=(
            jax.ShapeDtypeStruct((TOKENS, width), jnp.bfloat16),
            jax.ShapeDtypeStruct((TOKENS, width), jnp.bfloat16),
            jax.ShapeDtypeStruct((4, width), jnp.float32),
        ),
        in_specs=[pl.BlockSpec(memory_space=pltpu.VMEM)] * 6,
        out_specs=(pl.BlockSpec(memory_space=pltpu.VMEM),) * 3,
        scratch_shapes=[
            ring_buffer, ring_buffer, ring_buffer, ring_buffer,
            pltpu.VMEM((2, 3, ring, CAP, BLOCK_LENGTH, HEAD_WIDTH), jnp.bfloat16),
            pltpu.VMEM((2, 3, ring, CAP, BLOCK_LENGTH, HEAD_WIDTH), jnp.bfloat16),
            pltpu.VMEM((2, ring, 2, BLOCK_LENGTH, width), jnp.float32),
            pltpu.SMEM((4, 8, 128), jnp.int32),
            pltpu.SMEM((4, 8, 128), jnp.int32),
            pltpu.VMEM((rows_y, TOKENS, width), jnp.bfloat16),
            pltpu.VMEM((TOKENS, width), jnp.bfloat16),
            pltpu.VMEM((2, 2, 2, 4 * ring, width), jnp.float32),
            pltpu.VMEM((2, 2, 4 * ring, width), jnp.float32),
            pltpu.VMEM((3, 4 * ring, width), jnp.float32),
            pltpu.VMEM((ring, 4, width), jnp.float32),
            pltpu.VMEM((ring - 1, 4, width), jnp.float32),
            ring_sem, ring_sem, ring_sem, ring_sem,
            dma((2, 3, ring)), dma((2, 3, ring)), dma((2,)),
            dma((rows_y - 1,)), dma((rows_y - 1,)), dma, dma,
            dma((3,)), dma((3,)), dma((ring - 1,)), dma((ring - 1,)),
        ],
        compiler_params=pltpu.CompilerParams(
            collective_id=1, has_side_effects=True, vmem_limit_bytes=VMEM_BYTES
        ),
        name="reduce_blocks",
    )(parts, wants, index, dk, dv, xg)


def body(
    query_states,
    key_activations,
    value_activations,
    out_grad,
    logsumexp,
    row_delta,
    layer_input,
    chosen,
):
    shards = lax.axis_size("ctx")
    replicas = lax.axis_size("dp")
    ring = shards // 4
    rows_y = replicas // 2
    keys, values = key_activations[0], value_activations[0]
    slots, wants, index, meta, xg = gather_call(
        ring, rows_y, chosen[0].reshape(-1), keys, values, layer_input[0]
    )
    query_grad, dk, dv, parts = attend_call(
        meta, query_states[0], out_grad[0], keys, values, logsumexp[0], row_delta[0],
        slots.reshape(4 * ring * CAP, BLOCK_LENGTH, PAIR),
    )
    weight_scale = 1.0 / math.sqrt(TOKENS * shards * replicas)
    key_gradient, value_gradient, key_weight_grad = reduce_call(
        ring, rows_y, weight_scale, parts, wants, index, dk, dv, xg
    )
    return (query_grad[None], key_gradient[None], value_gradient[None], key_weight_grad)


def solution(mesh):
    seq = P("dp", "ctx", None)
    stat = P("dp", None, "ctx")
    return jax.shard_map(
        body,
        mesh=mesh,
        in_specs=(seq, seq, seq, seq, stat, stat, seq, P("dp", "ctx", None, None)),
        out_specs=(seq, seq, seq, P(("ctx", "dp"), None)),
        check_vma=False,
    )
```

```python
import functools
import math

import jax
import jax.numpy as jnp
from jax import lax
from jax.experimental import pallas as pl
from jax.experimental.pallas import tpu as pltpu
from jax.sharding import PartitionSpec as P

HEAD_WIDTH = 128
BLOCK_LENGTH = 64
CHOSEN_BLOCKS = 3
CAP = 2
KV_HEADS = 4
GROUP = 4
TOKENS = 128
UNITS = TOKENS // BLOCK_LENGTH * KV_HEADS
PAIR = 2 * HEAD_WIDTH
LAG = 5
AHEAD = 3
MULTIPLY, ADD_CORE, ADD_ROW = 2, 3, 4
VMEM_BYTES = 58 * 1024 * 1024
GATHER_INPUT, GATHER_SCRATCH = 6, 17
MESH = pl.DeviceIdType.MESH


def place(ring):
    i = lax.axis_index("ctx")
    return i // (2 * ring), lax.rem(i // 2, ring), lax.rem(i, 2)


def member(ring, j):
    x, z, c = place(ring)
    mx = lax.rem(x + j // 2, 2)
    mc = lax.rem(c + j % 2, 2)
    return mx * (2 * ring) + z * 2 + mc, mx * 2 + mc


def along(ring, step):
    x, z, c = place(ring)
    return x * (2 * ring) + lax.rem(z + step + ring, ring) * 2 + c


def column_mate(step):
    i, d = lax.axis_index("ctx"), lax.axis_index("dp")
    rows = lax.axis_size("dp") // 2
    return {"ctx": i, "dp": lax.rem(d // 2 + step, rows) * 2 + lax.rem(d, 2)}


def row_mate(ring, j):
    x, z, c = place(ring)
    d = lax.axis_index("dp")
    lo, hi = lax.rem(x + j // 2, 2), lax.rem(lax.rem(d, 2) + j % 2, 2)
    return {"ctx": lo * (2 * ring) + z * 2 + c, "dp": d // 2 * 2 + hi}, lo, hi


def greet(others):
    barrier = pltpu.get_barrier_semaphore()
    for other in others:
        pl.semaphore_signal(barrier, inc=1, device_id=other, device_id_type=MESH)
    pl.semaphore_wait(barrier, len(others))


def neighbours(ring):
    places = [along(ring, 1), along(ring, -1)] + [member(ring, j)[0] for j in (1, 2, 3)]
    return [{"ctx": other} for other in places]


def push(src, dst, send, recv, other):
    other = other if isinstance(other, dict) else {"ctx": other}
    return pltpu.make_async_remote_copy(
        src_ref=src, dst_ref=dst, send_sem=send, recv_sem=recv,
        device_id=other, device_id_type=MESH,
    )


def gather_stage(
    ring, rows_y, chosen_ref, k_ref, v_ref, x_ref, slots, wants, index, meta, want_smem, xg, near,
    up, down, stage, work, want, xt, xin,
    up_send, up_recv, down_send, down_recv, w_send, w_recv, s_send, s_recv, x_send, x_recv,
    smem_sem, in_sem,
):
    half = ring // 2
    x, z, c = place(ring)
    cls = x * 2 + c
    above, below = along(ring, 1), along(ring, -1)

    def up_copy(s, part, src=None):
        src = up.at[s - 1, part] if src is None else src
        return push(src, up.at[s, part], up_send.at[s, part], up_recv.at[s, part], above)

    def down_copy(s, part, src=None):
        src = down.at[s - 1, part] if src is None else src
        return push(src, down.at[s, part], down_send.at[s, part], down_recv.at[s, part], below)

    for part, ref in ((0, k_ref), (1, v_ref)):
        up_copy(0, part, ref).start()
        down_copy(0, part, ref).start()

    shape = (4, 8, 128)
    spot = lax.broadcasted_iota(jnp.int32, shape, 0) * 128 + lax.broadcasted_iota(jnp.int32, shape, 2)
    wanted = jnp.full(shape, -1, jnp.int32)
    spots = jnp.zeros(shape, jnp.int32)
    owners = []
    for i in range(2 * KV_HEADS * CHOSEN_BLOCKS):
        choice = chosen_ref[i]
        active = choice >= 0
        block = jnp.maximum(choice, 0)
        owner = block // 2
        marked = jnp.where(active, owner, -1)
        rank = jnp.int32(0)
        for other in owners:
            rank = rank + jnp.where(other == marked, 1, 0)
        owners.append(marked)
        line = (owner // (2 * ring)) * 2 + lax.rem(owner, 2)
        entry = lax.rem(owner // 2, ring) * CAP + rank
        hit = spot == jnp.where(active, line * 128 + entry, -1)
        wanted = jnp.where(hit, lax.rem(block, 2) * KV_HEADS + i // CHOSEN_BLOCKS % KV_HEADS, wanted)
        spots = jnp.where(hit, i, spots)
        meta[i] = jnp.where(active, line * ring * CAP + entry, 0)
        meta[64 + i] = jnp.where(active, 1, 0)
    want[...] = wanted
    index[...] = spots

    def want_copy(j):
        other, other_cls = member(ring, j)
        return push(want.at[other_cls], wants.at[j], w_send.at[j - 1], w_recv.at[j - 1], other)

    for j in (1, 2, 3):
        want_copy(j).start()
    wants[0] = want[cls]

    y = lax.axis_index("dp") // 2
    lines = 16 * ring
    half_width = lines * rows_y

    def x_copy(t):
        return push(
            xt.at[t], xg.at[:, :, pl.ds(pl.multiple_of(y * TOKENS, TOKENS), TOKENS)],
            x_send.at[t], x_recv.at[t], column_mate(t),
        )

    def keep_copy():
        return pltpu.make_async_copy(
            xt.at[0], xg.at[:, :, pl.ds(pl.multiple_of(y * TOKENS, TOKENS), TOKENS)], x_send.at[0]
        )

    def deal(t):
        to = lax.rem(y + t, rows_y)
        line = lax.broadcasted_iota(jnp.int32, (lines, half_width), 0)
        column = lax.broadcasted_iota(jnp.int32, (lines, half_width), 1)
        core, high, rest = line // (8 * ring), line // (4 * ring) % 2, line % (4 * ring)
        source = rest // 4 * (16 * rows_y) + core * (8 * rows_y) + to * 8 + high * 4 + rest % 4
        pick = jnp.where(column == source, 1.0, 0.0).astype(jnp.bfloat16)
        for lo in range(2):
            part = xin[:, lo * half_width : (lo + 1) * half_width]
            xt[t, lo] = lax.dot_general(
                pick, part, (((1,), (1,)), ((), ())), preferred_element_type=jnp.float32
            ).astype(jnp.bfloat16)

    loads = [
        pltpu.make_async_copy(src, dst, in_sem.at[i])
        for i, (src, dst) in enumerate(((k_ref, near.at[0]), (v_ref, near.at[1]), (x_ref, xin)))
    ]
    for load in loads:
        load.wait()
    for j in (1, 2, 3):
        want_copy(j).wait()
    table = pltpu.make_async_copy(wants, want_smem, smem_sem.at[0])
    table.start()
    table.wait()

    def slot_copy(j, r):
        owner = lax.rem(z + r, ring)
        return push(
            stage.at[r, j - 1], slots.at[pl.ds((cls * ring + owner) * CAP, CAP)],
            s_send.at[j - 1, r], s_recv.at[j - 1, r], member(ring, j)[0],
        )

    def extract(r, keys, values):
        owner = lax.rem(z + r, ring)
        for b in range(2):
            for h in range(KV_HEADS):
                rows, lanes = pl.ds(b * BLOCK_LENGTH, BLOCK_LENGTH), pl.ds(h * HEAD_WIDTH, HEAD_WIDTH)
                work[b * KV_HEADS + h, :, :HEAD_WIDTH] = keys[rows, lanes]
                work[b * KV_HEADS + h, :, HEAD_WIDTH:] = values[rows, lanes]
        for j in (2, 3, 1, 0):
            for rank in range(CAP):
                unit = jnp.maximum(want_smem[j, 0, owner * CAP + rank], 0)
                if j:
                    stage[r, j - 1, rank] = work[unit]
                else:
                    slots[(cls * ring + owner) * CAP + rank] = work[unit]
            if j:
                slot_copy(j, r).start()

    extract(0, near.at[0], near.at[1])
    for t in range(rows_y):
        deal(t)
        if t == 0:
            keep_copy().start()
        else:
            x_copy(t).start()

    def step(s, _):
        for part in range(2):
            up_copy(s, part, k_ref).wait_recv()
            up_copy(s + 1, part).start()
            down_copy(s, part, k_ref).wait_recv()
            down_copy(s + 1, part).start()
        extract(ring - 1 - s, up.at[s, 0], up.at[s, 1])
        extract(1 + s, down.at[s, 0], down.at[s, 1])
        return 0

    lax.fori_loop(0, half - 2, step, 0)
    s = half - 2
    for part in range(2):
        up_copy(s, part, k_ref).wait_recv()
        if part == 0:
            up_copy(s + 1, part).start()
        down_copy(s, part, k_ref).wait_recv()
        if part == 1:
            down_copy(s + 1, part).start()
    extract(ring - 1 - s, up.at[s, 0], up.at[s, 1])
    extract(1 + s, down.at[s, 0], down.at[s, 1])
    up_copy(half - 1, 0, k_ref).wait_recv()
    down_copy(half - 1, 1, k_ref).wait_recv()
    extract(half, up.at[half - 1, 0], down.at[half - 1, 1])

    def drain(s, _):
        for part in range(2):
            up_copy(s, part, k_ref).wait_send()
            down_copy(s, part, k_ref).wait_send()
        return 0

    lax.fori_loop(0, half - 1, drain, 0)
    up_copy(half - 1, 0, k_ref).wait_send()
    down_copy(half - 1, 1, k_ref).wait_send()

    def drain_slots(r, _):
        for j in (1, 2, 3):
            slot_copy(j, r).wait()
        return 0

    lax.fori_loop(0, ring, drain_slots, 0)
    keep_copy().wait()
    for t in range(1, rows_y):
        x_copy(t).wait()


def attend_stage(meta, lse_ref, delta_ref, slots, dq_ref, dk_ref, dv_ref, part_ref, q, g, near):
    scale = HEAD_WIDTH ** (-0.5)
    k, v = near.at[0], near.at[1]
    lse, delta = lse_ref[...].astype(jnp.float32), delta_ref[...].astype(jnp.float32)
    rows_n = GROUP * BLOCK_LENGTH
    nt = (((1,), (1,)), ((), ()))
    tn = (((0,), (0,)), ((), ()))

    def line(stat, h, b):
        return jnp.concatenate(
            [
                stat[h * GROUP + i : h * GROUP + i + 1, b * BLOCK_LENGTH : (b + 1) * BLOCK_LENGTH]
                for i in range(GROUP)
            ],
            axis=1,
        )

    def stack(ref, h, b):
        rows = slice(b * BLOCK_LENGTH, (b + 1) * BLOCK_LENGTH)
        heads = [h * GROUP + i for i in range(GROUP)]
        return jnp.concatenate(
            [ref[rows, i * HEAD_WIDTH : (i + 1) * HEAD_WIDTH] for i in heads], axis=0
        )

    for h in range(KV_HEADS):
        lanes = slice(h * HEAD_WIDTH, (h + 1) * HEAD_WIDTH)
        for b in range(2):
            first = (b * KV_HEADS + h) * CHOSEN_BLOCKS
            local = (b + 1) * BLOCK_LENGTH
            keys_n = local + CHOSEN_BLOCKS * BLOCK_LENGTH
            queries, grads = stack(q, h, b), stack(g, h, b)
            chosen = [slots[meta[first + i]] for i in range(CHOSEN_BLOCKS)]
            keys = jnp.concatenate([k[:local, lanes]] + [f[:, :HEAD_WIDTH] for f in chosen], axis=0)
            values = jnp.concatenate([v[:local, lanes]] + [f[:, HEAD_WIDTH:] for f in chosen], axis=0)
            row = lax.broadcasted_iota(jnp.int32, (keys_n, rows_n), 1) % BLOCK_LENGTH
            key = lax.broadcasted_iota(jnp.int32, (keys_n, rows_n), 0)
            mask = (key < local) & (key <= row + b * BLOCK_LENGTH)
            for i in range(CHOSEN_BLOCKS):
                begin = local + i * BLOCK_LENGTH
                limit = jnp.where(meta[64 + first + i] > 0, begin + BLOCK_LENGTH, begin)
                mask = mask | ((key >= begin) & (key < limit))
            scores = lax.dot_general(keys, queries, nt, preferred_element_type=jnp.float32) * scale
            prob = jnp.where(mask, jnp.exp(scores - line(lse, h, b)), 0.0)
            dprob = lax.dot_general(values, grads, nt, preferred_element_type=jnp.float32)
            dscore = (prob * (dprob - line(delta, h, b))).astype(jnp.bfloat16)
            prob_low = prob.astype(jnp.bfloat16)
            dq = lax.dot_general(dscore, keys, tn, preferred_element_type=jnp.float32) * scale
            dq = dq.astype(jnp.bfloat16)
            for i in range(GROUP):
                head = h * GROUP + i
                dq_ref[
                    b * BLOCK_LENGTH : (b + 1) * BLOCK_LENGTH,
                    head * HEAD_WIDTH : (head + 1) * HEAD_WIDTH,
                ] = dq[i * BLOCK_LENGTH : (i + 1) * BLOCK_LENGTH]
            dk = jnp.dot(dscore, queries, preferred_element_type=jnp.float32) * scale
            dv = jnp.dot(prob_low, grads, preferred_element_type=jnp.float32)
            for out, grad in ((dk_ref, dk), (dv_ref, dv)):
                if b == 0:
                    out[:BLOCK_LENGTH, lanes] = grad[:BLOCK_LENGTH]
                else:
                    out[:BLOCK_LENGTH, lanes] += grad[:BLOCK_LENGTH]
                    out[BLOCK_LENGTH:, lanes] = grad[BLOCK_LENGTH : 2 * BLOCK_LENGTH]
            for i in range(CHOSEN_BLOCKS):
                begin = local + i * BLOCK_LENGTH
                part_ref[0, first + i] = dk[begin : begin + BLOCK_LENGTH].astype(jnp.bfloat16)
                part_ref[1, first + i] = dv[begin : begin + BLOCK_LENGTH].astype(jnp.bfloat16)


def reduce_stage(
    ring, rows_y, weight_scale, part_ref, want_smem, index_smem, dk_ref, dv_ref, xg_ref,
    kg_ref, vg_ref, wg_ref,
    up, down, ups, downs, arrived, stage, mine,
    all_k, own, across, shared, from_x, pieces, from_z,
    up_send, up_recv, down_send, down_recv, s_send, s_recv,
    y_send, y_recv, c_send, c_recv, x_send, x_recv, z_send, z_recv,
):
    half = ring // 2
    x, z, c = place(ring)
    high = lax.rem(lax.axis_index("dp"), 2)
    cls = x * 2 + c
    above, below = along(ring, 1), along(ring, -1)

    def slot_copy(part, j, r):
        return push(
            stage.at[part, j - 1, r], arrived.at[part, j - 1, r],
            s_send.at[part, j - 1, r], s_recv.at[part, j - 1, r], member(ring, j)[0],
        )

    def term_of(part, line, owner, rank):
        return part_ref[part, index_smem[line, 0, owner * CAP + rank]]

    def send_slots(part, r):
        owner = lax.rem(z + r, ring)
        for j in (2, 3, 1):
            line = member(ring, j)[1]
            for rank in range(CAP):
                stage[part, j - 1, r, rank] = term_of(part, line, owner, rank)
            slot_copy(part, j, r).start()

    def both(act, part, s):
        act(part, half - s)
        pl.when((s > 0) & (s < half))(lambda: act(part, half + s))

    def up_copy(part, s, b):
        return push(
            ups.at[part, s, b], up.at[part, s, b], up_send.at[part, s, b], up_recv.at[part, s, b], above
        )

    def down_copy(part, s, b):
        return push(
            downs.at[part, s, b], down.at[part, s, b],
            down_send.at[part, s, b], down_recv.at[part, s, b], below,
        )

    def gather_terms(part, r):
        for j in (1, 2, 3):
            slot_copy(part, j, r).wait_recv()
        owner = lax.rem(z + r, ring)
        units = [[want_smem[j, 0, owner * CAP + rank] for rank in range(CAP)] for j in range(4)]
        for b in range(2):
            for h in range(KV_HEADS):
                acc = jnp.zeros((BLOCK_LENGTH, HEAD_WIDTH), jnp.float32)
                for j in range(4):
                    for rank in range(CAP):
                        if j == 0:
                            term = term_of(part, cls, owner, rank)
                        else:
                            term = arrived[part, j - 1, r, rank]
                        hit = units[j][rank] == b * KV_HEADS + h
                        acc = acc + jnp.where(hit, term.astype(jnp.float32), 0.0)
                mine[part, r, b, :, h * HEAD_WIDTH : (h + 1) * HEAD_WIDTH] = acc

    def first(part):
        ups[part, 0, 0] = mine[part, half, 0].astype(jnp.bfloat16)
        up_copy(part, 0, 0).start()
        downs[part, 0, 1] = mine[part, half, 1].astype(jnp.bfloat16)
        down_copy(part, 0, 1).start()

    def hop(part, s):
        up_copy(part, s - 1, 0).wait_recv()
        ups[part, s, 0] = (up[part, s - 1, 0].astype(jnp.float32) + mine[part, half - s, 0]).astype(
            jnp.bfloat16
        )
        up_copy(part, s, 0).start()
        down_copy(part, s - 1, 1).wait_recv()
        downs[part, s, 1] = (
            down[part, s - 1, 1].astype(jnp.float32) + mine[part, half + s, 1]
        ).astype(jnp.bfloat16)
        down_copy(part, s, 1).start()

        @pl.when(s > 1)
        def _():
            up_copy(part, s - 1, 1).wait_recv()

        ups[part, s, 1] = (up[part, s - 1, 1].astype(jnp.float32) + mine[part, half - s, 1]).astype(
            jnp.bfloat16
        )
        up_copy(part, s, 1).start()

        @pl.when(s > 1)
        def _():
            down_copy(part, s - 1, 0).wait_recv()

        downs[part, s, 0] = (
            down[part, s - 1, 0].astype(jnp.float32) + mine[part, half + s, 0]
        ).astype(jnp.bfloat16)
        down_copy(part, s, 0).start()

    def last(part):
        near, outs = ((dk_ref, (kg_ref, own)), (dv_ref, (vg_ref,)))[part]
        for b in range(2):
            up_copy(part, half - 1, b).wait_recv()
            down_copy(part, half - 1, b).wait_recv()
            rows = slice(b * BLOCK_LENGTH, (b + 1) * BLOCK_LENGTH)
            value = near[rows] + mine[part, 0, b]
            value = value + up[part, half - 1, b].astype(jnp.float32)
            value = value + down[part, half - 1, b].astype(jnp.float32)
            for out in outs:
                out[rows] = value.astype(jnp.bfloat16)

    for s in range(AHEAD + 1):
        both(send_slots, 0, s)
        if s >= LAG:
            both(send_slots, 1, s - LAG)
    blank = jnp.zeros((BLOCK_LENGTH, KV_HEADS * HEAD_WIDTH), jnp.bfloat16)
    for part in range(2):
        up[part, 0, 1] = blank
        down[part, 0, 0] = blank

    y = lax.axis_index("dp") // 2

    def y_copy(t):
        return push(own, all_k.at[y], y_send.at[t - 1], y_recv.at[t - 1], column_mate(t))

    def c_copy():
        return push(across.at[:, 1 - c], shared, c_send, c_recv, member(ring, 1)[0])

    def x_copy(j):
        mate, lo, hi = row_mate(ring, j)
        return push(
            across.at[lo, c, hi], from_x.at[j - 1], x_send.at[j - 1], x_recv.at[j - 1], mate
        )

    def z_copy(d):
        return push(
            pieces.at[lax.rem(z + d, ring)], from_z.at[d - 1],
            z_send.at[d - 1], z_recv.at[d - 1], along(ring, d),
        )

    def start_weights():
        for t in range(1, rows_y):
            y_copy(t).start()
        all_k[y] = own[...]

    def multiply():
        for t in range(1, rows_y):
            y_copy(t).wait_recv()
        gathered = all_k[...].reshape(rows_y * TOKENS, KV_HEADS * HEAD_WIDTH)
        for lo in range(2):
            product = jnp.dot(xg_ref[lo], gathered, preferred_element_type=jnp.float32)
            for core in range(2):
                for hi in range(2):
                    begin = (core * 2 + hi) * 4 * ring
                    across[lo, core, hi] = product[begin : begin + 4 * ring]
        c_copy().start()

    def add_core():
        c_copy().wait()
        for lo in range(2):
            for hi in range(2):
                across[lo, c, hi] += shared[lo, hi]
        for j in (1, 2, 3):
            x_copy(j).start()

    def add_row():
        for j in (1, 2, 3):
            x_copy(j).wait()
        value = across[x, c, high] + from_x[0] + from_x[1] + from_x[2]
        for i in range(ring):
            pieces[i] = value[4 * i : 4 * i + 4]
        for d in range(1, ring):
            z_copy(d).start()

    gather_terms(0, half)
    first(0)
    both(gather_terms, 0, 1)
    jobs = (
        (half, start_weights), (half + MULTIPLY, multiply), (half + ADD_CORE, add_core),
        (half + ADD_ROW, add_row),
    )
    end = half + LAG

    def step(t, _):
        pl.when(t < half)(lambda: hop(0, t))
        pl.when(t == LAG)(lambda: first(1))
        pl.when(t > LAG)(lambda: hop(1, t - LAG))
        pl.when(t == half)(lambda: last(0))
        for at, act in jobs:
            pl.when(t == at)(act)
        pl.when(t + AHEAD <= half)(lambda: both(send_slots, 0, t + AHEAD))
        pl.when((t + AHEAD >= LAG) & (t + AHEAD <= end))(lambda: both(send_slots, 1, t + AHEAD - LAG))
        pl.when(t + 1 <= half)(lambda: both(gather_terms, 0, t + 1))
        pl.when((t + 1 >= LAG) & (t + 1 <= end))(lambda: both(gather_terms, 1, t + 1 - LAG))
        return 0

    lax.fori_loop(1, end, step, 0)
    last(1)
    for at, act in jobs:
        if at >= end:
            act()
    value = pieces[z]
    for d in range(1, ring):
        z_copy(d).wait_recv()
        value = value + from_z[d - 1]
    wg_ref[...] = value * weight_scale

    for t in range(1, rows_y):
        y_copy(t).wait_send()
    for d in range(1, ring):
        z_copy(d).wait_send()
    for part in range(2):
        up_copy(part, 0, 0).wait_send()
        down_copy(part, 0, 1).wait_send()

        def drain(s, _):
            for b in range(2):
                up_copy(part, s, b).wait_send()
                down_copy(part, s, b).wait_send()
            return 0

        lax.fori_loop(1, half, drain, 0)

        def drain_slots(r, _):
            for j in (1, 2, 3):
                slot_copy(part, j, r).wait_send()
            return 0

        lax.fori_loop(0, ring, drain_slots, 0)


def fused_kernel(
    ring, rows_y, weight_scale, chosen_ref, k_ref, v_ref, x_ref, q_ref, g_ref, lse_ref, delta_ref,
    dq_ref, kg_ref, vg_ref, wg_ref,
    slots, wants, index, meta, want_smem, index_smem, xg, near, q, g, dk, dv, parts,
    in_sem, smem_sem, *scratch,
):
    loads = [
        pltpu.make_async_copy(src, dst, in_sem.at[i])
        for i, (src, dst) in enumerate(
            (
                (k_ref, near.at[0]), (v_ref, near.at[1]), (x_ref, scratch[GATHER_INPUT]),
                (q_ref, q), (g_ref, g),
            )
        )
    ]
    for load in loads:
        load.start()
    far_x = [row_mate(ring, j)[0] for j in (1, 3)]
    far_z = [{"ctx": along(ring, d)} for d in range(2, ring - 1)]
    greet(neighbours(ring) + [column_mate(t) for t in range(1, rows_y)] + far_x + far_z)
    gather_stage(
        ring, rows_y, chosen_ref, k_ref, v_ref, x_ref, slots, wants, index, meta, want_smem, xg, near,
        *scratch[:GATHER_SCRATCH], smem_sem, in_sem,
    )
    table = pltpu.make_async_copy(index, index_smem, smem_sem.at[1])
    table.start()
    for load in loads[3:]:
        load.wait()
    attend_stage(meta, lse_ref, delta_ref, slots, dq_ref, dk, dv, parts, q, g, near)
    table.wait()
    reduce_stage(
        ring, rows_y, weight_scale, parts, want_smem, index_smem, dk, dv, xg,
        kg_ref, vg_ref, wg_ref, *scratch[GATHER_SCRATCH:],
    )


def fused_call(ring, rows_y, weight_scale, chosen, keys, values, inputs, queries, grads, lse, delta):
    half = ring // 2
    lines = 16 * ring
    width = KV_HEADS * HEAD_WIDTH
    number = 2 * KV_HEADS * CHOSEN_BLOCKS
    hbm, vmem = pl.BlockSpec(memory_space=pl.ANY), pl.BlockSpec(memory_space=pltpu.VMEM)
    smem = pl.BlockSpec(memory_space=pltpu.SMEM)
    dma = pltpu.SemaphoreType.DMA
    low, full = jnp.bfloat16, jnp.float32
    table = (4, 8, 128)
    shared = [
        pltpu.VMEM((4 * ring * CAP, BLOCK_LENGTH, PAIR), low),
        pltpu.VMEM(table, jnp.int32),
        pltpu.VMEM(table, jnp.int32),
        pltpu.SMEM((128,), jnp.int32),
        pltpu.SMEM(table, jnp.int32),
        pltpu.SMEM(table, jnp.int32),
        pltpu.VMEM((2, lines, rows_y * TOKENS), low),
        pltpu.VMEM((2,) + keys.shape, low),
        pltpu.VMEM(queries.shape, low),
        pltpu.VMEM(queries.shape, low),
        pltpu.VMEM(keys.shape, full),
        pltpu.VMEM(keys.shape, full),
        pltpu.VMEM((2, number, BLOCK_LENGTH, HEAD_WIDTH), low),
        dma((5,)), dma((2,)),
    ]
    gather_ring, gather_sem = pltpu.VMEM((half, 2, TOKENS, width), low), dma((half, 2))
    gather = [
        gather_ring, gather_ring,
        pltpu.VMEM((ring, 3, CAP, BLOCK_LENGTH, PAIR), low),
        pltpu.VMEM((UNITS, BLOCK_LENGTH, PAIR), low),
        pltpu.VMEM(table, jnp.int32),
        pltpu.VMEM((rows_y, 2, lines, TOKENS), low),
        pltpu.VMEM(inputs.shape, low),
        gather_sem, gather_sem, gather_sem, gather_sem,
        dma((3,)), dma((3,)), dma((3, ring)), dma((3, ring)), dma((rows_y,)), dma((rows_y,)),
    ]
    reduce_ring, reduce_sem = pltpu.VMEM((2, half, 2, BLOCK_LENGTH, width), low), dma((2, half, 2))
    reduce = [
        reduce_ring, reduce_ring, reduce_ring, reduce_ring,
        pltpu.VMEM((2, 3, ring, CAP, BLOCK_LENGTH, HEAD_WIDTH), low),
        pltpu.VMEM((2, 3, ring, CAP, BLOCK_LENGTH, HEAD_WIDTH), low),
        pltpu.VMEM((2, ring, 2, BLOCK_LENGTH, width), full),
        pltpu.VMEM((rows_y, TOKENS, width), low),
        pltpu.VMEM((TOKENS, width), low),
        pltpu.VMEM((2, 2, 2, 4 * ring, width), full),
        pltpu.VMEM((2, 2, 4 * ring, width), full),
        pltpu.VMEM((3, 4 * ring, width), full),
        pltpu.VMEM((ring, 4, width), full),
        pltpu.VMEM((ring - 1, 4, width), full),
        reduce_sem, reduce_sem, reduce_sem, reduce_sem,
        dma((2, 3, ring)), dma((2, 3, ring)),
        dma((rows_y - 1,)), dma((rows_y - 1,)), dma, dma,
        dma((3,)), dma((3,)), dma((ring - 1,)), dma((ring - 1,)),
    ]
    assert len(gather) == GATHER_SCRATCH
    return pl.pallas_call(
        functools.partial(fused_kernel, ring, rows_y, weight_scale),
        out_shape=(
            jax.ShapeDtypeStruct(queries.shape, low),
            jax.ShapeDtypeStruct((TOKENS, width), low),
            jax.ShapeDtypeStruct((TOKENS, width), low),
            jax.ShapeDtypeStruct((4, width), full),
        ),
        in_specs=[smem, hbm, hbm, hbm, hbm, hbm, vmem, vmem],
        out_specs=(vmem,) * 4,
        scratch_shapes=shared + gather + reduce,
        compiler_params=pltpu.CompilerParams(
            collective_id=0, has_side_effects=True, vmem_limit_bytes=VMEM_BYTES
        ),
        name="fused_blocks",
    )(chosen, keys, values, inputs, queries, grads, lse, delta)


def hand_over_kernel(*refs):
    n = len(refs) // 2
    for i in range(n):
        refs[n + i][...] = refs[i][...]


def hand_over(*arrays):
    vmem = pl.BlockSpec(memory_space=pltpu.VMEM)
    return pl.pallas_call(
        hand_over_kernel,
        in_specs=[vmem] * len(arrays),
        out_specs=(vmem,) * len(arrays),
        out_shape=tuple(jax.ShapeDtypeStruct(a.shape, a.dtype) for a in arrays),
        name="hand_over",
    )(*arrays)


def body(
    query_states,
    key_activations,
    value_activations,
    out_grad,
    logsumexp,
    row_delta,
    layer_input,
    chosen,
):
    shards = lax.axis_size("ctx")
    replicas = lax.axis_size("dp")
    ring = shards // 4
    rows_y = replicas // 2
    keys, values = key_activations[0], value_activations[0]
    weight_scale = 1.0 / math.sqrt(TOKENS * shards * replicas)
    outputs = fused_call(
        ring, rows_y, weight_scale, chosen[0].reshape(-1), keys, values, layer_input[0],
        query_states[0], out_grad[0], logsumexp[0], row_delta[0],
    )
    query_grad, key_gradient, value_gradient, key_weight_grad = hand_over(*outputs)
    return (query_grad[None], key_gradient[None], value_gradient[None], key_weight_grad)


def solution(mesh):
    seq = P("dp", "ctx", None)
    stat = P("dp", None, "ctx")
    return jax.shard_map(
        body,
        mesh=mesh,
        in_specs=(seq, seq, seq, seq, stat, stat, seq, P("dp", "ctx", None, None)),
        out_specs=(seq, seq, seq, P(("ctx", "dp"), None)),
        check_vma=False,
    )
```

```python
import functools
import math

import jax
import jax.numpy as jnp
from jax import lax
from jax.experimental import pallas as pl
from jax.experimental.pallas import tpu as pltpu
from jax.sharding import PartitionSpec as P

HEAD_WIDTH = 128
BLOCK_LENGTH = 64
CHOSEN_BLOCKS = 3
CAP = 2
KV_HEADS = 4
GROUP = 4
TOKENS = 128
UNITS = TOKENS // BLOCK_LENGTH * KV_HEADS
LAG = 5
AHEAD = 4
AHEAD_V = 4
MULTIPLY, ADD_CORE, ADD_ROW = 2, 3, 4
VMEM_BYTES = 58 * 1024 * 1024
GATHER_INPUT, GATHER_SCRATCH = 6, 17
MESH = pl.DeviceIdType.MESH


def place(ring):
    i = lax.axis_index("ctx")
    return i // (2 * ring), lax.rem(i // 2, ring), lax.rem(i, 2)


def member(ring, j):
    x, z, c = place(ring)
    mx = lax.rem(x + j // 2, 2)
    mc = lax.rem(c + j % 2, 2)
    return mx * (2 * ring) + z * 2 + mc, mx * 2 + mc


def along(ring, step):
    x, z, c = place(ring)
    return x * (2 * ring) + lax.rem(z + step + ring, ring) * 2 + c


def column_mate(step):
    i, d = lax.axis_index("ctx"), lax.axis_index("dp")
    rows = lax.axis_size("dp") // 2
    return {"ctx": i, "dp": lax.rem(d // 2 + step, rows) * 2 + lax.rem(d, 2)}


def row_mate(ring, j):
    x, z, c = place(ring)
    d = lax.axis_index("dp")
    lo, hi = lax.rem(x + j // 2, 2), lax.rem(lax.rem(d, 2) + j % 2, 2)
    return {"ctx": lo * (2 * ring) + z * 2 + c, "dp": d // 2 * 2 + hi}, lo, hi


def greet(others):
    barrier = pltpu.get_barrier_semaphore()
    for other in others:
        pl.semaphore_signal(barrier, inc=1, device_id=other, device_id_type=MESH)
    pl.semaphore_wait(barrier, len(others))


def neighbours(ring):
    places = [along(ring, 1), along(ring, -1)] + [member(ring, j)[0] for j in (1, 2, 3)]
    return [{"ctx": other} for other in places]


def push(src, dst, send, recv, other):
    other = other if isinstance(other, dict) else {"ctx": other}
    return pltpu.make_async_remote_copy(
        src_ref=src, dst_ref=dst, send_sem=send, recv_sem=recv,
        device_id=other, device_id_type=MESH,
    )


def gather_stage(
    ring, rows_y, chosen_ref, k_ref, v_ref, x_ref, q_ref, g_ref, q, g, slots, wants, index, meta, want_smem, xg, near,
    up, down, stage, work, want, xt, xin,
    up_send, up_recv, down_send, down_recv, w_send, w_recv, s_send, s_recv, x_send, x_recv,
    smem_sem, in_sem, local_part,
):
    half = ring // 2
    x, z, c = place(ring)
    cls = x * 2 + c
    above, below = along(ring, 1), along(ring, -1)

    def up_copy(s, part, b, src=None):
        at = (s, part, b)
        src = up.at[s - 1, part, b] if src is None else src
        return push(src, up.at[at], up_send.at[at], up_recv.at[at], above)

    def down_copy(s, part, b, src=None):
        at = (s, part, b)
        src = down.at[s - 1, part, b] if src is None else src
        return push(src, down.at[at], down_send.at[at], down_recv.at[at], below)

    some = k_ref.at[:BLOCK_LENGTH]
    for part, ref in ((0, k_ref), (1, v_ref)):
        for b in range(2):
            rows = ref.at[b * BLOCK_LENGTH : (b + 1) * BLOCK_LENGTH]
            up_copy(0, part, b, rows).start()
            down_copy(0, part, b, rows).start()

    shape = (4, 8, 128)
    spot = lax.broadcasted_iota(jnp.int32, shape, 0) * 128 + lax.broadcasted_iota(jnp.int32, shape, 2)
    wanted = jnp.full(shape, -1, jnp.int32)
    spots = jnp.zeros(shape, jnp.int32)
    owners = []
    for i in range(2 * KV_HEADS * CHOSEN_BLOCKS):
        choice = chosen_ref[i // (KV_HEADS * CHOSEN_BLOCKS), i // CHOSEN_BLOCKS % KV_HEADS, i % CHOSEN_BLOCKS]
        active = choice >= 0
        block = jnp.maximum(choice, 0)
        owner = block // 2
        marked = jnp.where(active, owner, -1)
        rank = jnp.int32(0)
        for other in owners:
            rank = rank + jnp.where(other == marked, 1, 0)
        owners.append(marked)
        line = (owner // (2 * ring)) * 2 + lax.rem(owner, 2)
        entry = lax.rem(owner // 2, ring) * CAP + rank
        hit = spot == jnp.where(active, line * 128 + entry, -1)
        wanted = jnp.where(hit, lax.rem(block, 2) * KV_HEADS + i // CHOSEN_BLOCKS % KV_HEADS, wanted)
        spots = jnp.where(hit, i, spots)
        meta[i] = jnp.where(active, line * ring * CAP + entry, 0)
        meta[64 + i] = jnp.where(active, 1, 0)
    want[...] = wanted
    index[...] = spots

    def want_copy(j):
        other, other_cls = member(ring, j)
        return push(want.at[other_cls], wants.at[j], w_send.at[j - 1], w_recv.at[j - 1], other)

    for j in (1, 2, 3):
        want_copy(j).start()
    wants[0] = want[cls]

    y = lax.axis_index("dp") // 2
    lines = 16 * ring
    half_width = lines * rows_y

    def x_copy(t):
        return push(
            xt.at[t], xg.at[:, :, pl.ds(pl.multiple_of(y * TOKENS, TOKENS), TOKENS)],
            x_send.at[t], x_recv.at[t], column_mate(t),
        )

    def keep_copy():
        return pltpu.make_async_copy(
            xt.at[0], xg.at[:, :, pl.ds(pl.multiple_of(y * TOKENS, TOKENS), TOKENS)], x_send.at[0]
        )

    def deal(t):
        to = lax.rem(y + t, rows_y)
        line = lax.broadcasted_iota(jnp.int32, (lines, half_width), 0)
        column = lax.broadcasted_iota(jnp.int32, (lines, half_width), 1)
        core, high, rest = line // (8 * ring), line // (4 * ring) % 2, line % (4 * ring)
        source = rest // 4 * (16 * rows_y) + core * (8 * rows_y) + to * 8 + high * 4 + rest % 4
        pick = jnp.where(column == source, 1.0, 0.0).astype(jnp.bfloat16)
        for lo in range(2):
            part = xin[:, lo * half_width : (lo + 1) * half_width]
            xt[t, lo] = lax.dot_general(
                pick, part, (((1,), (1,)), ((), ())), preferred_element_type=jnp.float32
            ).astype(jnp.bfloat16)

    loads = [
        pltpu.make_async_copy(src, dst, in_sem.at[i])
        for i, (src, dst) in enumerate(
            (
                (k_ref, near.at[0]), (v_ref, near.at[1]), (x_ref, xin), (q_ref, q), (g_ref, g),
            )
        )
    ]
    for load in loads:
        load.wait()
    for j in (1, 2, 3):
        want_copy(j).wait()
    table = pltpu.make_async_copy(wants, want_smem, smem_sem.at[0])
    table.start()
    table.wait()

    def slot_copy(part, j, r):
        owner = lax.rem(z + r, ring)
        return push(
            stage.at[part, r, j - 1], slots.at[part, pl.ds((cls * ring + owner) * CAP, CAP)],
            s_send.at[part, j - 1, r], s_recv.at[part, j - 1, r], member(ring, j)[0],
        )

    def extract(part, r, chunk):
        owner = lax.rem(z + r, ring)
        for b in range(2):
            for h in range(KV_HEADS):
                work[b * KV_HEADS + h] = chunk(b)[:, h * HEAD_WIDTH : (h + 1) * HEAD_WIDTH]
        for j in (2, 3, 1, 0):
            for rank in range(CAP):
                unit = jnp.maximum(want_smem[j, 0, owner * CAP + rank], 0)
                if j:
                    stage[part, r, j - 1, rank] = work[unit]
                else:
                    slots[part, (cls * ring + owner) * CAP + rank] = work[unit]
            if j == 1:
                slot_copy(part, j, r).start()
            elif j:
                pl.when(x == 0)(lambda: slot_copy(part, j, r).start())

    for part in range(2):
        extract(part, 0, lambda b: near[part, b * BLOCK_LENGTH : (b + 1) * BLOCK_LENGTH])
    for t in range(rows_y):
        deal(t)
        if t == 0:
            keep_copy().start()
        else:
            x_copy(t).start()

    def from_below(s, part):
        extract(part, ring - 1 - s, lambda b: up[s, part, b])

    def from_above(s, part):
        extract(part, 1 + s, lambda b: down[s, part, b])

    def relay(s, part, b, parts_up, parts_down):
        up_copy(s, part, b, some).wait_recv()
        if part in parts_up:
            up_copy(s + 1, part, b).start()
        down_copy(s, part, b, some).wait_recv()
        if part in parts_down:
            down_copy(s + 1, part, b).start()

    def step(s, _):
        relay(s, 0, 0, (0, 1), (0, 1))
        pl.when(s > 0)(lambda: from_above(s - 1, 1))
        pl.when(s < KV_HEADS)(lambda: local_part(s, 0))
        relay(s, 0, 1, (0, 1), (0, 1))
        from_below(s, 0)
        relay(s, 1, 0, (0, 1), (0, 1))
        from_above(s, 0)
        pl.when(s < KV_HEADS)(lambda: local_part(s, 1))
        relay(s, 1, 1, (0, 1), (0, 1))
        from_below(s, 1)
        return 0

    lax.fori_loop(0, half - 2, step, 0)
    s = half - 2
    relay(s, 0, 0, (0,), (1,))
    from_above(s - 1, 1)
    relay(s, 0, 1, (0,), (1,))
    from_below(s, 0)
    relay(s, 1, 0, (0,), (1,))
    from_above(s, 0)
    relay(s, 1, 1, (0,), (1,))
    from_below(s, 1)
    from_above(s, 1)
    for b in range(2):
        up_copy(half - 1, 0, b, some).wait_recv()
    extract(0, half, lambda b: up[half - 1, 0, b])
    for b in range(2):
        down_copy(half - 1, 1, b, some).wait_recv()
    extract(1, half, lambda b: down[half - 1, 1, b])

    def drain(s, _):
        for part in range(2):
            for b in range(2):
                up_copy(s, part, b, some).wait_send()
                down_copy(s, part, b, some).wait_send()
        return 0

    lax.fori_loop(0, half - 1, drain, 0)
    for b in range(2):
        up_copy(half - 1, 0, b, some).wait_send()
        down_copy(half - 1, 1, b, some).wait_send()

    def drain_slots(r, _):
        for part in range(2):
            slot_copy(part, 1, r).wait()
            for j in (2, 3):
                pl.when(x == 0)(lambda: slot_copy(part, j, r).wait_send())
                pl.when(x == 1)(lambda: slot_copy(part, j, r).wait_recv())
        return 0

    lax.fori_loop(0, ring, drain_slots, 0)
    keep_copy().wait()
    for t in range(1, rows_y):
        x_copy(t).wait()


NT = (((1,), (1,)), ((), ()))
TN = (((0,), (0,)), ((), ()))
SCALE = HEAD_WIDTH ** (-0.5)


def stat_lines(lse_ref, delta_ref, lines):
    for which, ref in enumerate((lse_ref, delta_ref)):
        stat = ref[...].astype(jnp.float32)
        for b in range(2):
            for h in range(KV_HEADS):
                at = slice(b * BLOCK_LENGTH, (b + 1) * BLOCK_LENGTH)
                pieces = [stat[h * GROUP + i : h * GROUP + i + 1, at] for i in range(GROUP)]
                lines[which, b * KV_HEADS + h] = jnp.concatenate(pieces, axis=1)


def stacked_rows(ref, h, b):
    rows = slice(b * BLOCK_LENGTH, (b + 1) * BLOCK_LENGTH)
    return jnp.concatenate(
        [ref[rows, wide(h * GROUP + i)] for i in range(GROUP)], axis=0
    )


def wide(i):
    if isinstance(i, int):
        return slice(i * HEAD_WIDTH, (i + 1) * HEAD_WIDTH)
    return pl.ds(pl.multiple_of(i * HEAD_WIDTH, HEAD_WIDTH), HEAD_WIDTH)


def score_grads(keys, values, queries, grads, mask, lse, delta):
    scores = lax.dot_general(keys, queries, NT, preferred_element_type=jnp.float32) * SCALE
    prob = jnp.where(mask, jnp.exp(scores - lse), 0.0)
    dprob = lax.dot_general(values, grads, NT, preferred_element_type=jnp.float32)
    return prob.astype(jnp.bfloat16), (prob * (dprob - delta)).astype(jnp.bfloat16)


def attend_local(h, b, near, q, g, lines, dk, dv, dq_local):
    unit = b * KV_HEADS + h
    local = (b + 1) * BLOCK_LENGTH
    queries, grads = stacked_rows(q, h, b), stacked_rows(g, h, b)
    keys, values = near[0, :local, wide(h)], near[1, :local, wide(h)]
    shape = (local, GROUP * BLOCK_LENGTH)
    row = lax.broadcasted_iota(jnp.int32, shape, 1) % BLOCK_LENGTH + b * BLOCK_LENGTH
    mask = lax.broadcasted_iota(jnp.int32, shape, 0) <= row
    prob, dscore = score_grads(
        keys, values, queries, grads, mask, lines[0, unit], lines[1, unit]
    )
    dq_local[unit] = lax.dot_general(dscore, keys, TN, preferred_element_type=jnp.float32)
    key_part = jnp.dot(dscore, queries, preferred_element_type=jnp.float32) * SCALE
    value_part = jnp.dot(prob, grads, preferred_element_type=jnp.float32)
    for out, grad in ((dk, key_part), (dv, value_part)):
        if b == 0:
            out[:BLOCK_LENGTH, wide(h)] = grad
        else:
            out[:BLOCK_LENGTH, wide(h)] += grad[:BLOCK_LENGTH]
            out[BLOCK_LENGTH:, wide(h)] = grad[BLOCK_LENGTH:]


def chosen_rows(slots, meta, part, first):
    return jnp.concatenate(
        [slots[part, meta[first + i]] for i in range(CHOSEN_BLOCKS)], axis=0
    )


def attend_keys(meta, slots, q, g, lines, parts, probs, dscores):
    shape = (CHOSEN_BLOCKS * BLOCK_LENGTH, GROUP * BLOCK_LENGTH)
    key = lax.broadcasted_iota(jnp.int32, shape, 0)
    for b in range(2):
        for h in range(KV_HEADS):
            unit = b * KV_HEADS + h
            first = unit * CHOSEN_BLOCKS
            keys, values = (chosen_rows(slots, meta, part, first) for part in range(2))
            queries, grads = stacked_rows(q, h, b), stacked_rows(g, h, b)
            mask = None
            for i in range(CHOSEN_BLOCKS):
                begin = i * BLOCK_LENGTH
                limit = jnp.where(meta[64 + first + i] > 0, begin + BLOCK_LENGTH, begin)
                inside = (key >= begin) & (key < limit)
                mask = inside if mask is None else mask | inside
            prob, dscore = score_grads(
                keys, values, queries, grads, mask, lines[0, unit], lines[1, unit]
            )
            probs[unit] = prob
            dscores[unit] = dscore
            grad = (jnp.dot(dscore, queries, preferred_element_type=jnp.float32) * SCALE).astype(
                jnp.bfloat16
            )
            for i in range(CHOSEN_BLOCKS):
                parts[0, first + i] = grad[i * BLOCK_LENGTH : (i + 1) * BLOCK_LENGTH]


def attend_rest(meta, slots, g, parts, probs, dscores, dq_local, dq_ref):
    for b in range(2):
        for h in range(KV_HEADS):
            unit = b * KV_HEADS + h
            first = unit * CHOSEN_BLOCKS
            grad = jnp.dot(
                probs[unit], stacked_rows(g, h, b), preferred_element_type=jnp.float32
            ).astype(jnp.bfloat16)
            for i in range(CHOSEN_BLOCKS):
                parts[1, first + i] = grad[i * BLOCK_LENGTH : (i + 1) * BLOCK_LENGTH]
            keys = chosen_rows(slots, meta, 0, first)
            dq = dq_local[unit] + lax.dot_general(
                dscores[unit], keys, TN, preferred_element_type=jnp.float32
            )
            dq = (dq * SCALE).astype(jnp.bfloat16)
            for i in range(GROUP):
                dq_ref[b * BLOCK_LENGTH : (b + 1) * BLOCK_LENGTH, wide(h * GROUP + i)] = dq[
                    i * BLOCK_LENGTH : (i + 1) * BLOCK_LENGTH
                ]


def reduce_stage(
    ring, rows_y, weight_scale, part_ref, want_smem, index_smem, dk_ref, dv_ref, xg_ref,
    kg_ref, vg_ref, wg_ref,
    up, down, ups, downs, arrived, stage, mine,
    all_k, own, across, shared, to_x, from_x, pieces, to_z, from_z,
    up_send, up_recv, down_send, down_recv, s_send, s_recv,
    y_send, y_recv, c_send, c_recv, x_send, x_recv, z_send, z_recv, rest,
):
    half = ring // 2
    x, z, c = place(ring)
    high = lax.rem(lax.axis_index("dp"), 2)
    cls = x * 2 + c
    above, below = along(ring, 1), along(ring, -1)

    def slot_copy(part, j, r):
        return push(
            stage.at[part, j - 1, r], arrived.at[part, j - 1, r],
            s_send.at[part, j - 1, r], s_recv.at[part, j - 1, r], member(ring, j)[0],
        )

    def term_of(part, line, owner, rank):
        return part_ref[part, index_smem[line, 0, owner * CAP + rank]]

    def send_slots(part, r):
        owner = lax.rem(z + r, ring)

        def send(j):
            line = member(ring, j)[1]
            for rank in range(CAP):
                stage[part, j - 1, r, rank] = term_of(part, line, owner, rank)
            slot_copy(part, j, r).start()

        for j in (2, 3):
            pl.when(x == 1)(lambda: send(j))
        send(1)

    def below_of(act, part, s):
        pl.when((s >= 0) & (s <= half))(lambda: act(part, half - s))

    def above_of(act, part, s):
        pl.when((s > 0) & (s < half))(lambda: act(part, half + s))

    def up_copy(part, s, b):
        return push(
            ups.at[part, s, b], up.at[part, s, b], up_send.at[part, s, b], up_recv.at[part, s, b], above
        )

    def down_copy(part, s, b):
        return push(
            downs.at[part, s, b], down.at[part, s, b],
            down_send.at[part, s, b], down_recv.at[part, s, b], below,
        )

    def gather_terms(part, r):
        owner = lax.rem(z + r, ring)

        def add(mates, before):
            units = [[want_smem[j, 0, owner * CAP + rank] for rank in range(CAP)] for j in mates]
            for b in range(2):
                for h in range(KV_HEADS):
                    at = (part, r, b, slice(None), slice(h * HEAD_WIDTH, (h + 1) * HEAD_WIDTH))
                    acc = mine[at] if before else jnp.zeros((BLOCK_LENGTH, HEAD_WIDTH), jnp.float32)
                    for j, asked in zip(mates, units, strict=True):
                        for rank in range(CAP):
                            if j == 0:
                                term = term_of(part, cls, owner, rank)
                            else:
                                term = arrived[part, j - 1, r, rank]
                            hit = asked[rank] == b * KV_HEADS + h
                            acc = acc + jnp.where(hit, term.astype(jnp.float32), 0.0)
                    mine[at] = acc

        slot_copy(part, 1, r).wait_recv()
        add((0, 1), False)

        @pl.when(x == 0)
        def _():
            for j in (2, 3):
                slot_copy(part, j, r).wait_recv()
            add((2, 3), True)

    def first(part, d):
        copy, outgoing = ((up_copy, ups), (down_copy, downs))[d]
        outgoing[part, 0, d] = mine[part, half, d].astype(jnp.bfloat16)
        copy(part, 0, d).start()

    def hop(part, s, d, b):
        copy, arrival, outgoing = ((up_copy, up, ups), (down_copy, down, downs))[d]
        r = half + s if d else half - s
        if d == b:
            copy(part, s - 1, b).wait_recv()
        else:
            pl.when(s > 1)(lambda: copy(part, s - 1, b).wait_recv())
        value = arrival[part, s - 1, b].astype(jnp.float32) + mine[part, r, b]
        outgoing[part, s, b] = value.astype(jnp.bfloat16)
        copy(part, s, b).start()

    def last(part):
        near, outs = ((dk_ref, (kg_ref, own)), (dv_ref, (vg_ref,)))[part]
        for b in range(2):
            up_copy(part, half - 1, b).wait_recv()
            down_copy(part, half - 1, b).wait_recv()
            rows = slice(b * BLOCK_LENGTH, (b + 1) * BLOCK_LENGTH)
            value = near[rows] + mine[part, 0, b]
            value = value + up[part, half - 1, b].astype(jnp.float32)
            value = value + down[part, half - 1, b].astype(jnp.float32)
            for out in outs:
                out[rows] = value.astype(jnp.bfloat16)

    send_slots(0, half)
    for s in range(1, AHEAD + 1):
        send_slots(0, half - s)
        send_slots(0, half + s)
    blank = jnp.zeros((BLOCK_LENGTH, KV_HEADS * HEAD_WIDTH), jnp.bfloat16)
    for part in range(2):
        up[part, 0, 1] = blank
        down[part, 0, 0] = blank

    y = lax.axis_index("dp") // 2

    def y_copy(t):
        return push(own, all_k.at[y], y_send.at[t - 1], y_recv.at[t - 1], column_mate(t))

    def c_copy():
        return push(across.at[:, 1 - c], shared, c_send, c_recv, member(ring, 1)[0])

    def x_copy(j):
        mate, lo, hi = row_mate(ring, j)
        return push(
            to_x.at[lo, hi], from_x.at[j - 1], x_send.at[j - 1], x_recv.at[j - 1], mate
        )

    def z_copy(d):
        return push(
            to_z.at[lax.rem(z + d, ring)], from_z.at[d - 1],
            z_send.at[d - 1], z_recv.at[d - 1], along(ring, d),
        )

    def start_weights():
        for t in range(1, rows_y):
            y_copy(t).start()
        all_k[y] = own[...]

    def multiply():
        for t in range(1, rows_y):
            y_copy(t).wait_recv()
        gathered = all_k[...].reshape(rows_y * TOKENS, KV_HEADS * HEAD_WIDTH)
        for lo in range(2):
            product = jnp.dot(xg_ref[lo], gathered, preferred_element_type=jnp.float32)
            for core in range(2):
                for hi in range(2):
                    begin = (core * 2 + hi) * 4 * ring
                    across[lo, core, hi] = product[begin : begin + 4 * ring]
        c_copy().start()

    def add_core():
        c_copy().wait()
        for lo in range(2):
            for hi in range(2):
                value = across[lo, c, hi] + shared[lo, hi]
                across[lo, c, hi] = value
                to_x[lo, hi] = value.astype(jnp.bfloat16)
        for j in (1, 2, 3):
            x_copy(j).start()

    def add_row():
        for j in (1, 2, 3):
            x_copy(j).wait()
        value = across[x, c, high]
        for j in range(3):
            value = value + from_x[j].astype(jnp.float32)
        for i in range(ring):
            piece = value[4 * i : 4 * i + 4]
            pieces[i] = piece
            to_z[i] = jnp.concatenate([piece[:, wide(n)] for n in range(KV_HEADS)], axis=0).astype(
                jnp.bfloat16
            )
        for d in range(1, ring):
            z_copy(d).start()

    rest()
    gather_terms(0, half)
    first(0, 0)
    first(0, 1)
    gather_terms(0, half - 1)
    gather_terms(0, half + 1)
    jobs = (
        (half, start_weights), (half + MULTIPLY, multiply), (half + ADD_CORE, add_core),
        (half + ADD_ROW, add_row),
    )
    end = half + LAG

    def step(t, _):
        behind = t - LAG
        fillers = (
            (below_of, send_slots, AHEAD, AHEAD_V), (above_of, send_slots, AHEAD, AHEAD_V),
            (below_of, gather_terms, 1, 1), (above_of, gather_terms, 1, 1),
        )
        for (d, b), (of, act, lead, lead_v) in zip(((0, 0), (1, 1), (0, 1), (1, 0)), fillers, strict=True):
            pl.when(t < half)(lambda: hop(0, t, d, b))
            of(act, 0, t + lead)
            if d == b:
                pl.when(behind == 0)(lambda: first(1, d))
            pl.when(behind > 0)(lambda: hop(1, behind, d, b))
            of(act, 1, behind + lead_v)
        pl.when(t == half)(lambda: last(0))
        for at, act in jobs:
            pl.when(t == at)(act)
        return 0

    lax.fori_loop(1, end, step, 0)
    last(1)
    for at, act in jobs:
        if at >= end:
            act()
    value = jnp.zeros(from_z.shape[1:], jnp.float32)
    for d in range(1, ring):
        z_copy(d).wait_recv()
        value = value + from_z[d - 1].astype(jnp.float32)
    value = jnp.concatenate([value[4 * n : 4 * n + 4] for n in range(KV_HEADS)], axis=1)
    wg_ref[...] = (pieces[z] + value) * weight_scale

    for t in range(1, rows_y):
        y_copy(t).wait_send()
    for d in range(1, ring):
        z_copy(d).wait_send()
    for part in range(2):
        up_copy(part, 0, 0).wait_send()
        down_copy(part, 0, 1).wait_send()

        def drain(s, _):
            for b in range(2):
                up_copy(part, s, b).wait_send()
                down_copy(part, s, b).wait_send()
            return 0

        lax.fori_loop(1, half, drain, 0)

        def drain_slots(r, _):
            slot_copy(part, 1, r).wait_send()
            for j in (2, 3):
                pl.when(x == 1)(lambda: slot_copy(part, j, r).wait_send())
            return 0

        lax.fori_loop(0, ring, drain_slots, 0)


def fused_kernel(
    ring, rows_y, weight_scale, chosen_ref, k_ref, v_ref, x_ref, q_ref, g_ref, lse_ref, delta_ref,
    dq_ref, kg_ref, vg_ref, wg_ref,
    slots, wants, index, meta, want_smem, index_smem, xg, near, q, g, dk, dv, parts,
    lines, dq_local, probs, dscores,
    in_sem, smem_sem, *scratch,
):
    loads = [
        pltpu.make_async_copy(src, dst, in_sem.at[i])
        for i, (src, dst) in enumerate(
            (
                (k_ref, near.at[0]), (v_ref, near.at[1]), (x_ref, scratch[GATHER_INPUT]),
                (q_ref, q), (g_ref, g),
            )
        )
    ]
    for load in loads:
        load.start()
    far_x = [row_mate(ring, j)[0] for j in (1, 3)]
    far_z = [{"ctx": along(ring, d)} for d in range(2, ring - 1)]
    stat_lines(lse_ref, delta_ref, lines)
    greet(neighbours(ring) + [column_mate(t) for t in range(1, rows_y)] + far_x + far_z)
    gather_stage(
        ring, rows_y, chosen_ref, k_ref, v_ref, x_ref, q_ref, g_ref, q, g, slots, wants, index, meta, want_smem, xg, near,
        *scratch[:GATHER_SCRATCH], smem_sem, in_sem,
        lambda h, b: attend_local(h, b, near, q, g, lines, dk, dv, dq_local),
    )
    table = pltpu.make_async_copy(index, index_smem, smem_sem.at[1])
    table.start()
    attend_keys(meta, slots, q, g, lines, parts, probs, dscores)
    table.wait()
    reduce_stage(
        ring, rows_y, weight_scale, parts, want_smem, index_smem, dk, dv, xg,
        kg_ref, vg_ref, wg_ref, *scratch[GATHER_SCRATCH:],
        lambda: attend_rest(meta, slots, g, parts, probs, dscores, dq_local, dq_ref),
    )


def fused_call(ring, rows_y, weight_scale, chosen, keys, values, inputs, queries, grads, lse, delta):
    half = ring // 2
    lines = 16 * ring
    width = KV_HEADS * HEAD_WIDTH
    number = 2 * KV_HEADS * CHOSEN_BLOCKS
    hbm, vmem = pl.BlockSpec(memory_space=pl.ANY), pl.BlockSpec(memory_space=pltpu.VMEM)
    smem = pl.BlockSpec(memory_space=pltpu.SMEM)
    dma = pltpu.SemaphoreType.DMA
    low, full = jnp.bfloat16, jnp.float32
    table = (4, 8, 128)
    shared = [
        pltpu.VMEM((2, 4 * ring * CAP, BLOCK_LENGTH, HEAD_WIDTH), low),
        pltpu.VMEM(table, jnp.int32),
        pltpu.VMEM(table, jnp.int32),
        pltpu.SMEM((128,), jnp.int32),
        pltpu.SMEM(table, jnp.int32),
        pltpu.SMEM(table, jnp.int32),
        pltpu.VMEM((2, lines, rows_y * TOKENS), low),
        pltpu.VMEM((2,) + keys.shape, low),
        pltpu.VMEM(queries.shape, low),
        pltpu.VMEM(queries.shape, low),
        pltpu.VMEM(keys.shape, full),
        pltpu.VMEM(keys.shape, full),
        pltpu.VMEM((2, number, BLOCK_LENGTH, HEAD_WIDTH), low),
        pltpu.VMEM((2, UNITS, 1, GROUP * BLOCK_LENGTH), full),
        pltpu.VMEM((UNITS, GROUP * BLOCK_LENGTH, HEAD_WIDTH), full),
        pltpu.VMEM((UNITS, CHOSEN_BLOCKS * BLOCK_LENGTH, GROUP * BLOCK_LENGTH), low),
        pltpu.VMEM((UNITS, CHOSEN_BLOCKS * BLOCK_LENGTH, GROUP * BLOCK_LENGTH), low),
        dma((5,)), dma((2,)),
    ]
    gather_ring = pltpu.VMEM((half, 2, 2, BLOCK_LENGTH, width), low)
    gather_sem = dma((half, 2, 2))
    gather = [
        gather_ring, gather_ring,
        pltpu.VMEM((2, ring, 3, CAP, BLOCK_LENGTH, HEAD_WIDTH), low),
        pltpu.VMEM((UNITS, BLOCK_LENGTH, HEAD_WIDTH), low),
        pltpu.VMEM(table, jnp.int32),
        pltpu.VMEM((rows_y, 2, lines, TOKENS), low),
        pltpu.VMEM(inputs.shape, low),
        gather_sem, gather_sem, gather_sem, gather_sem,
        dma((3,)), dma((3,)), dma((2, 3, ring)), dma((2, 3, ring)), dma((rows_y,)), dma((rows_y,)),
    ]
    reduce_ring, reduce_sem = pltpu.VMEM((2, half, 2, BLOCK_LENGTH, width), low), dma((2, half, 2))
    reduce = [
        reduce_ring, reduce_ring, reduce_ring, reduce_ring,
        pltpu.VMEM((2, 3, ring, CAP, BLOCK_LENGTH, HEAD_WIDTH), low),
        pltpu.VMEM((2, 3, ring, CAP, BLOCK_LENGTH, HEAD_WIDTH), low),
        pltpu.VMEM((2, ring, 2, BLOCK_LENGTH, width), full),
        pltpu.VMEM((rows_y, TOKENS, width), low),
        pltpu.VMEM((TOKENS, width), low),
        pltpu.VMEM((2, 2, 2, 4 * ring, width), full),
        pltpu.VMEM((2, 2, 4 * ring, width), full),
        pltpu.VMEM((2, 2, 4 * ring, width), low),
        pltpu.VMEM((3, 4 * ring, width), low),
        pltpu.VMEM((ring, 4, width), full),
        pltpu.VMEM((ring, 4 * KV_HEADS, HEAD_WIDTH), low),
        pltpu.VMEM((ring - 1, 4 * KV_HEADS, HEAD_WIDTH), low),
        reduce_sem, reduce_sem, reduce_sem, reduce_sem,
        dma((2, 3, ring)), dma((2, 3, ring)),
        dma((rows_y - 1,)), dma((rows_y - 1,)), dma, dma,
        dma((3,)), dma((3,)), dma((ring - 1,)), dma((ring - 1,)),
    ]
    assert len(gather) == GATHER_SCRATCH
    return pl.pallas_call(
        functools.partial(fused_kernel, ring, rows_y, weight_scale),
        out_shape=(
            jax.ShapeDtypeStruct(queries.shape, low),
            jax.ShapeDtypeStruct((TOKENS, width), low),
            jax.ShapeDtypeStruct((TOKENS, width), low),
            jax.ShapeDtypeStruct((4, width), full),
        ),
        in_specs=[smem, hbm, hbm, hbm, hbm, hbm, vmem, vmem],
        out_specs=(vmem,) * 4,
        scratch_shapes=shared + gather + reduce,
        compiler_params=pltpu.CompilerParams(
            collective_id=0, has_side_effects=True, vmem_limit_bytes=VMEM_BYTES
        ),
        name="fused_blocks",
    )(chosen, keys, values, inputs, queries, grads, lse, delta)


def hand_over_kernel(*refs):
    n = len(refs) // 2
    for i in range(n):
        refs[n + i][...] = refs[i][...]


def hand_over(*arrays):
    vmem = pl.BlockSpec(memory_space=pltpu.VMEM)
    return pl.pallas_call(
        hand_over_kernel,
        in_specs=[vmem] * len(arrays),
        out_specs=(vmem,) * len(arrays),
        out_shape=tuple(jax.ShapeDtypeStruct(a.shape, a.dtype) for a in arrays),
        name="hand_over",
    )(*arrays)


def body(
    query_states,
    key_activations,
    value_activations,
    out_grad,
    logsumexp,
    row_delta,
    layer_input,
    chosen,
):
    shards = lax.axis_size("ctx")
    replicas = lax.axis_size("dp")
    ring = shards // 4
    rows_y = replicas // 2
    keys, values = key_activations[0], value_activations[0]
    weight_scale = 1.0 / math.sqrt(TOKENS * shards * replicas)
    outputs = fused_call(
        ring, rows_y, weight_scale, chosen[0], keys, values, layer_input[0],
        query_states[0], out_grad[0], logsumexp[0], row_delta[0],
    )
    query_grad, key_gradient, value_gradient, key_weight_grad = hand_over(*outputs)
    return (query_grad[None], key_gradient[None], value_gradient[None], key_weight_grad)


def solution(mesh):
    seq = P("dp", "ctx", None)
    stat = P("dp", None, "ctx")
    return jax.shard_map(
        body,
        mesh=mesh,
        in_specs=(seq, seq, seq, seq, stat, stat, seq, P("dp", "ctx", None, None)),
        out_specs=(seq, seq, seq, P(("ctx", "dp"), None)),
        check_vma=False,
    )
```

```python
import functools
import math

import jax
import jax.numpy as jnp
from jax import lax
from jax.experimental import pallas as pl
from jax.experimental.pallas import tpu as pltpu
from jax.sharding import PartitionSpec as P

HEAD_WIDTH = 128
BLOCK_LENGTH = 64
CHOSEN_BLOCKS = 3
CAP = 2
KV_HEADS = 4
GROUP = 4
TOKENS = 128
UNITS = TOKENS // BLOCK_LENGTH * KV_HEADS
LAG = 5
AHEAD = 4
AHEAD_V = 4
MULTIPLY, ADD_CORE, ADD_ROW = 2, 3, 4
VMEM_BYTES = 58 * 1024 * 1024
GATHER_INPUT, GATHER_SCRATCH = 6, 17
MESH = pl.DeviceIdType.MESH


def place(ring):
    i = lax.axis_index("ctx")
    return i // (2 * ring), lax.rem(i // 2, ring), lax.rem(i, 2)


def member(ring, j):
    x, z, c = place(ring)
    mx = lax.rem(x + j // 2, 2)
    mc = lax.rem(c + j % 2, 2)
    return mx * (2 * ring) + z * 2 + mc, mx * 2 + mc


def along(ring, step):
    x, z, c = place(ring)
    return x * (2 * ring) + lax.rem(z + step + ring, ring) * 2 + c


def column_mate(step):
    i, d = lax.axis_index("ctx"), lax.axis_index("dp")
    rows = lax.axis_size("dp") // 2
    return {"ctx": i, "dp": lax.rem(d // 2 + step, rows) * 2 + lax.rem(d, 2)}


def row_mate(ring, j):
    x, z, c = place(ring)
    d = lax.axis_index("dp")
    lo, hi = lax.rem(x + j // 2, 2), lax.rem(lax.rem(d, 2) + j % 2, 2)
    return {"ctx": lo * (2 * ring) + z * 2 + c, "dp": d // 2 * 2 + hi}, lo, hi


def greet(others, meanwhile):
    barrier = pltpu.get_barrier_semaphore()
    for other in others:
        pl.semaphore_signal(barrier, inc=1, device_id=other, device_id_type=MESH)
    meanwhile()
    pl.semaphore_wait(barrier, len(others))


def neighbours(ring):
    places = [along(ring, 1), along(ring, -1)] + [member(ring, j)[0] for j in (1, 2, 3)]
    return [{"ctx": other} for other in places]


def push(src, dst, send, recv, other):
    other = other if isinstance(other, dict) else {"ctx": other}
    return pltpu.make_async_remote_copy(
        src_ref=src, dst_ref=dst, send_sem=send, recv_sem=recv,
        device_id=other, device_id_type=MESH,
    )


def gather_stage(
    ring, rows_y, chosen_ref, k_ref, v_ref, x_ref, q_ref, g_ref, q, g, slots, wants, index, meta, want_smem, xg, near,
    up, down, stage, work, want, xt, xin,
    up_send, up_recv, down_send, down_recv, w_send, w_recv, s_send, s_recv, x_send, x_recv,
    smem_sem, in_sem, local_part,
):
    half = ring // 2
    x, z, c = place(ring)
    cls = x * 2 + c
    above, below = along(ring, 1), along(ring, -1)

    def up_copy(s, part, b, src=None):
        at = (s, part, b)
        src = up.at[s - 1, part, b] if src is None else src
        return push(src, up.at[at], up_send.at[at], up_recv.at[at], above)

    def down_copy(s, part, b, src=None):
        at = (s, part, b)
        src = down.at[s - 1, part, b] if src is None else src
        return push(src, down.at[at], down_send.at[at], down_recv.at[at], below)

    some = k_ref.at[:BLOCK_LENGTH]
    for part, ref in ((0, k_ref), (1, v_ref)):
        for b in range(2):
            rows = ref.at[b * BLOCK_LENGTH : (b + 1) * BLOCK_LENGTH]
            up_copy(0, part, b, rows).start()
            down_copy(0, part, b, rows).start()

    shape = (4, 8, 128)
    spot = lax.broadcasted_iota(jnp.int32, shape, 0) * 128 + lax.broadcasted_iota(jnp.int32, shape, 2)
    wanted = jnp.full(shape, -1, jnp.int32)
    spots = jnp.zeros(shape, jnp.int32)
    owners = []
    for i in range(2 * KV_HEADS * CHOSEN_BLOCKS):
        b, h = i // (KV_HEADS * CHOSEN_BLOCKS), i // CHOSEN_BLOCKS % KV_HEADS
        choice = chosen_ref[0, i % CHOSEN_BLOCKS, b, h]
        active = choice >= 0
        block = jnp.maximum(choice, 0)
        owner = block // 2
        marked = jnp.where(active, owner, -1)
        rank = jnp.int32(0)
        for other in owners:
            rank = rank + jnp.where(other == marked, 1, 0)
        owners.append(marked)
        line = (owner // (2 * ring)) * 2 + lax.rem(owner, 2)
        entry = lax.rem(owner // 2, ring) * CAP + rank
        hit = spot == jnp.where(active, line * 128 + entry, -1)
        wanted = jnp.where(hit, lax.rem(block, 2) * KV_HEADS + i // CHOSEN_BLOCKS % KV_HEADS, wanted)
        spots = jnp.where(hit, i, spots)
        meta[i] = jnp.where(active, line * ring * CAP + entry, 0)
        meta[64 + i] = jnp.where(active, 1, 0)
    want[...] = wanted
    index[...] = spots

    def want_copy(j):
        other, other_cls = member(ring, j)
        return push(want.at[other_cls], wants.at[j], w_send.at[j - 1], w_recv.at[j - 1], other)

    for j in (1, 2, 3):
        want_copy(j).start()
    wants[0] = want[cls]

    y = lax.axis_index("dp") // 2
    lines = 16 * ring
    half_width = lines * rows_y

    def x_copy(t):
        return push(
            xt.at[t], xg.at[:, :, pl.ds(pl.multiple_of(y * TOKENS, TOKENS), TOKENS)],
            x_send.at[t], x_recv.at[t], column_mate(t),
        )

    def keep_copy():
        return pltpu.make_async_copy(
            xt.at[0], xg.at[:, :, pl.ds(pl.multiple_of(y * TOKENS, TOKENS), TOKENS)], x_send.at[0]
        )

    def deal(t):
        to = lax.rem(y + t, rows_y)
        line = lax.broadcasted_iota(jnp.int32, (lines, half_width), 0)
        column = lax.broadcasted_iota(jnp.int32, (lines, half_width), 1)
        core, high, rest = line // (8 * ring), line // (4 * ring) % 2, line % (4 * ring)
        source = rest // 4 * (16 * rows_y) + core * (8 * rows_y) + to * 8 + high * 4 + rest % 4
        pick = jnp.where(column == source, 1.0, 0.0).astype(jnp.bfloat16)
        for lo in range(2):
            part = xin[:, lo * half_width : (lo + 1) * half_width]
            xt[t, lo] = lax.dot_general(
                pick, part, (((1,), (1,)), ((), ())), preferred_element_type=jnp.float32
            ).astype(jnp.bfloat16)

    loads = [
        pltpu.make_async_copy(src, dst, in_sem.at[i])
        for i, (src, dst) in enumerate(
            (
                (k_ref, near.at[0]), (v_ref, near.at[1]), (x_ref, xin), (q_ref, q), (g_ref, g),
            )
        )
    ]
    for load in loads:
        load.wait()
    for j in (1, 2, 3):
        want_copy(j).wait()
    table = pltpu.make_async_copy(wants, want_smem, smem_sem.at[0])
    table.start()
    table.wait()

    def slot_copy(part, j, r):
        owner = lax.rem(z + r, ring)
        return push(
            stage.at[part, r, j - 1], slots.at[part, pl.ds((cls * ring + owner) * CAP, CAP)],
            s_send.at[part, j - 1, r], s_recv.at[part, j - 1, r], member(ring, j)[0],
        )

    def extract(part, r, chunk):
        owner = lax.rem(z + r, ring)
        for b in range(2):
            for h in range(KV_HEADS):
                work[b * KV_HEADS + h] = chunk(b)[:, h * HEAD_WIDTH : (h + 1) * HEAD_WIDTH]
        for j in (2, 3, 1, 0):
            for rank in range(CAP):
                unit = jnp.maximum(want_smem[j, 0, owner * CAP + rank], 0)
                if j:
                    stage[part, r, j - 1, rank] = work[unit]
                else:
                    slots[part, (cls * ring + owner) * CAP + rank] = work[unit]
            if j == 1:
                slot_copy(part, j, r).start()
            elif j:
                pl.when(x == 0)(lambda: slot_copy(part, j, r).start())

    for part in range(2):
        extract(part, 0, lambda b: near[part, b * BLOCK_LENGTH : (b + 1) * BLOCK_LENGTH])
    for t in range(rows_y):
        deal(t)
        if t == 0:
            keep_copy().start()
        else:
            x_copy(t).start()

    def from_below(s, part):
        extract(part, ring - 1 - s, lambda b: up[s, part, b])

    def from_above(s, part):
        extract(part, 1 + s, lambda b: down[s, part, b])

    def relay(s, part, b, parts_up, parts_down):
        up_copy(s, part, b, some).wait_recv()
        if part in parts_up:
            up_copy(s + 1, part, b).start()
        down_copy(s, part, b, some).wait_recv()
        if part in parts_down:
            down_copy(s + 1, part, b).start()

    def step(s, _):
        relay(s, 0, 0, (0, 1), (0, 1))
        pl.when(s > 0)(lambda: from_above(s - 1, 1))
        pl.when(s < KV_HEADS)(lambda: local_part(s, 0))
        relay(s, 0, 1, (0, 1), (0, 1))
        from_below(s, 0)
        relay(s, 1, 0, (0, 1), (0, 1))
        from_above(s, 0)
        pl.when(s < KV_HEADS)(lambda: local_part(s, 1))
        relay(s, 1, 1, (0, 1), (0, 1))
        from_below(s, 1)
        return 0

    lax.fori_loop(0, half - 2, step, 0)
    s = half - 2
    relay(s, 0, 0, (0,), (1,))
    from_above(s - 1, 1)
    relay(s, 0, 1, (0,), (1,))
    from_below(s, 0)
    relay(s, 1, 0, (0,), (1,))
    from_above(s, 0)
    relay(s, 1, 1, (0,), (1,))
    from_below(s, 1)
    from_above(s, 1)
    for b in range(2):
        up_copy(half - 1, 0, b, some).wait_recv()
    extract(0, half, lambda b: up[half - 1, 0, b])
    for b in range(2):
        down_copy(half - 1, 1, b, some).wait_recv()
    extract(1, half, lambda b: down[half - 1, 1, b])

    def drain(s, _):
        for part in range(2):
            for b in range(2):
                up_copy(s, part, b, some).wait_send()
                down_copy(s, part, b, some).wait_send()
        return 0

    lax.fori_loop(0, half - 1, drain, 0)
    for b in range(2):
        up_copy(half - 1, 0, b, some).wait_send()
        down_copy(half - 1, 1, b, some).wait_send()

    def drain_slots(r, _):
        for part in range(2):
            slot_copy(part, 1, r).wait()
            for j in (2, 3):
                pl.when(x == 0)(lambda: slot_copy(part, j, r).wait_send())
                pl.when(x == 1)(lambda: slot_copy(part, j, r).wait_recv())
        return 0

    lax.fori_loop(0, ring, drain_slots, 0)
    keep_copy().wait()
    for t in range(1, rows_y):
        x_copy(t).wait()


NT = (((1,), (1,)), ((), ()))
TN = (((0,), (0,)), ((), ()))
SCALE = HEAD_WIDTH ** (-0.5)


def stat_lines(lse_ref, delta_ref, lines):
    for which, ref in enumerate((lse_ref, delta_ref)):
        stat = ref[...].astype(jnp.float32)
        for b in range(2):
            for h in range(KV_HEADS):
                at = slice(b * BLOCK_LENGTH, (b + 1) * BLOCK_LENGTH)
                pieces = [stat[h * GROUP + i : h * GROUP + i + 1, at] for i in range(GROUP)]
                lines[which, b * KV_HEADS + h] = jnp.concatenate(pieces, axis=1)


def stacked_rows(ref, h, b):
    rows = slice(b * BLOCK_LENGTH, (b + 1) * BLOCK_LENGTH)
    return jnp.concatenate(
        [ref[rows, wide(h * GROUP + i)] for i in range(GROUP)], axis=0
    )


def wide(i):
    if isinstance(i, int):
        return slice(i * HEAD_WIDTH, (i + 1) * HEAD_WIDTH)
    return pl.ds(pl.multiple_of(i * HEAD_WIDTH, HEAD_WIDTH), HEAD_WIDTH)


def score_grads(keys, values, queries, grads, mask, lse, delta):
    scores = lax.dot_general(keys, queries, NT, preferred_element_type=jnp.float32) * SCALE
    prob = jnp.where(mask, jnp.exp(scores - lse), 0.0)
    dprob = lax.dot_general(values, grads, NT, preferred_element_type=jnp.float32)
    return prob.astype(jnp.bfloat16), (prob * (dprob - delta)).astype(jnp.bfloat16)


def attend_local(h, b, near, q, g, lines, dk, dv, dq_local):
    unit = b * KV_HEADS + h
    local = (b + 1) * BLOCK_LENGTH
    queries, grads = stacked_rows(q, h, b), stacked_rows(g, h, b)
    keys, values = near[0, :local, wide(h)], near[1, :local, wide(h)]
    shape = (local, GROUP * BLOCK_LENGTH)
    row = lax.broadcasted_iota(jnp.int32, shape, 1) % BLOCK_LENGTH + b * BLOCK_LENGTH
    mask = lax.broadcasted_iota(jnp.int32, shape, 0) <= row
    prob, dscore = score_grads(
        keys, values, queries, grads, mask, lines[0, unit], lines[1, unit]
    )
    dq_local[unit] = lax.dot_general(dscore, keys, TN, preferred_element_type=jnp.float32)
    key_part = jnp.dot(dscore, queries, preferred_element_type=jnp.float32) * SCALE
    value_part = jnp.dot(prob, grads, preferred_element_type=jnp.float32)
    for out, grad in ((dk, key_part), (dv, value_part)):
        if b == 0:
            out[:BLOCK_LENGTH, wide(h)] = grad
        else:
            out[:BLOCK_LENGTH, wide(h)] += grad[:BLOCK_LENGTH]
            out[BLOCK_LENGTH:, wide(h)] = grad[BLOCK_LENGTH:]


def chosen_rows(slots, meta, part, first):
    return jnp.concatenate(
        [slots[part, meta[first + i]] for i in range(CHOSEN_BLOCKS)], axis=0
    )


def attend_keys(meta, slots, q, g, lines, parts, probs, dscores):
    shape = (CHOSEN_BLOCKS * BLOCK_LENGTH, GROUP * BLOCK_LENGTH)
    key = lax.broadcasted_iota(jnp.int32, shape, 0)
    for b in range(2):
        for h in range(KV_HEADS):
            unit = b * KV_HEADS + h
            first = unit * CHOSEN_BLOCKS
            keys, values = (chosen_rows(slots, meta, part, first) for part in range(2))
            queries, grads = stacked_rows(q, h, b), stacked_rows(g, h, b)
            mask = None
            for i in range(CHOSEN_BLOCKS):
                begin = i * BLOCK_LENGTH
                limit = jnp.where(meta[64 + first + i] > 0, begin + BLOCK_LENGTH, begin)
                inside = (key >= begin) & (key < limit)
                mask = inside if mask is None else mask | inside
            prob, dscore = score_grads(
                keys, values, queries, grads, mask, lines[0, unit], lines[1, unit]
            )
            probs[unit] = prob
            dscores[unit] = dscore
            grad = (jnp.dot(dscore, queries, preferred_element_type=jnp.float32) * SCALE).astype(
                jnp.bfloat16
            )
            for i in range(CHOSEN_BLOCKS):
                parts[0, first + i] = grad[i * BLOCK_LENGTH : (i + 1) * BLOCK_LENGTH]


def attend_rest(meta, slots, g, parts, probs, dscores, dq_local, dq_ref):
    for b in range(2):
        for h in range(KV_HEADS):
            unit = b * KV_HEADS + h
            first = unit * CHOSEN_BLOCKS
            grad = jnp.dot(
                probs[unit], stacked_rows(g, h, b), preferred_element_type=jnp.float32
            ).astype(jnp.bfloat16)
            for i in range(CHOSEN_BLOCKS):
                parts[1, first + i] = grad[i * BLOCK_LENGTH : (i + 1) * BLOCK_LENGTH]
            keys = chosen_rows(slots, meta, 0, first)
            dq = dq_local[unit] + lax.dot_general(
                dscores[unit], keys, TN, preferred_element_type=jnp.float32
            )
            dq = (dq * SCALE).astype(jnp.bfloat16)
            for i in range(GROUP):
                dq_ref[b * BLOCK_LENGTH : (b + 1) * BLOCK_LENGTH, wide(h * GROUP + i)] = dq[
                    i * BLOCK_LENGTH : (i + 1) * BLOCK_LENGTH
                ]


def reduce_stage(
    ring, rows_y, weight_scale, part_ref, want_smem, index_smem, dk_ref, dv_ref, xg_ref,
    kg_ref, vg_ref, wg_ref,
    up, down, ups, downs, arrived, stage, mine,
    all_k, own, across, shared, to_x, from_x, pieces, to_z, from_z,
    up_send, up_recv, down_send, down_recv, s_send, s_recv,
    y_send, y_recv, c_send, c_recv, x_send, x_recv, z_send, z_recv, rest,
):
    half = ring // 2
    x, z, c = place(ring)
    high = lax.rem(lax.axis_index("dp"), 2)
    cls = x * 2 + c
    above, below = along(ring, 1), along(ring, -1)

    def slot_copy(part, j, r):
        return push(
            stage.at[part, j - 1, r], arrived.at[part, j - 1, r],
            s_send.at[part, j - 1, r], s_recv.at[part, j - 1, r], member(ring, j)[0],
        )

    def term_of(part, line, owner, rank):
        return part_ref[part, index_smem[line, 0, owner * CAP + rank]]

    def send_slots(part, r):
        owner = lax.rem(z + r, ring)

        def send(j):
            line = member(ring, j)[1]
            for rank in range(CAP):
                stage[part, j - 1, r, rank] = term_of(part, line, owner, rank)
            slot_copy(part, j, r).start()

        for j in (2, 3):
            pl.when(x == 1)(lambda: send(j))
        send(1)

    def below_of(act, part, s):
        pl.when((s >= 0) & (s <= half))(lambda: act(part, half - s))

    def above_of(act, part, s):
        pl.when((s > 0) & (s < half))(lambda: act(part, half + s))

    def up_copy(part, s, b):
        return push(
            ups.at[part, s, b], up.at[part, s, b], up_send.at[part, s, b], up_recv.at[part, s, b], above
        )

    def down_copy(part, s, b):
        return push(
            downs.at[part, s, b], down.at[part, s, b],
            down_send.at[part, s, b], down_recv.at[part, s, b], below,
        )

    def gather_terms(part, r):
        owner = lax.rem(z + r, ring)

        def add(mates, before):
            units = [[want_smem[j, 0, owner * CAP + rank] for rank in range(CAP)] for j in mates]
            for b in range(2):
                for h in range(KV_HEADS):
                    at = (part, r, b, slice(None), slice(h * HEAD_WIDTH, (h + 1) * HEAD_WIDTH))
                    acc = mine[at] if before else jnp.zeros((BLOCK_LENGTH, HEAD_WIDTH), jnp.float32)
                    for j, asked in zip(mates, units, strict=True):
                        for rank in range(CAP):
                            if j == 0:
                                term = term_of(part, cls, owner, rank)
                            else:
                                term = arrived[part, j - 1, r, rank]
                            hit = asked[rank] == b * KV_HEADS + h
                            acc = acc + jnp.where(hit, term.astype(jnp.float32), 0.0)
                    mine[at] = acc

        slot_copy(part, 1, r).wait_recv()
        add((0, 1), False)

        @pl.when(x == 0)
        def _():
            for j in (2, 3):
                slot_copy(part, j, r).wait_recv()
            add((2, 3), True)

    def first(part, d):
        copy, outgoing = ((up_copy, ups), (down_copy, downs))[d]
        outgoing[part, 0, d] = mine[part, half, d].astype(jnp.bfloat16)
        copy(part, 0, d).start()

    def hop(part, s, d, b):
        copy, arrival, outgoing = ((up_copy, up, ups), (down_copy, down, downs))[d]
        r = half + s if d else half - s
        if d == b:
            copy(part, s - 1, b).wait_recv()
        else:
            pl.when(s > 1)(lambda: copy(part, s - 1, b).wait_recv())
        value = arrival[part, s - 1, b].astype(jnp.float32) + mine[part, r, b]
        outgoing[part, s, b] = value.astype(jnp.bfloat16)
        copy(part, s, b).start()

    def last(part):
        near, outs = ((dk_ref, (kg_ref, own)), (dv_ref, (vg_ref,)))[part]
        for b in range(2):
            up_copy(part, half - 1, b).wait_recv()
            down_copy(part, half - 1, b).wait_recv()
            rows = slice(b * BLOCK_LENGTH, (b + 1) * BLOCK_LENGTH)
            value = near[rows] + mine[part, 0, b]
            value = value + up[part, half - 1, b].astype(jnp.float32)
            value = value + down[part, half - 1, b].astype(jnp.float32)
            for out in outs:
                out[rows] = value.astype(jnp.bfloat16)

    send_slots(0, half)
    for s in range(1, AHEAD + 1):
        send_slots(0, half - s)
        send_slots(0, half + s)
    blank = jnp.zeros((BLOCK_LENGTH, KV_HEADS * HEAD_WIDTH), jnp.bfloat16)
    for part in range(2):
        up[part, 0, 1] = blank
        down[part, 0, 0] = blank

    y = lax.axis_index("dp") // 2

    def y_copy(t):
        return push(own, all_k.at[y], y_send.at[t - 1], y_recv.at[t - 1], column_mate(t))

    def c_copy():
        return push(across.at[:, 1 - c], shared, c_send, c_recv, member(ring, 1)[0])

    def x_copy(j):
        mate, lo, hi = row_mate(ring, j)
        return push(
            to_x.at[lo, hi], from_x.at[j - 1], x_send.at[j - 1], x_recv.at[j - 1], mate
        )

    def z_copy(d):
        return push(
            to_z.at[lax.rem(z + d, ring)], from_z.at[d - 1],
            z_send.at[d - 1], z_recv.at[d - 1], along(ring, d),
        )

    def start_weights():
        for t in range(1, rows_y):
            y_copy(t).start()
        all_k[y] = own[...]

    def multiply():
        for t in range(1, rows_y):
            y_copy(t).wait_recv()
        gathered = all_k[...].reshape(rows_y * TOKENS, KV_HEADS * HEAD_WIDTH)
        for lo in range(2):
            product = jnp.dot(xg_ref[lo], gathered, preferred_element_type=jnp.float32)
            for core in range(2):
                for hi in range(2):
                    begin = (core * 2 + hi) * 4 * ring
                    across[lo, core, hi] = product[begin : begin + 4 * ring]
        c_copy().start()

    def add_core():
        c_copy().wait()
        for lo in range(2):
            for hi in range(2):
                value = across[lo, c, hi] + shared[lo, hi]
                across[lo, c, hi] = value
                to_x[lo, hi] = value.astype(jnp.bfloat16)
        for j in (1, 2, 3):
            x_copy(j).start()

    def add_row():
        for j in (1, 2, 3):
            x_copy(j).wait()
        value = across[x, c, high]
        for j in range(3):
            value = value + from_x[j].astype(jnp.float32)
        for i in range(ring):
            piece = value[4 * i : 4 * i + 4]
            pieces[i] = piece
            to_z[i] = jnp.concatenate([piece[:, wide(n)] for n in range(KV_HEADS)], axis=0).astype(
                jnp.bfloat16
            )
        for d in range(1, ring):
            z_copy(d).start()

    rest()
    gather_terms(0, half)
    first(0, 0)
    first(0, 1)
    gather_terms(0, half - 1)
    gather_terms(0, half + 1)
    jobs = (
        (half, start_weights), (half + MULTIPLY, multiply), (half + ADD_CORE, add_core),
        (half + ADD_ROW, add_row),
    )
    end = half + LAG

    def step(t, _):
        behind = t - LAG
        fillers = (
            (below_of, send_slots, AHEAD, AHEAD_V), (above_of, send_slots, AHEAD, AHEAD_V),
            (below_of, gather_terms, 1, 1), (above_of, gather_terms, 1, 1),
        )
        for (d, b), (of, act, lead, lead_v) in zip(((0, 0), (1, 1), (0, 1), (1, 0)), fillers, strict=True):
            pl.when(t < half)(lambda: hop(0, t, d, b))
            of(act, 0, t + lead)
            if d == b:
                pl.when(behind == 0)(lambda: first(1, d))
            pl.when(behind > 0)(lambda: hop(1, behind, d, b))
            of(act, 1, behind + lead_v)
        pl.when(t == half)(lambda: last(0))
        for at, act in jobs:
            pl.when(t == at)(act)
        return 0

    lax.fori_loop(1, end, step, 0)
    last(1)
    for at, act in jobs:
        if at >= end:
            act()
    value = jnp.zeros(from_z.shape[1:], jnp.float32)
    for d in range(1, ring):
        z_copy(d).wait_recv()
        value = value + from_z[d - 1].astype(jnp.float32)
    value = jnp.concatenate([value[4 * n : 4 * n + 4] for n in range(KV_HEADS)], axis=1)
    wg_ref[...] = (pieces[z] + value) * weight_scale

    for t in range(1, rows_y):
        y_copy(t).wait_send()
    for d in range(1, ring):
        z_copy(d).wait_send()
    for part in range(2):
        up_copy(part, 0, 0).wait_send()
        down_copy(part, 0, 1).wait_send()

        def drain(s, _):
            for b in range(2):
                up_copy(part, s, b).wait_send()
                down_copy(part, s, b).wait_send()
            return 0

        lax.fori_loop(1, half, drain, 0)

        def drain_slots(r, _):
            slot_copy(part, 1, r).wait_send()
            for j in (2, 3):
                pl.when(x == 1)(lambda: slot_copy(part, j, r).wait_send())
            return 0

        lax.fori_loop(0, ring, drain_slots, 0)


def fused_kernel(
    ring, rows_y, weight_scale, chosen_ref, k_ref, v_ref, x_ref, q_ref, g_ref, lse_ref, delta_ref,
    dq_ref, kg_ref, vg_ref, wg_ref,
    slots, wants, index, meta, want_smem, index_smem, xg, near, q, g, dk, dv, parts,
    lines, dq_local, probs, dscores, chosen_smem,
    in_sem, smem_sem, *scratch,
):
    loads = [
        pltpu.make_async_copy(src, dst, in_sem.at[i])
        for i, (src, dst) in enumerate(
            (
                (k_ref, near.at[0]), (v_ref, near.at[1]), (x_ref, scratch[GATHER_INPUT]),
                (q_ref, q), (g_ref, g),
            )
        )
    ]
    for load in loads:
        load.start()
    choices = pltpu.make_async_copy(chosen_ref, chosen_smem, in_sem.at[5])
    choices.start()
    far_x = [row_mate(ring, j)[0] for j in (1, 3)]
    far_z = [{"ctx": along(ring, d)} for d in range(2, ring - 1)]
    greet(
        neighbours(ring) + [column_mate(t) for t in range(1, rows_y)] + far_x + far_z,
        lambda: stat_lines(lse_ref, delta_ref, lines),
    )
    choices.wait()
    gather_stage(
        ring, rows_y, chosen_smem, k_ref, v_ref, x_ref, q_ref, g_ref, q, g, slots, wants, index, meta, want_smem, xg, near,
        *scratch[:GATHER_SCRATCH], smem_sem, in_sem,
        lambda h, b: attend_local(h, b, near, q, g, lines, dk, dv, dq_local),
    )
    table = pltpu.make_async_copy(index, index_smem, smem_sem.at[1])
    table.start()
    attend_keys(meta, slots, q, g, lines, parts, probs, dscores)
    table.wait()
    reduce_stage(
        ring, rows_y, weight_scale, parts, want_smem, index_smem, dk, dv, xg,
        kg_ref, vg_ref, wg_ref, *scratch[GATHER_SCRATCH:],
        lambda: attend_rest(meta, slots, g, parts, probs, dscores, dq_local, dq_ref),
    )


def fused_call(ring, rows_y, weight_scale, chosen, keys, values, inputs, queries, grads, lse, delta):
    half = ring // 2
    lines = 16 * ring
    width = KV_HEADS * HEAD_WIDTH
    number = 2 * KV_HEADS * CHOSEN_BLOCKS
    hbm, vmem = pl.BlockSpec(memory_space=pl.ANY), pl.BlockSpec(memory_space=pltpu.VMEM)
    dma = pltpu.SemaphoreType.DMA
    low, full = jnp.bfloat16, jnp.float32
    table = (4, 8, 128)
    shared = [
        pltpu.VMEM((2, 4 * ring * CAP, BLOCK_LENGTH, HEAD_WIDTH), low),
        pltpu.VMEM(table, jnp.int32),
        pltpu.VMEM(table, jnp.int32),
        pltpu.SMEM((128,), jnp.int32),
        pltpu.SMEM(table, jnp.int32),
        pltpu.SMEM(table, jnp.int32),
        pltpu.VMEM((2, lines, rows_y * TOKENS), low),
        pltpu.VMEM((2,) + keys.shape, low),
        pltpu.VMEM(queries.shape, low),
        pltpu.VMEM(queries.shape, low),
        pltpu.VMEM(keys.shape, full),
        pltpu.VMEM(keys.shape, full),
        pltpu.VMEM((2, number, BLOCK_LENGTH, HEAD_WIDTH), low),
        pltpu.VMEM((2, UNITS, 1, GROUP * BLOCK_LENGTH), full),
        pltpu.VMEM((UNITS, GROUP * BLOCK_LENGTH, HEAD_WIDTH), full),
        pltpu.VMEM((UNITS, CHOSEN_BLOCKS * BLOCK_LENGTH, GROUP * BLOCK_LENGTH), low),
        pltpu.VMEM((UNITS, CHOSEN_BLOCKS * BLOCK_LENGTH, GROUP * BLOCK_LENGTH), low),
        pltpu.SMEM(chosen.shape, jnp.int32),
        dma((6,)), dma((2,)),
    ]
    gather_ring = pltpu.VMEM((half, 2, 2, BLOCK_LENGTH, width), low)
    gather_sem = dma((half, 2, 2))
    gather = [
        gather_ring, gather_ring,
        pltpu.VMEM((2, ring, 3, CAP, BLOCK_LENGTH, HEAD_WIDTH), low),
        pltpu.VMEM((UNITS, BLOCK_LENGTH, HEAD_WIDTH), low),
        pltpu.VMEM(table, jnp.int32),
        pltpu.VMEM((rows_y, 2, lines, TOKENS), low),
        pltpu.VMEM(inputs.shape, low),
        gather_sem, gather_sem, gather_sem, gather_sem,
        dma((3,)), dma((3,)), dma((2, 3, ring)), dma((2, 3, ring)), dma((rows_y,)), dma((rows_y,)),
    ]
    reduce_ring, reduce_sem = pltpu.VMEM((2, half, 2, BLOCK_LENGTH, width), low), dma((2, half, 2))
    reduce = [
        reduce_ring, reduce_ring, reduce_ring, reduce_ring,
        pltpu.VMEM((2, 3, ring, CAP, BLOCK_LENGTH, HEAD_WIDTH), low),
        pltpu.VMEM((2, 3, ring, CAP, BLOCK_LENGTH, HEAD_WIDTH), low),
        pltpu.VMEM((2, ring, 2, BLOCK_LENGTH, width), full),
        pltpu.VMEM((rows_y, TOKENS, width), low),
        pltpu.VMEM((TOKENS, width), low),
        pltpu.VMEM((2, 2, 2, 4 * ring, width), full),
        pltpu.VMEM((2, 2, 4 * ring, width), full),
        pltpu.VMEM((2, 2, 4 * ring, width), low),
        pltpu.VMEM((3, 4 * ring, width), low),
        pltpu.VMEM((ring, 4, width), full),
        pltpu.VMEM((ring, 4 * KV_HEADS, HEAD_WIDTH), low),
        pltpu.VMEM((ring - 1, 4 * KV_HEADS, HEAD_WIDTH), low),
        reduce_sem, reduce_sem, reduce_sem, reduce_sem,
        dma((2, 3, ring)), dma((2, 3, ring)),
        dma((rows_y - 1,)), dma((rows_y - 1,)), dma, dma,
        dma((3,)), dma((3,)), dma((ring - 1,)), dma((ring - 1,)),
    ]
    assert len(gather) == GATHER_SCRATCH
    return pl.pallas_call(
        functools.partial(fused_kernel, ring, rows_y, weight_scale),
        out_shape=(
            jax.ShapeDtypeStruct(queries.shape, low),
            jax.ShapeDtypeStruct((TOKENS, width), low),
            jax.ShapeDtypeStruct((TOKENS, width), low),
            jax.ShapeDtypeStruct((4, width), full),
        ),
        in_specs=[hbm, hbm, hbm, hbm, hbm, hbm, vmem, vmem],
        out_specs=(vmem,) * 4,
        scratch_shapes=shared + gather + reduce,
        compiler_params=pltpu.CompilerParams(
            collective_id=0, has_side_effects=True, vmem_limit_bytes=VMEM_BYTES
        ),
        name="fused_blocks",
    )(chosen, keys, values, inputs, queries, grads, lse, delta)


def hand_over_kernel(*refs):
    n = len(refs) // 2
    for i in range(n):
        refs[n + i][...] = refs[i][...]


def hand_over(*arrays):
    vmem = pl.BlockSpec(memory_space=pltpu.VMEM)
    return pl.pallas_call(
        hand_over_kernel,
        in_specs=[vmem] * len(arrays),
        out_specs=(vmem,) * len(arrays),
        out_shape=tuple(jax.ShapeDtypeStruct(a.shape, a.dtype) for a in arrays),
        name="hand_over",
    )(*arrays)


def body(
    query_states,
    key_activations,
    value_activations,
    out_grad,
    logsumexp,
    row_delta,
    layer_input,
    chosen,
):
    shards = lax.axis_size("ctx")
    replicas = lax.axis_size("dp")
    ring = shards // 4
    rows_y = replicas // 2
    keys, values = key_activations[0], value_activations[0]
    weight_scale = 1.0 / math.sqrt(TOKENS * shards * replicas)
    outputs = fused_call(
        ring, rows_y, weight_scale, chosen.transpose(0, 3, 1, 2), keys, values, layer_input[0],
        query_states[0], out_grad[0], logsumexp[0], row_delta[0],
    )
    query_grad, key_gradient, value_gradient, key_weight_grad = hand_over(*outputs)
    return (query_grad[None], key_gradient[None], value_gradient[None], key_weight_grad)


def solution(mesh):
    seq = P("dp", "ctx", None)
    stat = P("dp", None, "ctx")
    return jax.shard_map(
        body,
        mesh=mesh,
        in_specs=(seq, seq, seq, seq, stat, stat, seq, P("dp", "ctx", None, None)),
        out_specs=(seq, seq, seq, P(("ctx", "dp"), None)),
        check_vma=False,
    )
```

```python
import functools
import math

import jax
import jax.numpy as jnp
from jax import lax
from jax.experimental import pallas as pl
from jax.experimental.pallas import tpu as pltpu
from jax.sharding import PartitionSpec as P

HEAD_WIDTH = 128
BLOCK_LENGTH = 64
CHOSEN_BLOCKS = 3
CAP = 2
KV_HEADS = 4
GROUP = 4
TOKENS = 128
UNITS = TOKENS // BLOCK_LENGTH * KV_HEADS
LAG = 6
AHEAD = 4
AHEAD_V = 4
MULTIPLY, ADD_CORE, ADD_ROW = 2, 3, 4
VMEM_BYTES = 58 * 1024 * 1024
GATHER_INPUT, GATHER_SCRATCH = 6, 17
MESH = pl.DeviceIdType.MESH


def place(ring):
    i = lax.axis_index("ctx")
    return i // (2 * ring), lax.rem(i // 2, ring), lax.rem(i, 2)


def member(ring, j):
    x, z, c = place(ring)
    mx = lax.rem(x + j // 2, 2)
    mc = lax.rem(c + j % 2, 2)
    return mx * (2 * ring) + z * 2 + mc, mx * 2 + mc


def along(ring, step):
    x, z, c = place(ring)
    return x * (2 * ring) + lax.rem(z + step + ring, ring) * 2 + c


def column_mate(step):
    i, d = lax.axis_index("ctx"), lax.axis_index("dp")
    rows = lax.axis_size("dp") // 2
    return {"ctx": i, "dp": lax.rem(d // 2 + step, rows) * 2 + lax.rem(d, 2)}


def row_mate(ring, j):
    x, z, c = place(ring)
    d = lax.axis_index("dp")
    lo, hi = lax.rem(x + j // 2, 2), lax.rem(lax.rem(d, 2) + j % 2, 2)
    return {"ctx": lo * (2 * ring) + z * 2 + c, "dp": d // 2 * 2 + hi}, lo, hi


def greet(others, meanwhile):
    barrier = pltpu.get_barrier_semaphore()
    for other in others:
        pl.semaphore_signal(barrier, inc=1, device_id=other, device_id_type=MESH)
    meanwhile()
    pl.semaphore_wait(barrier, len(others))


def neighbours(ring):
    places = [along(ring, 1), along(ring, -1)] + [member(ring, j)[0] for j in (1, 2, 3)]
    return [{"ctx": other} for other in places]


def push(src, dst, send, recv, other):
    other = other if isinstance(other, dict) else {"ctx": other}
    return pltpu.make_async_remote_copy(
        src_ref=src, dst_ref=dst, send_sem=send, recv_sem=recv,
        device_id=other, device_id_type=MESH,
    )


def gather_stage(
    ring, rows_y, chosen_ref, k_ref, v_ref, x_ref, q_ref, g_ref, q, g, slots, wants, index, meta, want_smem, xg, near,
    up, down, stage, work, want, xt, xin,
    up_send, up_recv, down_send, down_recv, w_send, w_recv, s_send, s_recv, x_send, x_recv,
    smem_sem, in_sem, local_part,
):
    half = ring // 2
    x, z, c = place(ring)
    cls = x * 2 + c
    above, below = along(ring, 1), along(ring, -1)

    def up_copy(s, part, b, src=None):
        at = (s, part, b)
        src = up.at[s - 1, part, b] if src is None else src
        return push(src, up.at[at], up_send.at[at], up_recv.at[at], above)

    def down_copy(s, part, b, src=None):
        at = (s, part, b)
        src = down.at[s - 1, part, b] if src is None else src
        return push(src, down.at[at], down_send.at[at], down_recv.at[at], below)

    some = k_ref.at[:BLOCK_LENGTH]
    for part, ref in ((0, k_ref), (1, v_ref)):
        for b in range(2):
            rows = ref.at[b * BLOCK_LENGTH : (b + 1) * BLOCK_LENGTH]
            up_copy(0, part, b, rows).start()
            down_copy(0, part, b, rows).start()

    shape = (4, 8, 128)
    spot = lax.broadcasted_iota(jnp.int32, shape, 0) * 128 + lax.broadcasted_iota(jnp.int32, shape, 2)
    wanted = jnp.full(shape, -1, jnp.int32)
    spots = jnp.zeros(shape, jnp.int32)
    owners = []
    for i in range(2 * KV_HEADS * CHOSEN_BLOCKS):
        b, h = i // (KV_HEADS * CHOSEN_BLOCKS), i // CHOSEN_BLOCKS % KV_HEADS
        choice = chosen_ref[0, i % CHOSEN_BLOCKS, b, h]
        active = choice >= 0
        block = jnp.maximum(choice, 0)
        owner = block // 2
        marked = jnp.where(active, owner, -1)
        rank = jnp.int32(0)
        for other in owners:
            rank = rank + jnp.where(other == marked, 1, 0)
        owners.append(marked)
        line = (owner // (2 * ring)) * 2 + lax.rem(owner, 2)
        entry = lax.rem(owner // 2, ring) * CAP + rank
        hit = spot == jnp.where(active, line * 128 + entry, -1)
        wanted = jnp.where(hit, lax.rem(block, 2) * KV_HEADS + i // CHOSEN_BLOCKS % KV_HEADS, wanted)
        spots = jnp.where(hit, i, spots)
        meta[i] = jnp.where(active, line * ring * CAP + entry, 0)
        meta[64 + i] = jnp.where(active, 1, 0)
    want[...] = wanted
    index[...] = spots

    def want_copy(j):
        other, other_cls = member(ring, j)
        return push(want.at[other_cls], wants.at[j], w_send.at[j - 1], w_recv.at[j - 1], other)

    for j in (1, 2, 3):
        want_copy(j).start()
    wants[0] = want[cls]

    y = lax.axis_index("dp") // 2
    lines = 16 * ring
    half_width = lines * rows_y

    def x_copy(t):
        return push(
            xt.at[t], xg.at[:, :, pl.ds(pl.multiple_of(y * TOKENS, TOKENS), TOKENS)],
            x_send.at[t], x_recv.at[t], column_mate(t),
        )

    def keep_copy():
        return pltpu.make_async_copy(
            xt.at[0], xg.at[:, :, pl.ds(pl.multiple_of(y * TOKENS, TOKENS), TOKENS)], x_send.at[0]
        )

    def deal(t):
        to = lax.rem(y + t, rows_y)
        line = lax.broadcasted_iota(jnp.int32, (lines, half_width), 0)
        column = lax.broadcasted_iota(jnp.int32, (lines, half_width), 1)
        core, high, rest = line // (8 * ring), line // (4 * ring) % 2, line % (4 * ring)
        source = rest // 4 * (16 * rows_y) + core * (8 * rows_y) + to * 8 + high * 4 + rest % 4
        pick = jnp.where(column == source, 1.0, 0.0).astype(jnp.bfloat16)
        for lo in range(2):
            part = xin[:, lo * half_width : (lo + 1) * half_width]
            xt[t, lo] = lax.dot_general(
                pick, part, (((1,), (1,)), ((), ())), preferred_element_type=jnp.float32
            ).astype(jnp.bfloat16)

    loads = [
        pltpu.make_async_copy(src, dst, in_sem.at[i])
        for i, (src, dst) in enumerate(
            (
                (k_ref, near.at[0]), (v_ref, near.at[1]), (x_ref, xin), (q_ref, q), (g_ref, g),
            )
        )
    ]
    for load in loads:
        load.wait()
    for j in (1, 2, 3):
        want_copy(j).wait()
    table = pltpu.make_async_copy(wants, want_smem, smem_sem.at[0])
    table.start()
    table.wait()

    def slot_copy(part, j, r):
        owner = lax.rem(z + r, ring)
        return push(
            stage.at[part, r, j - 1], slots.at[part, pl.ds((cls * ring + owner) * CAP, CAP)],
            s_send.at[part, j - 1, r], s_recv.at[part, j - 1, r], member(ring, j)[0],
        )

    def extract(part, r, chunk):
        owner = lax.rem(z + r, ring)
        for b in range(2):
            for h in range(KV_HEADS):
                work[b * KV_HEADS + h] = chunk(b)[:, h * HEAD_WIDTH : (h + 1) * HEAD_WIDTH]
        for j in (2, 3, 1, 0):
            for rank in range(CAP):
                unit = jnp.maximum(want_smem[j, 0, owner * CAP + rank], 0)
                if j:
                    stage[part, r, j - 1, rank] = work[unit]
                else:
                    slots[part, (cls * ring + owner) * CAP + rank] = work[unit]
            if j == 1:
                slot_copy(part, j, r).start()
            elif j:
                pl.when(x == 0)(lambda: slot_copy(part, j, r).start())

    for part in range(2):
        extract(part, 0, lambda b: near[part, b * BLOCK_LENGTH : (b + 1) * BLOCK_LENGTH])
    for t in range(rows_y):
        deal(t)
        if t == 0:
            keep_copy().start()
        else:
            x_copy(t).start()

    def from_below(s, part):
        extract(part, ring - 1 - s, lambda b: up[s, part, b])

    def from_above(s, part):
        extract(part, 1 + s, lambda b: down[s, part, b])

    def relay(s, part, b, parts_up, parts_down):
        up_copy(s, part, b, some).wait_recv()
        if part in parts_up:
            up_copy(s + 1, part, b).start()
        down_copy(s, part, b, some).wait_recv()
        if part in parts_down:
            down_copy(s + 1, part, b).start()

    def step(s, _):
        relay(s, 0, 0, (0, 1), (0, 1))
        pl.when(s > 0)(lambda: from_above(s - 1, 1))
        pl.when(s < KV_HEADS)(lambda: local_part(s, 0))
        relay(s, 0, 1, (0, 1), (0, 1))
        from_below(s, 0)
        relay(s, 1, 0, (0, 1), (0, 1))
        from_above(s, 0)
        pl.when(s < KV_HEADS)(lambda: local_part(s, 1))
        relay(s, 1, 1, (0, 1), (0, 1))
        from_below(s, 1)
        return 0

    lax.fori_loop(0, half - 2, step, 0)
    s = half - 2
    relay(s, 0, 0, (0,), (1,))
    from_above(s - 1, 1)
    relay(s, 0, 1, (0,), (1,))
    from_below(s, 0)
    relay(s, 1, 0, (0,), (1,))
    from_above(s, 0)
    relay(s, 1, 1, (0,), (1,))
    from_below(s, 1)
    from_above(s, 1)
    for b in range(2):
        up_copy(half - 1, 0, b, some).wait_recv()
    extract(0, half, lambda b: up[half - 1, 0, b])
    for b in range(2):
        down_copy(half - 1, 1, b, some).wait_recv()
    extract(1, half, lambda b: down[half - 1, 1, b])

    def drain(s, _):
        for part in range(2):
            for b in range(2):
                up_copy(s, part, b, some).wait_send()
                down_copy(s, part, b, some).wait_send()
        return 0

    lax.fori_loop(0, half - 1, drain, 0)
    for b in range(2):
        up_copy(half - 1, 0, b, some).wait_send()
        down_copy(half - 1, 1, b, some).wait_send()

    def drain_slots(r, _):
        for part in range(2):
            slot_copy(part, 1, r).wait()
            for j in (2, 3):
                pl.when(x == 0)(lambda: slot_copy(part, j, r).wait_send())
                pl.when(x == 1)(lambda: slot_copy(part, j, r).wait_recv())
        return 0

    lax.fori_loop(0, ring, drain_slots, 0)
    keep_copy().wait()
    for t in range(1, rows_y):
        x_copy(t).wait()


NT = (((1,), (1,)), ((), ()))
TN = (((0,), (0,)), ((), ()))
SCALE = HEAD_WIDTH ** (-0.5)


def stat_lines(lse_ref, delta_ref, lines):
    for which, ref in enumerate((lse_ref, delta_ref)):
        stat = ref[...].astype(jnp.float32)
        for b in range(2):
            for h in range(KV_HEADS):
                at = slice(b * BLOCK_LENGTH, (b + 1) * BLOCK_LENGTH)
                pieces = [stat[h * GROUP + i : h * GROUP + i + 1, at] for i in range(GROUP)]
                lines[which, b * KV_HEADS + h] = jnp.concatenate(pieces, axis=1)


def stacked_rows(ref, h, b):
    rows = slice(b * BLOCK_LENGTH, (b + 1) * BLOCK_LENGTH)
    return jnp.concatenate(
        [ref[rows, wide(h * GROUP + i)] for i in range(GROUP)], axis=0
    )


def wide(i):
    if isinstance(i, int):
        return slice(i * HEAD_WIDTH, (i + 1) * HEAD_WIDTH)
    return pl.ds(pl.multiple_of(i * HEAD_WIDTH, HEAD_WIDTH), HEAD_WIDTH)


def score_grads(keys, values, queries, grads, mask, lse, delta):
    scores = lax.dot_general(keys, queries, NT, preferred_element_type=jnp.float32) * SCALE
    prob = jnp.where(mask, jnp.exp(scores - lse), 0.0)
    dprob = lax.dot_general(values, grads, NT, preferred_element_type=jnp.float32)
    return prob.astype(jnp.bfloat16), (prob * (dprob - delta)).astype(jnp.bfloat16)


def attend_local(h, b, near, q, g, lines, dk, dv, dq_local):
    unit = b * KV_HEADS + h
    local = (b + 1) * BLOCK_LENGTH
    queries, grads = stacked_rows(q, h, b), stacked_rows(g, h, b)
    keys, values = near[0, :local, wide(h)], near[1, :local, wide(h)]
    shape = (local, GROUP * BLOCK_LENGTH)
    row = lax.broadcasted_iota(jnp.int32, shape, 1) % BLOCK_LENGTH + b * BLOCK_LENGTH
    mask = lax.broadcasted_iota(jnp.int32, shape, 0) <= row
    prob, dscore = score_grads(
        keys, values, queries, grads, mask, lines[0, unit], lines[1, unit]
    )
    dq_local[unit] = lax.dot_general(dscore, keys, TN, preferred_element_type=jnp.float32)
    key_part = jnp.dot(dscore, queries, preferred_element_type=jnp.float32) * SCALE
    value_part = jnp.dot(prob, grads, preferred_element_type=jnp.float32)
    for out, grad in ((dk, key_part), (dv, value_part)):
        if b == 0:
            out[:BLOCK_LENGTH, wide(h)] = grad
        else:
            out[:BLOCK_LENGTH, wide(h)] += grad[:BLOCK_LENGTH]
            out[BLOCK_LENGTH:, wide(h)] = grad[BLOCK_LENGTH:]


def chosen_rows(slots, meta, part, first):
    return jnp.concatenate(
        [slots[part, meta[first + i]] for i in range(CHOSEN_BLOCKS)], axis=0
    )


def attend_keys(meta, slots, q, g, lines, parts, probs, dscores):
    shape = (CHOSEN_BLOCKS * BLOCK_LENGTH, GROUP * BLOCK_LENGTH)
    key = lax.broadcasted_iota(jnp.int32, shape, 0)
    for b in range(2):
        for h in range(KV_HEADS):
            unit = b * KV_HEADS + h
            first = unit * CHOSEN_BLOCKS
            keys, values = (chosen_rows(slots, meta, part, first) for part in range(2))
            queries, grads = stacked_rows(q, h, b), stacked_rows(g, h, b)
            mask = None
            for i in range(CHOSEN_BLOCKS):
                begin = i * BLOCK_LENGTH
                limit = jnp.where(meta[64 + first + i] > 0, begin + BLOCK_LENGTH, begin)
                inside = (key >= begin) & (key < limit)
                mask = inside if mask is None else mask | inside
            prob, dscore = score_grads(
                keys, values, queries, grads, mask, lines[0, unit], lines[1, unit]
            )
            probs[unit] = prob
            dscores[unit] = dscore
            grad = (jnp.dot(dscore, queries, preferred_element_type=jnp.float32) * SCALE).astype(
                jnp.bfloat16
            )
            for i in range(CHOSEN_BLOCKS):
                parts[0, first + i] = grad[i * BLOCK_LENGTH : (i + 1) * BLOCK_LENGTH]


def attend_rest(meta, slots, g, parts, probs, dscores, dq_local, dq_ref):
    for b in range(2):
        for h in range(KV_HEADS):
            unit = b * KV_HEADS + h
            first = unit * CHOSEN_BLOCKS
            grad = jnp.dot(
                probs[unit], stacked_rows(g, h, b), preferred_element_type=jnp.float32
            ).astype(jnp.bfloat16)
            for i in range(CHOSEN_BLOCKS):
                parts[1, first + i] = grad[i * BLOCK_LENGTH : (i + 1) * BLOCK_LENGTH]
            keys = chosen_rows(slots, meta, 0, first)
            dq = dq_local[unit] + lax.dot_general(
                dscores[unit], keys, TN, preferred_element_type=jnp.float32
            )
            dq = (dq * SCALE).astype(jnp.bfloat16)
            for i in range(GROUP):
                dq_ref[b * BLOCK_LENGTH : (b + 1) * BLOCK_LENGTH, wide(h * GROUP + i)] = dq[
                    i * BLOCK_LENGTH : (i + 1) * BLOCK_LENGTH
                ]


def reduce_stage(
    ring, rows_y, weight_scale, part_ref, want_smem, index_smem, dk_ref, dv_ref, xg_ref,
    kg_ref, vg_ref, wg_ref,
    up, down, ups, downs, arrived, stage, mine,
    all_k, own, across, shared, to_x, from_x, pieces, to_z, from_z,
    up_send, up_recv, down_send, down_recv, s_send, s_recv,
    y_send, y_recv, c_send, c_recv, x_send, x_recv, z_send, z_recv, rest,
):
    half = ring // 2
    x, z, c = place(ring)
    high = lax.rem(lax.axis_index("dp"), 2)
    cls = x * 2 + c
    above, below = along(ring, 1), along(ring, -1)

    def slot_copy(part, j, r):
        return push(
            stage.at[part, j - 1, r], arrived.at[part, j - 1, r],
            s_send.at[part, j - 1, r], s_recv.at[part, j - 1, r], member(ring, j)[0],
        )

    def term_of(part, line, owner, rank):
        return part_ref[part, index_smem[line, 0, owner * CAP + rank]]

    def send_slots(part, r):
        owner = lax.rem(z + r, ring)

        def send(j):
            line = member(ring, j)[1]
            for rank in range(CAP):
                stage[part, j - 1, r, rank] = term_of(part, line, owner, rank)
            slot_copy(part, j, r).start()

        for j in (2, 3):
            pl.when(x == 1)(lambda: send(j))
        send(1)

    def below_of(act, part, s):
        pl.when((s >= 0) & (s <= half))(lambda: act(part, half - s))

    def above_of(act, part, s):
        pl.when((s > 0) & (s < half))(lambda: act(part, half + s))

    def up_copy(part, s, b):
        return push(
            ups.at[part, s, b], up.at[part, s, b], up_send.at[part, s, b], up_recv.at[part, s, b], above
        )

    def down_copy(part, s, b):
        return push(
            downs.at[part, s, b], down.at[part, s, b],
            down_send.at[part, s, b], down_recv.at[part, s, b], below,
        )

    def gather_terms(part, r):
        owner = lax.rem(z + r, ring)

        def add(mates, before):
            units = [[want_smem[j, 0, owner * CAP + rank] for rank in range(CAP)] for j in mates]
            for b in range(2):
                for h in range(KV_HEADS):
                    at = (part, r, b, slice(None), slice(h * HEAD_WIDTH, (h + 1) * HEAD_WIDTH))
                    acc = mine[at] if before else jnp.zeros((BLOCK_LENGTH, HEAD_WIDTH), jnp.float32)
                    for j, asked in zip(mates, units, strict=True):
                        for rank in range(CAP):
                            if j == 0:
                                term = term_of(part, cls, owner, rank)
                            else:
                                term = arrived[part, j - 1, r, rank]
                            hit = asked[rank] == b * KV_HEADS + h
                            acc = acc + jnp.where(hit, term.astype(jnp.float32), 0.0)
                    mine[at] = acc

        slot_copy(part, 1, r).wait_recv()
        add((0, 1), False)

        @pl.when(x == 0)
        def _():
            for j in (2, 3):
                slot_copy(part, j, r).wait_recv()
            add((2, 3), True)

    def first(part, d):
        copy, outgoing = ((up_copy, ups), (down_copy, downs))[d]
        outgoing[part, 0, d] = mine[part, half, d].astype(jnp.bfloat16)
        copy(part, 0, d).start()

    def hop(part, s, d, b):
        copy, arrival, outgoing = ((up_copy, up, ups), (down_copy, down, downs))[d]
        r = half + s if d else half - s
        if d == b:
            copy(part, s - 1, b).wait_recv()
        else:
            pl.when(s > 1)(lambda: copy(part, s - 1, b).wait_recv())
        value = arrival[part, s - 1, b].astype(jnp.float32) + mine[part, r, b]
        outgoing[part, s, b] = value.astype(jnp.bfloat16)
        copy(part, s, b).start()

    def last(part):
        near, outs = ((dk_ref, (kg_ref, own)), (dv_ref, (vg_ref,)))[part]
        for b in range(2):
            up_copy(part, half - 1, b).wait_recv()
            down_copy(part, half - 1, b).wait_recv()
            rows = slice(b * BLOCK_LENGTH, (b + 1) * BLOCK_LENGTH)
            value = near[rows] + mine[part, 0, b]
            value = value + up[part, half - 1, b].astype(jnp.float32)
            value = value + down[part, half - 1, b].astype(jnp.float32)
            for out in outs:
                out[rows] = value.astype(jnp.bfloat16)

    send_slots(0, half)
    for s in range(1, AHEAD + 1):
        send_slots(0, half - s)
        send_slots(0, half + s)
    blank = jnp.zeros((BLOCK_LENGTH, KV_HEADS * HEAD_WIDTH), jnp.bfloat16)
    for part in range(2):
        up[part, 0, 1] = blank
        down[part, 0, 0] = blank

    y = lax.axis_index("dp") // 2

    def y_copy(t):
        return push(own, all_k.at[y], y_send.at[t - 1], y_recv.at[t - 1], column_mate(t))

    def c_copy():
        return push(across.at[:, 1 - c], shared, c_send, c_recv, member(ring, 1)[0])

    def x_copy(j):
        mate, lo, hi = row_mate(ring, j)
        return push(
            to_x.at[lo, hi], from_x.at[j - 1], x_send.at[j - 1], x_recv.at[j - 1], mate
        )

    def z_copy(d):
        return push(
            to_z.at[lax.rem(z + d, ring)], from_z.at[d - 1],
            z_send.at[d - 1], z_recv.at[d - 1], along(ring, d),
        )

    def start_weights():
        for t in range(1, rows_y):
            y_copy(t).start()
        all_k[y] = own[...]

    def multiply():
        for t in range(1, rows_y):
            y_copy(t).wait_recv()
        gathered = all_k[...].reshape(rows_y * TOKENS, KV_HEADS * HEAD_WIDTH)
        for lo in range(2):
            product = jnp.dot(xg_ref[lo], gathered, preferred_element_type=jnp.float32)
            for core in range(2):
                for hi in range(2):
                    begin = (core * 2 + hi) * 4 * ring
                    across[lo, core, hi] = product[begin : begin + 4 * ring]
        c_copy().start()

    def add_core():
        c_copy().wait()
        for lo in range(2):
            for hi in range(2):
                value = across[lo, c, hi] + shared[lo, hi]
                across[lo, c, hi] = value
                to_x[lo, hi] = value.astype(jnp.bfloat16)
        for j in (1, 2, 3):
            x_copy(j).start()

    def add_row():
        for j in (1, 2, 3):
            x_copy(j).wait()
        value = across[x, c, high]
        for j in range(3):
            value = value + from_x[j].astype(jnp.float32)
        for i in range(ring):
            piece = value[4 * i : 4 * i + 4]
            pieces[i] = piece
            to_z[i] = jnp.concatenate([piece[:, wide(n)] for n in range(KV_HEADS)], axis=0).astype(
                jnp.bfloat16
            )
        for d in range(1, ring):
            z_copy(d).start()

    rest()
    gather_terms(0, half)
    first(0, 0)
    first(0, 1)
    gather_terms(0, half - 1)
    gather_terms(0, half + 1)
    jobs = (
        (half, start_weights), (half + MULTIPLY, multiply), (half + ADD_CORE, add_core),
        (half + ADD_ROW, add_row),
    )
    end = half + LAG

    def step(t, _):
        behind = t - LAG
        fillers = (
            (below_of, send_slots, AHEAD, AHEAD_V), (above_of, send_slots, AHEAD, AHEAD_V),
            (below_of, gather_terms, 1, 1), (above_of, gather_terms, 1, 1),
        )
        for (d, b), (of, act, lead, lead_v) in zip(((0, 0), (1, 1), (0, 1), (1, 0)), fillers, strict=True):
            pl.when(t < half)(lambda: hop(0, t, d, b))
            of(act, 0, t + lead)
            if d == b:
                pl.when(behind == 0)(lambda: first(1, d))
            pl.when(behind > 0)(lambda: hop(1, behind, d, b))
            of(act, 1, behind + lead_v)
        pl.when(t == half)(lambda: last(0))
        for at, act in jobs:
            pl.when(t == at)(act)
        return 0

    lax.fori_loop(1, end, step, 0)
    last(1)
    for at, act in jobs:
        if at >= end:
            act()
    value = jnp.zeros(from_z.shape[1:], jnp.float32)
    for d in range(1, ring):
        z_copy(d).wait_recv()
        value = value + from_z[d - 1].astype(jnp.float32)
    value = jnp.concatenate([value[4 * n : 4 * n + 4] for n in range(KV_HEADS)], axis=1)
    wg_ref[...] = (pieces[z] + value) * weight_scale

    for t in range(1, rows_y):
        y_copy(t).wait_send()
    for d in range(1, ring):
        z_copy(d).wait_send()
    for part in range(2):
        up_copy(part, 0, 0).wait_send()
        down_copy(part, 0, 1).wait_send()

        def drain(s, _):
            for b in range(2):
                up_copy(part, s, b).wait_send()
                down_copy(part, s, b).wait_send()
            return 0

        lax.fori_loop(1, half, drain, 0)

        def drain_slots(r, _):
            slot_copy(part, 1, r).wait_send()
            for j in (2, 3):
                pl.when(x == 1)(lambda: slot_copy(part, j, r).wait_send())
            return 0

        lax.fori_loop(0, ring, drain_slots, 0)


def fused_kernel(
    ring, rows_y, weight_scale, chosen_ref, k_ref, v_ref, x_ref, q_ref, g_ref, lse_ref, delta_ref,
    dq_ref, kg_ref, vg_ref, wg_ref,
    slots, wants, index, meta, want_smem, index_smem, xg, near, q, g, dk, dv, parts,
    lines, dq_local, probs, dscores, chosen_smem,
    in_sem, smem_sem, *scratch,
):
    loads = [
        pltpu.make_async_copy(src, dst, in_sem.at[i])
        for i, (src, dst) in enumerate(
            (
                (k_ref, near.at[0]), (v_ref, near.at[1]), (x_ref, scratch[GATHER_INPUT]),
                (q_ref, q), (g_ref, g),
            )
        )
    ]
    for load in loads:
        load.start()
    choices = pltpu.make_async_copy(chosen_ref, chosen_smem, in_sem.at[5])
    choices.start()
    far_x = [row_mate(ring, j)[0] for j in (1, 3)]
    far_z = [{"ctx": along(ring, d)} for d in range(2, ring - 1)]
    greet(
        neighbours(ring) + [column_mate(t) for t in range(1, rows_y)] + far_x + far_z,
        lambda: stat_lines(lse_ref, delta_ref, lines),
    )
    choices.wait()
    gather_stage(
        ring, rows_y, chosen_smem, k_ref, v_ref, x_ref, q_ref, g_ref, q, g, slots, wants, index, meta, want_smem, xg, near,
        *scratch[:GATHER_SCRATCH], smem_sem, in_sem,
        lambda h, b: attend_local(h, b, near, q, g, lines, dk, dv, dq_local),
    )
    table = pltpu.make_async_copy(index, index_smem, smem_sem.at[1])
    table.start()
    attend_keys(meta, slots, q, g, lines, parts, probs, dscores)
    table.wait()
    reduce_stage(
        ring, rows_y, weight_scale, parts, want_smem, index_smem, dk, dv, xg,
        kg_ref, vg_ref, wg_ref, *scratch[GATHER_SCRATCH:],
        lambda: attend_rest(meta, slots, g, parts, probs, dscores, dq_local, dq_ref),
    )


def fused_call(ring, rows_y, weight_scale, chosen, keys, values, inputs, queries, grads, lse, delta):
    half = ring // 2
    lines = 16 * ring
    width = KV_HEADS * HEAD_WIDTH
    number = 2 * KV_HEADS * CHOSEN_BLOCKS
    hbm, vmem = pl.BlockSpec(memory_space=pl.ANY), pl.BlockSpec(memory_space=pltpu.VMEM)
    dma = pltpu.SemaphoreType.DMA
    low, full = jnp.bfloat16, jnp.float32
    table = (4, 8, 128)
    shared = [
        pltpu.VMEM((2, 4 * ring * CAP, BLOCK_LENGTH, HEAD_WIDTH), low),
        pltpu.VMEM(table, jnp.int32),
        pltpu.VMEM(table, jnp.int32),
        pltpu.SMEM((128,), jnp.int32),
        pltpu.SMEM(table, jnp.int32),
        pltpu.SMEM(table, jnp.int32),
        pltpu.VMEM((2, lines, rows_y * TOKENS), low),
        pltpu.VMEM((2,) + keys.shape, low),
        pltpu.VMEM(queries.shape, low),
        pltpu.VMEM(queries.shape, low),
        pltpu.VMEM(keys.shape, full),
        pltpu.VMEM(keys.shape, full),
        pltpu.VMEM((2, number, BLOCK_LENGTH, HEAD_WIDTH), low),
        pltpu.VMEM((2, UNITS, 1, GROUP * BLOCK_LENGTH), full),
        pltpu.VMEM((UNITS, GROUP * BLOCK_LENGTH, HEAD_WIDTH), full),
        pltpu.VMEM((UNITS, CHOSEN_BLOCKS * BLOCK_LENGTH, GROUP * BLOCK_LENGTH), low),
        pltpu.VMEM((UNITS, CHOSEN_BLOCKS * BLOCK_LENGTH, GROUP * BLOCK_LENGTH), low),
        pltpu.SMEM(chosen.shape, jnp.int32),
        dma((6,)), dma((2,)),
    ]
    gather_ring = pltpu.VMEM((half, 2, 2, BLOCK_LENGTH, width), low)
    gather_sem = dma((half, 2, 2))
    gather = [
        gather_ring, gather_ring,
        pltpu.VMEM((2, ring, 3, CAP, BLOCK_LENGTH, HEAD_WIDTH), low),
        pltpu.VMEM((UNITS, BLOCK_LENGTH, HEAD_WIDTH), low),
        pltpu.VMEM(table, jnp.int32),
        pltpu.VMEM((rows_y, 2, lines, TOKENS), low),
        pltpu.VMEM(inputs.shape, low),
        gather_sem, gather_sem, gather_sem, gather_sem,
        dma((3,)), dma((3,)), dma((2, 3, ring)), dma((2, 3, ring)), dma((rows_y,)), dma((rows_y,)),
    ]
    reduce_ring, reduce_sem = pltpu.VMEM((2, half, 2, BLOCK_LENGTH, width), low), dma((2, half, 2))
    reduce = [
        reduce_ring, reduce_ring, reduce_ring, reduce_ring,
        pltpu.VMEM((2, 3, ring, CAP, BLOCK_LENGTH, HEAD_WIDTH), low),
        pltpu.VMEM((2, 3, ring, CAP, BLOCK_LENGTH, HEAD_WIDTH), low),
        pltpu.VMEM((2, ring, 2, BLOCK_LENGTH, width), full),
        pltpu.VMEM((rows_y, TOKENS, width), low),
        pltpu.VMEM((TOKENS, width), low),
        pltpu.VMEM((2, 2, 2, 4 * ring, width), full),
        pltpu.VMEM((2, 2, 4 * ring, width), full),
        pltpu.VMEM((2, 2, 4 * ring, width), low),
        pltpu.VMEM((3, 4 * ring, width), low),
        pltpu.VMEM((ring, 4, width), full),
        pltpu.VMEM((ring, 4 * KV_HEADS, HEAD_WIDTH), low),
        pltpu.VMEM((ring - 1, 4 * KV_HEADS, HEAD_WIDTH), low),
        reduce_sem, reduce_sem, reduce_sem, reduce_sem,
        dma((2, 3, ring)), dma((2, 3, ring)),
        dma((rows_y - 1,)), dma((rows_y - 1,)), dma, dma,
        dma((3,)), dma((3,)), dma((ring - 1,)), dma((ring - 1,)),
    ]
    assert len(gather) == GATHER_SCRATCH
    return pl.pallas_call(
        functools.partial(fused_kernel, ring, rows_y, weight_scale),
        out_shape=(
            jax.ShapeDtypeStruct(queries.shape, low),
            jax.ShapeDtypeStruct((TOKENS, width), low),
            jax.ShapeDtypeStruct((TOKENS, width), low),
            jax.ShapeDtypeStruct((4, width), full),
        ),
        in_specs=[hbm, hbm, hbm, hbm, hbm, hbm, vmem, vmem],
        out_specs=(vmem,) * 4,
        scratch_shapes=shared + gather + reduce,
        compiler_params=pltpu.CompilerParams(
            collective_id=0, has_side_effects=True, vmem_limit_bytes=VMEM_BYTES
        ),
        name="fused_blocks",
    )(chosen, keys, values, inputs, queries, grads, lse, delta)


def hand_over_kernel(*refs):
    n = len(refs) // 2
    for i in range(n):
        refs[n + i][...] = refs[i][...]


def hand_over(*arrays):
    vmem = pl.BlockSpec(memory_space=pltpu.VMEM)
    return pl.pallas_call(
        hand_over_kernel,
        in_specs=[vmem] * len(arrays),
        out_specs=(vmem,) * len(arrays),
        out_shape=tuple(jax.ShapeDtypeStruct(a.shape, a.dtype) for a in arrays),
        name="hand_over",
    )(*arrays)


def body(
    query_states,
    key_activations,
    value_activations,
    out_grad,
    logsumexp,
    row_delta,
    layer_input,
    chosen,
):
    shards = lax.axis_size("ctx")
    replicas = lax.axis_size("dp")
    ring = shards // 4
    rows_y = replicas // 2
    keys, values = key_activations[0], value_activations[0]
    weight_scale = 1.0 / math.sqrt(TOKENS * shards * replicas)
    outputs = fused_call(
        ring, rows_y, weight_scale, chosen.transpose(0, 3, 1, 2), keys, values, layer_input[0],
        query_states[0], out_grad[0], logsumexp[0], row_delta[0],
    )
    query_grad, key_gradient, value_gradient, key_weight_grad = hand_over(*outputs)
    return (query_grad[None], key_gradient[None], value_gradient[None], key_weight_grad)


def solution(mesh):
    seq = P("dp", "ctx", None)
    stat = P("dp", None, "ctx")
    return jax.shard_map(
        body,
        mesh=mesh,
        in_specs=(seq, seq, seq, seq, stat, stat, seq, P("dp", "ctx", None, None)),
        out_specs=(seq, seq, seq, P(("ctx", "dp"), None)),
        check_vma=False,
    )
```
